32 devices in a mesh: lon: 8 (over z, y), lat: 4 (over x, core).
Axes of the slice: x: 2, y: 2, z: 4, core: 2. Of those that a mesh axis runs over, the one named last changes fastest.
Arguments:
- spectrum: float32 [36, 36, 32, 512], P(None, None, 'lon', 'lat'), may hold values from 0.05 to 2
- sea_mask: int32 [32, 512], P('lon', 'lat'), may hold values 0 or 1
- refraction: float32 [2, 32, 512], P(None, 'lon', 'lat'), may hold values from -0.35 to 0.35
- atm_wind: float32 [2, 2, 4096], P(None, None, ('lon', 'lat')), may hold values from -20 to 20
- hour_fraction: float32 [1], replicated, may hold values from 0 to 1
- send_cells: int32 [32, 192], P(('lon', 'lat')), may hold values from 0 to 127, as said below
- recv_slots: int32 [4, 32, 512], P(None, 'lon', 'lat'), may hold values from 0 to 191, as said below
- recv_weights: float32 [4, 32, 512], P(None, 'lon', 'lat'), may hold values from 0.05 to 0.45
Outputs:
- spectrum_next: float32 [36, 36, 32, 512], P(None, None, 'lon', 'lat')
- surface_wind: float32 [2, 32, 512], P(None, 'lon', 'lat')
The draws below stay inside these ranges and needn't reach their ends.
Inputs may be any that keep to these rules, and one draw needn't show every extreme that they name: `send_cells`: row t holds, for each of the 8 wave tiles of tile t's latitude band in lon order, a block of 24 local atmosphere cells of tile t; every entry is read by some wave cell. `recv_slots`: entry e of a wave cell refers to position e % 24 of the block that the atmosphere tile at lon index e // 24 of the same latitude band lists for this cell's wave tile.
All inputs are finite; a program needn't handle non-finite values. No bound on the sum of `sea_mask` on one device may be relied on, other than what follows from the above.
Results may differ from the reference program's by a relative error of at most 0.0003.
Values sent between devices are 32-bit elements; how exact they have to be, the bound alone decides.
No kernel may reach another device: no remote copies, remote signals or barrier semaphores. Data moves between devices by JAX's collectives and lax.ppermute only.
A program may use at most 128 MiB of HBM per device.

```python
import math
import jax
import jax.numpy as jnp
from jax import lax

FREQ = 36
DIRS = 36
CLON = 4
CLAT = 128
NSUB = 1
LON_TILES = 8
LAT_TILES = 4
TILES = 32
NLON = 32
NLAT = 512
ARW = 8
CAP = 24
ATM_DEV = 128
ATM = 4096


def slot_orders(key):
    order_key = jax.random.fold_in(key, 7)
    scores = jax.random.randint(order_key, (TILES, LON_TILES, CAP), 0, 1 << 20)
    scores = scores * CAP + jnp.arange(CAP, dtype=jnp.int32)
    ordering = jnp.argsort(scores, axis=-1, stable=True).astype(jnp.int32)
    inverse = jnp.argsort(ordering, axis=-1, stable=True).astype(jnp.int32)
    return (ordering, inverse)


def draw_send_cells(key, part):
    ordering, inverse = slot_orders(key)
    row_width = CLON // 2 + 1
    atm_row = ordering // row_width
    offset = ordering % row_width
    target = jnp.arange(LON_TILES, dtype=jnp.int32)[None, :, None]
    atm_lon = (target * (CLON // 2) + offset) % (NLON // 2)
    cells = atm_row * (NLON // 2) + atm_lon
    return cells.reshape(TILES, LON_TILES * CAP).astype(jnp.int32)


def draw_recv_slots(key, part):
    ordering, inverse = slot_orders(key)
    row_width = CLON // 2 + 1
    lon_cells = jnp.arange(NLON, dtype=jnp.int32)[:, None]
    lat_cells = jnp.arange(NLAT, dtype=jnp.int32)[None, :]
    lon_tile = lon_cells // CLON
    lon_local = lon_cells % CLON
    lat_tile = lat_cells // CLAT
    lat_local = lat_cells % CLAT
    slots_list = []
    for corner in range(4):
        offset = lon_local // 2 + corner % 2
        atm_row = jnp.minimum(lat_local // 2 + corner // 2, CLAT // 2 - 1)
        source_lon = atm_row // ARW
        canonical = atm_row % ARW * row_width + offset
        source_tile = source_lon * LAT_TILES + lat_tile
        slot_value = source_lon * CAP + inverse[source_tile, lon_tile, canonical]
        slots_list.append(slot_value)
    return jnp.stack(slots_list, axis=0).astype(jnp.int32)


def place_ends(values, stream_key, smallest, top_value):
    shape = values.shape
    index_at = [jax.random.randint(jax.random.fold_in(stream_key, axis), (), 0, shape[axis]) for axis in range(len(shape))]
    values = values.at[tuple(index_at)].set(smallest)
    longest = shape.index(max(shape))
    index_at[longest] = (index_at[longest] + 1) % shape[longest]
    return values.at[tuple(index_at)].set(top_value)


def steps_of(stream_key, shape, cuts, smallest, high):
    gain, own = 1.0, jax.random.fold_in(stream_key, 6)
    for axis_at, shards_of in cuts:
        steps = jnp.exp(jax.random.uniform(jax.random.fold_in(own, axis_at), (shards_of,), jnp.float32, smallest / len(cuts), high / len(cuts)))
        gain = gain * jnp.repeat(steps, shape[axis_at] // shards_of).reshape([-1 if axis == axis_at else 1 for axis in range(len(shape))])
    return gain


def setup_inputs(seed: int = 0) -> dict:
    keys = jax.random.split(jax.random.key(seed), 9)
    return {
        "spectrum": jnp.clip(jnp.exp(math.log(2.0) - 3.6888794 * jax.random.uniform(keys[0], (FREQ, DIRS, NLON, NLAT), jnp.float32) ** steps_of(keys[0], (FREQ, DIRS, NLON, NLAT), ((2, 8), (3, 4)), -0.2, 0.2)), 0.05, 2.0),
        "sea_mask": place_ends((jax.random.randint(keys[1], (NLON, NLAT), 0, 4) < 3).astype(jnp.int32), jax.random.fold_in(keys[1], 1), 0, 1),
        "refraction": jnp.clip(jax.random.uniform(keys[2], (2, NLON, NLAT), jnp.float32, -0.35, 0.35) * steps_of(keys[2], (2, NLON, NLAT), ((1, 8), (2, 4)), -0.4, 0.0), -0.35, 0.35),
        "atm_wind": jnp.clip(jax.random.uniform(keys[3], (2, 2, ATM), jnp.float32, -20.0, 20.0) * steps_of(keys[3], (2, 2, ATM), ((2, 32),), -0.4, 0.0), -20.0, 20.0),
        "hour_fraction": jnp.clip(jax.random.uniform(keys[4], (1,), jnp.float32, 0.0, 1.0), 0.0, 1.0),
        "send_cells": draw_send_cells(jax.random.fold_in(keys[8], 71), 0),
        "recv_slots": draw_recv_slots(jax.random.fold_in(keys[8], 71), 0),
        "recv_weights": jnp.clip(0.05 + 0.39999999 * jax.random.uniform(keys[7], (4, NLON, NLAT), jnp.float32) ** steps_of(keys[7], (4, NLON, NLAT), ((1, 8), (2, 4)), -0.2, 0.2), 0.05, 0.45),
    }


base_freq = 0.035
freq_step = 1.1
courant_max = 0.9
gravity = 9.81
input_rate = 0.05
damping_rate = 0.8
energy_ref = 0.5

def spectral_tables(freq_count, dir_count):
    frequencies = base_freq * freq_step ** jnp.arange(freq_count, dtype=jnp.float32)
    spacing = 2.0 * math.pi / dir_count
    angles = (jnp.arange(dir_count, dtype=jnp.float32) + 0.5) * spacing
    face_angles = (jnp.arange(dir_count, dtype=jnp.float32) + 1.0) * spacing
    return (frequencies, angles, face_angles)

def transport(padded, courant, dimension):
    length = padded.shape[dimension] - 4
    far_left = lax.slice_in_dim(padded, 0, length + 1, axis=dimension)
    left_cell = lax.slice_in_dim(padded, 1, length + 2, axis=dimension)
    right_cell = lax.slice_in_dim(padded, 2, length + 3, axis=dimension)
    far_right = lax.slice_in_dim(padded, 3, length + 4, axis=dimension)
    forward = courant > 0
    upwind = jnp.where(forward, left_cell, right_cell)
    downwind = jnp.where(forward, right_cell, left_cell)
    beyond = jnp.where(forward, far_left, far_right)
    magnitude = jnp.abs(courant)
    face_flux = courant * (upwind + 0.5 * (1.0 - magnitude) * (downwind - upwind) - (1.0 - magnitude * magnitude) / 6.0 * (downwind - 2.0 * upwind + beyond))
    return lax.slice_in_dim(face_flux, 1, length + 1, axis=dimension) - lax.slice_in_dim(face_flux, 0, length, axis=dimension)

def reference(spectrum, sea_mask, refraction, atm_wind, hour_fraction, send_cells, recv_slots, recv_weights):
    sea_frac = sea_mask.astype(jnp.float32)
    frequencies, angles, face_angles = spectral_tables(FREQ, DIRS)
    period_ratio = base_freq / frequencies
    courant_lon = courant_max * period_ratio[:, None] * jnp.cos(angles)[None, :]
    courant_lat = courant_max * period_ratio[:, None] * jnp.sin(angles)[None, :]
    bending = jnp.sqrt(period_ratio)
    face_sin = jnp.sin(face_angles)[:, None, None]
    face_cos = jnp.cos(face_angles)[:, None, None]

    def advance(inputs):
        density, along_lon, along_lat, bend_rate = inputs
        for substep in range(NSUB):
            padded = jnp.concatenate([density[:, -2:], density, density[:, :2]], axis=1)
            density = (density - transport(padded, along_lon[:, None, None], 1)) * sea_frac
            padded = jnp.pad(density, ((0, 0), (0, 0), (2, 2)))
            density = (density - transport(padded, along_lat[:, None, None], 2)) * sea_frac
        face_speed = bend_rate * (refraction[0][None] * face_sin - refraction[1][None] * face_cos)
        next_dir = jnp.roll(density, -1, axis=0)
        face_flux = jnp.maximum(face_speed, 0.0) * density + jnp.minimum(face_speed, 0.0) * next_dir
        return density - (face_flux - jnp.roll(face_flux, 1, axis=0))
    refracted = lax.map(advance, (spectrum, courant_lon, courant_lat, bending))
    weight_late = hour_fraction[0]
    wind_now = (1.0 - weight_late) * atm_wind[0] + weight_late * atm_wind[1]
    lon_cells = jnp.arange(NLON, dtype=jnp.int32)[:, None]
    lat_cells = jnp.arange(NLAT, dtype=jnp.int32)[None, :]
    lon_tile = (lon_cells // CLON).astype(jnp.int32)
    lat_tile = (lat_cells // CLAT).astype(jnp.int32)
    source_lon = (recv_slots // CAP).astype(jnp.int32)
    position = (recv_slots % CAP).astype(jnp.int32)
    source_tile = (source_lon * LAT_TILES + lat_tile[None]).astype(jnp.int32)
    local_cell = send_cells[source_tile, lon_tile[None] * CAP + position]
    picked = wind_now[:, (source_tile * ATM_DEV + local_cell).astype(jnp.int32)]
    surface_wind = lax.optimization_barrier(jnp.sum(recv_weights[None] * picked, axis=1))
    energy = lax.optimization_barrier(jnp.mean(refracted, axis=(0, 1)))
    energy_ratio = energy / energy_ref
    damping = energy_ratio * energy_ratio
    projected = surface_wind[0][None] * jnp.cos(angles)[:, None, None] + surface_wind[1][None] * jnp.sin(angles)[:, None, None]
    rel_freq = frequencies / frequencies[FREQ - 1]
    slowness_all = 2.0 * math.pi * frequencies / gravity

    def apply_sources(inputs):
        density, relative, slowness = inputs
        growth = input_rate * relative * jnp.maximum(projected * slowness - 1.0, 0.0)
        decay_rate = damping_rate * relative * damping
        return density * jnp.exp(growth - decay_rate)
    spectrum_next = lax.map(apply_sources, (refracted, rel_freq, slowness_all))
    return (spectrum_next, surface_wind)
```

```python
import math

import jax
import jax.numpy as jnp
import numpy as np
from jax import lax
from jax.experimental import pallas as pl
from jax.experimental.pallas import tpu as pltpu
from jax.sharding import PartitionSpec as P

base_freq = 0.035
freq_step = 1.1
courant_max = 0.9
gravity = 9.81
input_rate = 0.05
damping_rate = 0.8
energy_ref = 0.5

F32 = jnp.float32
FREQS = 36
DIRS = 36
CELLS = 4
LANES = 128
ROWS = DIRS * CELLS
BLOCKS = (0, 8, 16, 24, 28)
GROUP = 4
HALO = DIRS + DIRS // 2
NEAR_SPLIT = 16
FAR = DIRS // 2
PACK = 6
CHUNKS = (4, 12, 16, 4)
VMEM = 48 * 1024 * 1024

freqs = base_freq * freq_step ** np.arange(FREQS, dtype=np.float64)
spacing = 2.0 * math.pi / DIRS
theta = (np.arange(DIRS) + 0.5) * spacing
phi = (np.arange(DIRS) + 1.0) * spacing
ratio = base_freq / freqs
SCALARS = np.stack(
    [
        courant_max * ratio,
        np.sqrt(ratio),
        input_rate * freqs / freqs[-1],
        2.0 * math.pi * freqs / gravity,
        freqs / freqs[-1],
    ]
).astype(np.float32)
ANGLES = np.broadcast_to(
    np.stack(
        [np.abs(np.cos(theta)), np.abs(np.sin(theta)), np.cos(theta), np.sin(theta), np.sin(phi), np.cos(phi)]
    )[:, :, None],
    (6, DIRS, LANES),
).astype(np.float32)


def stencil(a):
    one_m = 1.0 - a * a
    beyond = a * one_m * (-1.0 / 6.0)
    half = a * (0.5 - 0.5 * a)
    down = half + beyond
    up = a - half - 2.0 * beyond
    return beyond, up - beyond, 1.0 + down - up, -down


def packed_weights():
    out = np.zeros((5, FREQS // PACK, 8, LANES), np.float64)
    for k in range(FREQS):
        for b, j0 in enumerate(BLOCKS):
            c = courant_max * ratio[k] * np.cos(theta[j0 : j0 + 8])
            far, up, own, down = stencil(np.abs(c))
            zero = np.zeros(8)
            pos = c > 0
            five = [
                np.where(pos, far, zero),
                np.where(pos, up, down),
                own,
                np.where(pos, down, up),
                np.where(pos, zero, far),
            ]
            lane = 4 * ((k % PACK) * len(BLOCKS) + b)
            for d in range(5):
                out[d, k // PACK, :, lane : lane + 4] = five[d][:, None]
    return out.astype(np.float32)


PACKED = packed_weights()


def any_spec():
    return pl.BlockSpec(memory_space=pl.ANY)


def vmem_spec():
    return pl.BlockSpec(memory_space=pltpu.VMEM)


def smem_spec():
    return pl.BlockSpec(memory_space=pltpu.SMEM)


def prep_body(first, count, x_hbm, right_ref, left_ref, xbuf, sem):
    copy = pltpu.make_async_copy(x_hbm.at[pl.ds(first, count)], xbuf, sem)
    copy.start()
    copy.wait()

    def body(i, _):
        for kk in range(GROUP):
            k = i * GROUP + kk
            base = HALO * kk
            half = FAR // 2
            for ref, near, far in ((right_ref, 3, 2), (left_ref, 0, 1)):
                for row, j, n in ((0, 0, 8), (8, 8, 8), (34, 16, 8), (42, 24, 8), (50, 32, 4)):
                    ref[i, pl.ds(base + row, n), :] = xbuf[k, pl.ds(near + 4 * j, n, stride=4), :]
                if far == 2:
                    runs = ((16, 0, 8), (24, 8, 1), (25, 27, 8), (33, 35, 1))
                else:
                    runs = ((16, 9, 8), (24, 17, 8), (32, 25, 2))
                for row, j, n in runs:
                    ref[i, pl.ds(base + row, n), :] = xbuf[k, pl.ds(far + 4 * j, n, stride=4), :]
        return 0

    lax.fori_loop(0, count // GROUP, body, 0)


def prep(x, first, count):
    shape = jax.ShapeDtypeStruct((count // GROUP, GROUP * HALO, LANES), F32)
    return pl.pallas_call(
        lambda *refs: prep_body(first, count, *refs),
        out_shape=(shape, shape),
        in_specs=[any_spec()],
        out_specs=(vmem_spec(), vmem_spec()),
        scratch_shapes=[pltpu.VMEM((count, ROWS, LANES), F32), pltpu.SemaphoreType.DMA],
        compiler_params=pltpu.CompilerParams(vmem_limit_bytes=VMEM),
        cost_estimate=pl.CostEstimate(flops=count * 1000, bytes_accessed=count * 150000, transcendentals=0),
        name="halo_rows",
    )(x)


def lane_ids():
    return lax.broadcasted_iota(jnp.int32, (8, LANES), 1)


def pack_body(x_hbm, q_ref, xbuf, sem):
    copy = pltpu.make_async_copy(x_hbm, xbuf, sem)
    copy.start()
    copy.wait()
    lane = lane_ids()
    block = lane // 4

    def body(g, _):
        for cell in range(CELLS):
            acc = jnp.zeros((8, LANES), F32)
            for r in range(PACK):
                for b, j0 in enumerate(BLOCKS):
                    at = r * len(BLOCKS) + b
                    rows = xbuf[g * PACK + r, pl.ds(cell + 4 * j0, 8, stride=4), :]
                    acc = jnp.where(block == at, pltpu.roll(rows, (4 * at + 2) % LANES, 1), acc)
            q_ref[cell, g] = acc
        return 0

    lax.fori_loop(0, FREQS // PACK, body, 0)


def pack_edges(x):
    return pl.pallas_call(
        pack_body,
        out_shape=jax.ShapeDtypeStruct((CELLS, FREQS // PACK, 8, LANES), F32),
        in_specs=[any_spec()],
        out_specs=vmem_spec(),
        scratch_shapes=[pltpu.VMEM((FREQS, ROWS, LANES), F32), pltpu.SemaphoreType.DMA],
        compiler_params=pltpu.CompilerParams(vmem_limit_bytes=VMEM),
        cost_estimate=pl.CostEstimate(flops=4000000, bytes_accessed=4000000, transcendentals=0),
        name="edge_columns",
    )(x)


def setup_tables(ang, sea, refr, wind, sea8, turn, proj):
    for cell in range(CELLS):
        row = pl.ds(cell, 1)
        sea8[cell] = jnp.broadcast_to(sea[row, :], (8, LANES))
        for j0 in BLOCKS:
            j = pl.ds(j0, 8)
            turn[cell, j, :] = refr[0, row, :] * ang[4, j, :] - refr[1, row, :] * ang[5, j, :]
            proj[cell, j, :] = wind[0, row, :] * ang[2, j, :] + wind[1, row, :] * ang[3, j, :]


def chunk_pass(
    first, count, scal, ang, x, from_west, from_east, edges, sea8, turn, proj, zs, gs, out, out_first
):
    lane = lane_ids()
    sub = lax.broadcasted_iota(jnp.int32, (8, LANES), 0)
    near_rows = (0, 8, 34, 42, 46)

    def one(i, kk, sums):
        k = first + i * GROUP + kk
        base = HALO * kk
        cour = scal[0, k]
        bend = scal[1, k]
        rate = scal[2, k]
        slow = scal[3, k]
        group = k // PACK
        at0 = (k - group * PACK) * len(BLOCKS)
        for b, j0 in enumerate(BLOCKS):
            w0, w1, w2, w3 = stencil(cour * ang[0, pl.ds(j0, 8), :])
            v0, v1, v2, v3 = stencil(cour * ang[1, pl.ds(j0, 8), :])
            cells = [x[i * GROUP + kk, pl.ds(c + 4 * j0, 8, stride=4), :] for c in range(CELLS)]
            west = from_west[i, pl.ds(base + near_rows[b], 8), :]
            east = from_east[i, pl.ds(base + near_rows[b], 8), :]
            plus = [west, *cells, east]
            minus = plus[::-1]
            if b == 0:
                far, seq = from_west[i, pl.ds(base + 16, 8), :], plus
            elif b == 2:
                far, seq = from_east[i, pl.ds(base + 23, 8), :], minus
            elif b == 4:
                far, seq = from_west[i, pl.ds(base + 26, 8), :], plus
            else:
                if b == 1:
                    pos = sub < 1
                    far_p, far_m = from_west[i, pl.ds(base + 24, 8), :], from_east[i, pl.ds(base + 15, 8), :]
                else:
                    pos = sub >= 3
                    far_p, far_m = from_west[i, pl.ds(base + 22, 8), :], from_east[i, pl.ds(base + 31, 8), :]
                far = jnp.where(pos, far_p, far_m)
                seq = [jnp.where(pos, p, m) for p, m in zip(plus, minus)]
            seq = [far, *seq]
            moved = [
                w0 * seq[c] + w1 * seq[c + 1] + w2 * seq[c + 2] + w3 * seq[c + 3] for c in range(CELLS)
            ]
            if b == 2:
                moved = moved[::-1]
            elif b in (1, 3):
                moved = [jnp.where(pos, p, m) for p, m in zip(moved, moved[::-1])]
            shift = LANES - (4 * (at0 + b) + 2)
            for c in range(CELLS):
                z = moved[c] * sea8[c]
                ghost = pltpu.roll(edges[c, group], shift, 1)
                s1 = pltpu.roll(jnp.where(lane == LANES - 1, ghost, z), 1, 1)
                n1 = pltpu.roll(jnp.where(lane == 0, ghost, z), LANES - 1, 1)
                if b <= 2:
                    s2 = pltpu.roll(jnp.where(lane >= LANES - 2, ghost, z), 2, 1)
                if b >= 2:
                    n2 = pltpu.roll(jnp.where(lane < 2, ghost, z), LANES - 2, 1)
                if b < 2:
                    up, down, far = s1, n1, s2
                elif b > 2:
                    up, down, far = n1, s1, n2
                else:
                    p = sub < 2
                    up, down = jnp.where(p, s1, n1), jnp.where(p, n1, s1)
                    far = jnp.where(p, s2, n2)
                z = (v0 * far + v1 * up + v2 * z + v3 * down) * sea8[c]
                zs[kk, c, pl.ds(8 + j0, 8), :] = z
        out_sums = []
        for c in range(CELLS):
            zs[kk, c, pl.ds(8 + DIRS, 1), :] = zs[kk, c, pl.ds(8, 1), :]
            for b, j0 in enumerate(BLOCKS):
                own = zs[kk, c, pl.ds(8 + j0, 8), :]
                nxt = zs[kk, c, pl.ds(9 + j0, 8), :]
                s = bend * turn[c, pl.ds(j0, 8), :]
                gs[kk, c, pl.ds(8 + j0, 8), :] = jnp.maximum(s, 0.0) * own + jnp.minimum(s, 0.0) * nxt
            gs[kk, c, pl.ds(7, 1), :] = gs[kk, c, pl.ds(7 + DIRS, 1), :]
            total = sums[c]
            for b, j0 in enumerate(BLOCKS):
                own = zs[kk, c, pl.ds(8 + j0, 8), :]
                flux = gs[kk, c, pl.ds(8 + j0, 8), :]
                prev = gs[kk, c, pl.ds(7 + j0, 8), :]
                refracted = own - (flux - prev)
                total = total + (jnp.where(sub >= 4, refracted, 0.0) if b == 4 else refracted)
                growth = rate * jnp.maximum(proj[c, pl.ds(j0, 8), :] * slow - 1.0, 0.0)
                out[out_first + i * GROUP + kk, pl.ds(c + 4 * j0, 8, stride=4), :] = refracted * jnp.exp(growth)
            out_sums.append(total)
        return tuple(out_sums)

    def body(i, sums):
        for kk in range(GROUP):
            sums = one(i, kk, sums)
        return sums

    zero = jnp.zeros((8, LANES), F32)
    return lax.fori_loop(0, count // GROUP, body, (zero,) * CELLS)


def merge_edges(south_ref, north_ref, edges):
    pick = lane_ids() % 4 < 2
    for c in range(CELLS):
        for g in range(FREQS // PACK):
            edges[c, g] = jnp.where(pick, south_ref[c, g], north_ref[c, g])


def main_body(
    first, count, scal, ang, x_hbm, west, east, south, north, sea, refr, wind, out, energy,
    xbuf, edges, sea8, turn, proj, zs, gs, sem,
):
    copy = pltpu.make_async_copy(x_hbm.at[pl.ds(first, count)], xbuf, sem)
    copy.start()
    setup_tables(ang, sea, refr, wind, sea8, turn, proj)
    merge_edges(south, north, edges)
    copy.wait()
    sums = chunk_pass(
        first, count, scal, ang, xbuf, west, east, edges, sea8, turn, proj, zs, gs, out, 0
    )
    for c in range(CELLS):
        energy[c] = sums[c]


def pass_scratch():
    return [
        pltpu.VMEM((CELLS, FREQS // PACK, 8, LANES), F32),
        pltpu.VMEM((CELLS, 8, LANES), F32),
        pltpu.VMEM((CELLS, DIRS, LANES), F32),
        pltpu.VMEM((CELLS, DIRS, LANES), F32),
        pltpu.VMEM((GROUP, CELLS, 56, LANES), F32),
        pltpu.VMEM((GROUP, CELLS, 56, LANES), F32),
    ]


def main_chunk(first, count, x, west, east, south, north, sea, refr, wind):
    return pl.pallas_call(
        lambda *refs: main_body(first, count, *refs),
        out_shape=(
            jax.ShapeDtypeStruct((count, ROWS, LANES), F32),
            jax.ShapeDtypeStruct((CELLS, 8, LANES), F32),
        ),
        in_specs=[smem_spec(), vmem_spec(), any_spec()] + [vmem_spec()] * 7,
        out_specs=(vmem_spec(), vmem_spec()),
        scratch_shapes=[pltpu.VMEM((count, ROWS, LANES), F32), *pass_scratch(), pltpu.SemaphoreType.DMA],
        compiler_params=pltpu.CompilerParams(vmem_limit_bytes=VMEM),
        cost_estimate=pl.CostEstimate(
            flops=count * 1500000, bytes_accessed=count * 300000, transcendentals=count * 18432
        ),
        name="chunk",
    )(SCALARS, ANGLES, x, west, east, south, north, sea, refr, wind)


def tail_body(
    sizes, scal, ang, x_hbm, west, east, south, north, sea, refr, wind, *rest
):
    done = len(sizes) - 1
    parts, energies = rest[:done], rest[done : 2 * done]
    out_hbm = rest[2 * done]
    xbuf, obuf, edges, sea8, turn, proj, zs, gs, sem, part_sem, out_sem = rest[2 * done + 1 :]
    count = sizes[-1]
    first = FREQS - count
    copy = pltpu.make_async_copy(x_hbm.at[pl.ds(first, count)], xbuf, sem)
    copy.start()
    loads, at = [], 0
    for n, size in enumerate(sizes[:-1]):
        loads.append(pltpu.make_async_copy(parts[n], obuf.at[pl.ds(at, size)], part_sem.at[n]))
        loads[-1].start()
        at += size
    setup_tables(ang, sea, refr, wind, sea8, turn, proj)
    merge_edges(south, north, edges)
    copy.wait()
    sums = chunk_pass(
        first, count, scal, ang, xbuf, west, east, edges, sea8, turn, proj, zs, gs, obuf, first
    )
    sub = lax.broadcasted_iota(jnp.int32, (8, LANES), 0)
    pattern = jnp.zeros((8, LANES), F32)
    for c in range(CELLS):
        total = sums[c]
        for energy in energies:
            total = total + energy[c]
        mean = jnp.sum(total, axis=0, keepdims=True) * (1.0 / (FREQS * DIRS))
        level = mean * (1.0 / energy_ref)
        pattern = jnp.where(sub % CELLS == c, damping_rate * (level * level), pattern)
    for load in loads:
        load.wait()
    stores = []
    step = FREQS // 6
    for n in range(6):
        def body(i, _):
            k = n * step + i
            scale = jnp.exp(-(scal[4, k] * pattern))
            for r in range(0, ROWS, 8):
                obuf[k, pl.ds(r, 8), :] = obuf[k, pl.ds(r, 8), :] * scale
            return 0

        lax.fori_loop(0, step, body, 0)
        span = pl.ds(n * step, step)
        stores.append(pltpu.make_async_copy(obuf.at[span], out_hbm.at[span], out_sem.at[n]))
        stores[-1].start()
    for store in stores:
        store.wait()


def tail_chunk(sizes, x, west, east, south, north, sea, refr, wind, parts, energies):
    count = sizes[-1]
    done = len(sizes) - 1
    return pl.pallas_call(
        lambda *refs: tail_body(sizes, *refs),
        out_shape=jax.ShapeDtypeStruct((FREQS, ROWS, LANES), F32),
        in_specs=[smem_spec(), vmem_spec(), any_spec()]
        + [vmem_spec()] * 7
        + [any_spec()] * done
        + [vmem_spec()] * done,
        out_specs=any_spec(),
        scratch_shapes=[
            pltpu.VMEM((count, ROWS, LANES), F32),
            pltpu.VMEM((FREQS, ROWS, LANES), F32),
            *pass_scratch(),
            pltpu.SemaphoreType.DMA,
            pltpu.SemaphoreType.DMA((done,)),
            pltpu.SemaphoreType.DMA((6,)),
        ],
        compiler_params=pltpu.CompilerParams(vmem_limit_bytes=VMEM),
        cost_estimate=pl.CostEstimate(
            flops=count * 1500000, bytes_accessed=6000000, transcendentals=count * 18432
        ),
        name="last_chunk",
    )(SCALARS, ANGLES, x, west, east, south, north, sea, refr, wind, *parts, *energies)


def ring(axis, wrap):
    size = lax.axis_size(axis)
    up = [(i, (i + 1) % size) for i in range(size if wrap else size - 1)]
    return up, [(j, i) for i, j in up]


def local(
    spectrum, sea_mask, refraction, atm_wind, hour_fraction, send_cells, recv_slots, recv_weights
):
    east_way, west_way = ring("lon", True)
    north_way, south_way = ring("lat", False)
    x = spectrum.reshape(FREQS, ROWS, LANES)
    sea = sea_mask.astype(F32)

    firsts = [sum(CHUNKS[:n]) for n in range(len(CHUNKS))]
    halos = []
    for first, count in zip(firsts, CHUNKS):
        to_east, to_west = prep(x, first, count)
        halos.append((lax.ppermute(to_east, "lon", east_way), lax.ppermute(to_west, "lon", west_way)))

    late = hour_fraction[0]
    wind_now = (1.0 - late) * atm_wind[0] + late * atm_wind[1]
    packed = wind_now[:, send_cells[0]]
    received = lax.all_to_all(packed, "lon", split_axis=1, concat_axis=1, tiled=True)
    picked = received[:, recv_slots]
    surface_wind = jnp.sum(recv_weights[None] * picked, axis=1)

    q = pack_edges(x)
    q_west = lax.ppermute(q[2:], "lon", east_way)
    q_east = lax.ppermute(q[:2], "lon", west_way)
    ext = jnp.concatenate([q_west, q, q_east], axis=0)
    moved = sum(PACKED[d][None] * ext[d : d + CELLS] for d in range(5))
    sea_edge = jnp.tile(jnp.concatenate([sea[:, -2:], sea[:, :2]], axis=1), (1, LANES // 4))
    moved = moved * sea_edge[:, None, None, :]
    south = lax.ppermute(moved, "lat", north_way)
    north = lax.ppermute(moved, "lat", south_way)

    parts, energies = [], []
    for n, (first, count) in enumerate(zip(firsts, CHUNKS)):
        west, east = halos[n]
        if n < len(CHUNKS) - 1:
            part, energy = main_chunk(
                first, count, x, west, east, south, north, sea, refraction, surface_wind
            )
            parts.append(part)
            energies.append(energy)
        else:
            out = tail_chunk(
                CHUNKS, x, west, east, south, north, sea, refraction, surface_wind, parts, energies
            )
    return (out.reshape(spectrum.shape), surface_wind)


def solution(mesh):
    in_specs = (
        P(None, None, "lon", "lat"),
        P("lon", "lat"),
        P(None, "lon", "lat"),
        P(None, None, ("lon", "lat")),
        P(),
        P(("lon", "lat"), None),
        P(None, "lon", "lat"),
        P(None, "lon", "lat"),
    )
    out_specs = (P(None, None, "lon", "lat"), P(None, "lon", "lat"))
    return jax.shard_map(local, mesh=mesh, in_specs=in_specs, out_specs=out_specs, check_vma=False)
```

```python
import math

import jax
import jax.numpy as jnp
import numpy as np
from jax import lax
from jax.experimental import pallas as pl
from jax.experimental.pallas import tpu as pltpu
from jax.sharding import PartitionSpec as P

base_freq = 0.035
freq_step = 1.1
courant_max = 0.9
gravity = 9.81
input_rate = 0.05
damping_rate = 0.8
energy_ref = 0.5

F32 = jnp.float32
FREQS = 36
DIRS = 36
CELLS = 4
LANES = 128
ROWS = DIRS * CELLS
BLOCKS = (0, 8, 16, 24, 28)
GROUP = 4
HALO = DIRS + DIRS // 2
NEAR_SPLIT = 16
FAR = DIRS // 2
PACK = 6
CHUNKS = (8, 8, 12, 8)
GROUPS = FREQS // PACK
EDGE_ROWS = 2 * (FREQS // PACK) * 8
VMEM = 32 * 1024 * 1024
FIRST_VMEM = 63000000

freqs = base_freq * freq_step ** np.arange(FREQS, dtype=np.float64)
spacing = 2.0 * math.pi / DIRS
theta = (np.arange(DIRS) + 0.5) * spacing
phi = (np.arange(DIRS) + 1.0) * spacing
ratio = base_freq / freqs
SCALARS = np.stack(
    [
        courant_max * ratio,
        np.sqrt(ratio),
        input_rate * freqs / freqs[-1],
        2.0 * math.pi * freqs / gravity,
        freqs / freqs[-1],
    ]
).astype(np.float32)
ANGLES = np.broadcast_to(
    np.stack(
        [np.abs(np.cos(theta)), np.abs(np.sin(theta)), np.cos(theta), np.sin(theta), np.sin(phi), np.cos(phi)]
    )[:, :, None],
    (6, DIRS, LANES),
).astype(np.float32)


def stencil(a):
    one_m = 1.0 - a * a
    beyond = a * one_m * (-1.0 / 6.0)
    half = a * (0.5 - 0.5 * a)
    down = half + beyond
    up = a - half - 2.0 * beyond
    return beyond, up - beyond, 1.0 + down - up, -down


def packed_weights():
    out = np.zeros((5, FREQS // PACK, 8, LANES), np.float64)
    for k in range(FREQS):
        for b, j0 in enumerate(BLOCKS):
            c = courant_max * ratio[k] * np.cos(theta[j0 : j0 + 8])
            far, up, own, down = stencil(np.abs(c))
            zero = np.zeros(8)
            pos = c > 0
            five = [
                np.where(pos, far, zero),
                np.where(pos, up, down),
                own,
                np.where(pos, down, up),
                np.where(pos, zero, far),
            ]
            lane = 4 * ((k % PACK) * len(BLOCKS) + b)
            for d in range(5):
                out[d, k // PACK, :, lane : lane + 4] = five[d][:, None]
    return out.astype(np.float32)


PACKED = packed_weights()


def any_spec():
    return pl.BlockSpec(memory_space=pl.ANY)


def vmem_spec():
    return pl.BlockSpec(memory_space=pltpu.VMEM)


def smem_spec():
    return pl.BlockSpec(memory_space=pltpu.SMEM)


def halo_rows(x, start, right, left, low, high):
    def body(i, _):
        for kk in range(GROUP):
            k = start + i * GROUP + kk
            for ref, near, far in ((right, 3, 2), (left, 0, 1)):
                if far == 2:
                    runs = ((16, 0, 8), (24, 8, 1), (25, 27, 8), (33, 35, 1))
                else:
                    runs = ((16, 9, 8), (24, 17, 8), (32, 25, 2))
                for cell, rows in (
                    (near, ((0, 0, 8), (8, 8, 8), (34, 16, 8), (42, 24, 8), (50, 32, 4))),
                    (far, runs),
                ):
                    for row, j, n in rows:
                        ref[halo_at(i, kk, row, n), :] = x[k, pl.ds(cell + 4 * j, n, stride=4), :]
        return 0

    lax.fori_loop(low // GROUP, high // GROUP, body, 0)


def halo_at(i, kk, row, n):
    return pl.ds(pl.multiple_of(i * (GROUP * HALO), 8) + HALO * kk + row, n)


def lane_ids():
    return lax.broadcasted_iota(jnp.int32, (8, LANES), 1)


def first_body(count, x_hbm, hour, wind_hbm, cells_hbm, right, left, packed, x, wind, cells, sem, small):
    copies = []
    for n in range(count // GROUP):
        span = pl.ds(n * GROUP, GROUP)
        copies.append(pltpu.make_async_copy(x_hbm.at[span], x.at[span], sem.at[n]))
        copies[-1].start()
    few = [
        pltpu.make_async_copy(wind_hbm, wind, small.at[0]),
        pltpu.make_async_copy(cells_hbm, cells, small.at[1]),
    ]
    for copy in few:
        copy.start()
    for copy in few:
        copy.wait()
    late = hour[0]
    now = (1.0 - late) * wind[pl.ds(0, 2), :] + late * wind[pl.ds(2, 2), :]
    width = cells.shape[1]
    index = jnp.concatenate([cells[:, :LANES], cells[:, width - LANES :]] * 4, axis=0)
    table = jnp.concatenate([now[:1]] * 2 + [now[1:]] * 2 + [now[:1]] * 4, axis=0)
    listed = jnp.take_along_axis(table, index, axis=1)
    for ref, row in ((packed, 0), (right, count * HALO), (left, count * HALO)):
        ref[pl.ds(row, 8), :] = listed
    for n in range(count // GROUP):
        copies[n].wait()
        halo_rows(x, 0, right, left, n * GROUP, (n + 1) * GROUP)


def message(count, extra=0):
    return pltpu.VMEM((count * HALO + extra, LANES), F32)


def first_halos(x, count, hour, wind, cells):
    return pl.pallas_call(
        lambda *refs: first_body(count, *refs),
        out_shape=(message(count, 8), message(count, 8), jax.ShapeDtypeStruct((8, LANES), F32)),
        in_specs=[any_spec(), smem_spec(), any_spec(), any_spec()],
        out_specs=(vmem_spec(),) * 3,
        scratch_shapes=[
            pltpu.VMEM((count, *x.shape[1:]), F32),
            pltpu.VMEM(wind.shape, F32),
            pltpu.VMEM(cells.shape, cells.dtype),
            pltpu.SemaphoreType.DMA((count // GROUP,)),
            pltpu.SemaphoreType.DMA((2,)),
        ],
        compiler_params=pltpu.CompilerParams(vmem_limit_bytes=FIRST_VMEM),
        cost_estimate=pl.CostEstimate(flops=0, bytes_accessed=2000000, transcendentals=0),
        name="first_halos",
    )(x, hour, wind, cells)


def edge_body(x, sea, after, q):
    lane = lane_ids()
    block = lane // 4

    def body(g, _):
        for cell in range(CELLS):
            acc = jnp.zeros((8, LANES), F32)
            for r in range(PACK):
                for b, j0 in enumerate(BLOCKS):
                    at = r * len(BLOCKS) + b
                    rows = x[g * PACK + r, pl.ds(cell + 4 * j0, 8, stride=4), :]
                    acc = jnp.where(block == at, pltpu.roll(rows, (4 * at + 2) % LANES, 1), acc)
            q[cell, g] = acc
        return 0

    lax.fori_loop(0, GROUPS, body, 0)
    for cell in range(CELLS):
        mask = jnp.zeros((8, LANES), F32)
        for n, at in enumerate((LANES - 2, LANES - 1, 0, 1)):
            mask = jnp.where(lane % 4 == n, sea[pl.ds(cell, 1), pl.ds(at, 1)].astype(F32), mask)
        q[cell, GROUPS] = mask


def pack_edges(x, sea, after):
    return pl.pallas_call(
        edge_body,
        out_shape=jax.ShapeDtypeStruct((CELLS, GROUPS + 1, 8, LANES), F32),
        in_specs=[vmem_spec()] * 3,
        out_specs=vmem_spec(),
        compiler_params=pltpu.CompilerParams(vmem_limit_bytes=VMEM),
        cost_estimate=pl.CostEstimate(flops=0, bytes_accessed=4000000, transcendentals=0),
        name="pack_edges",
    )(x, sea, after)


def middle_body(spans, x, south, north, after_east, after_west, *refs):
    outs, merged = refs[:-1], refs[-1]
    row = spans[0][1] * HALO
    pick = lane_ids() % 4 < 2
    for c in range(CELLS):
        side, slot = (outs[1], c) if c < 2 else (outs[0], c - 2)
        for g in range(GROUPS + 1):
            both = jnp.where(pick, south[c, g], north[c, g])
            merged[c, g] = both
            if g < GROUPS:
                side[pl.ds(row + (slot * GROUPS + g) * 8, 8), :] = both
    for n, (start, count) in enumerate(spans):
        halo_rows(x, start, outs[2 * n], outs[2 * n + 1], 0, count)


def middle_halos(x, spans, south, north, after):
    extra = [EDGE_ROWS] + [0] * (len(spans) - 1)
    return pl.pallas_call(
        lambda *refs: middle_body(spans, *refs),
        out_shape=tuple(message(count, more) for (_, count), more in zip(spans, extra) for _ in range(2))
        + (jax.ShapeDtypeStruct((CELLS, GROUPS + 1, 8, LANES), F32),),
        in_specs=[vmem_spec()] * 5,
        out_specs=(vmem_spec(),) * (2 * len(spans) + 1),
        compiler_params=pltpu.CompilerParams(vmem_limit_bytes=VMEM),
        cost_estimate=pl.CostEstimate(flops=0, bytes_accessed=6000000, transcendentals=0),
        name="middle_halos",
    )(x, south, north, *after)


def last_halos(x, start, count, *after):
    return pl.pallas_call(
        lambda x, east, west, winds, right, left: halo_rows(x, start, right, left, 0, count),
        out_shape=(message(count), message(count)),
        in_specs=[vmem_spec()] * 4,
        out_specs=(vmem_spec(),) * 2,
        compiler_params=pltpu.CompilerParams(vmem_limit_bytes=VMEM),
        cost_estimate=pl.CostEstimate(flops=0, bytes_accessed=1000000, transcendentals=0),
        name="last_halos",
    )(x, *after)


def ghost_body(count, merged, west, east, weights, ghosts):
    def body(g, _):
        rows = [
            pl.ds(pl.multiple_of(count * HALO + (n * GROUPS + g) * 8, 8), 8) for n in range(2)
        ]
        ext = [west[rows[0], :], west[rows[1], :]] + [merged[c, g] for c in range(CELLS)]
        ext += [east[rows[0], :], east[rows[1], :]]
        for c in range(CELLS):
            total = weights[0, g] * ext[c]
            for d in range(1, 5):
                total = total + weights[d, g] * ext[c + d]
            total = total * merged[c, GROUPS]
            for r in range(PACK):
                for b in range(len(BLOCKS)):
                    shift = LANES - (4 * (r * len(BLOCKS) + b) + 2)
                    ghosts[g * PACK + r, c, b] = pltpu.roll(total, shift, 1)
        return 0

    lax.fori_loop(0, GROUPS, body, 0)


def move_ghosts(count, merged, west, east):
    return pl.pallas_call(
        lambda *refs: ghost_body(count, *refs),
        out_shape=jax.ShapeDtypeStruct((FREQS, CELLS, len(BLOCKS), 8, LANES), F32),
        in_specs=[vmem_spec()] * 4,
        out_specs=vmem_spec(),
        compiler_params=pltpu.CompilerParams(vmem_limit_bytes=VMEM),
        cost_estimate=pl.CostEstimate(flops=0, bytes_accessed=2000000, transcendentals=0),
        name="move_ghosts",
    )(merged, west, east, PACKED)


def wind_body(cap, sources, slots, weights, ang, sea, refr, *rest):
    picked = [[jnp.zeros((8, LANES), F32) for _ in range(2)] for _ in range(2)]
    pieces, (wind, sea8, turn, proj, table) = rest[:-5], rest[-5:]
    at = 0
    for piece in pieces:
        table[pl.ds(at, piece.shape[0]), :] = piece[...]
        at += piece.shape[0]
    width = cap * sources
    me = lax.axis_index("lon")
    mine = cap * me
    for half in range(2):
        index = slots[pl.ds(8 * half, 8), :]
        for s in range(sources):
            place = index - cap * s
            here = (place >= 0) & (place < cap)
            place = jnp.clip(place, 0, cap - 1) + mine
            low = place < LANES
            place = jnp.where(low, place, place - (width - LANES))
            for c in range(2):
                row = [
                    jnp.broadcast_to(table[pl.ds(8 * (s ^ me) + 2 * c + n, 1), :], (8, LANES)) for n in range(2)
                ]
                value = [jnp.take_along_axis(r, place, axis=1) for r in row]
                value = jnp.where(low, value[0], value[1])
                picked[half][c] = jnp.where(here, value, picked[half][c])
    for c in range(2):
        total = weights[pl.ds(0, 8), :] * picked[0][c]
        total = total + weights[pl.ds(8, 8), :] * picked[1][c]
        wind[c] = total[:CELLS] + total[CELLS:]
    for cell in range(CELLS):
        row = pl.ds(cell, 1)
        sea8[cell] = jnp.broadcast_to(sea[row, :], (8, LANES)).astype(F32)
        for j0 in BLOCKS:
            j = pl.ds(j0, 8)
            turn[cell, j, :] = refr[0, row, :] * ang[4, j, :] - refr[1, row, :] * ang[5, j, :]
            proj[cell, j, :] = wind[0, row, :] * ang[2, j, :] + wind[1, row, :] * ang[3, j, :]


def surface(cap, sources, pieces, slots, weights, sea, refr):
    return pl.pallas_call(
        lambda *refs: wind_body(cap, sources, *refs),
        out_shape=(
            jax.ShapeDtypeStruct((2, CELLS, LANES), F32),
            jax.ShapeDtypeStruct((CELLS, 8, LANES), F32),
            jax.ShapeDtypeStruct((CELLS, DIRS, LANES), F32),
            jax.ShapeDtypeStruct((CELLS, DIRS, LANES), F32),
        ),
        in_specs=[vmem_spec()] * (5 + len(pieces)),
        out_specs=(vmem_spec(),) * 4,
        scratch_shapes=[pltpu.VMEM((8 * sources, LANES), F32)],
        compiler_params=pltpu.CompilerParams(vmem_limit_bytes=VMEM),
        cost_estimate=pl.CostEstimate(flops=0, bytes_accessed=2000000, transcendentals=0),
        name="surface_wind",
    )(slots, weights, ANGLES, sea, refr, *pieces)


def chunk_pass(
    first, count, scal, ang, x, from_west, from_east, ghosts, sea8, turn, proj, zs, gs, out, out_first
):
    lane = lane_ids()
    sub = lax.broadcasted_iota(jnp.int32, (8, LANES), 0)
    near_rows = (0, 8, 34, 42, 46)

    def one(i, kk, sums):
        k = first + i * GROUP + kk
        cour = scal[0, k]
        bend = scal[1, k]
        rate = scal[2, k]
        slow = scal[3, k]
        for b, j0 in enumerate(BLOCKS):
            w0, w1, w2, w3 = stencil(cour * ang[0, pl.ds(j0, 8), :])
            v0, v1, v2, v3 = stencil(cour * ang[1, pl.ds(j0, 8), :])
            cells = [x[k, pl.ds(c + 4 * j0, 8, stride=4), :] for c in range(CELLS)]
            west = from_west[halo_at(i, kk, near_rows[b], 8), :]
            east = from_east[halo_at(i, kk, near_rows[b], 8), :]
            plus = [west, *cells, east]
            minus = plus[::-1]
            if b == 0:
                far, seq = from_west[halo_at(i, kk, 16, 8), :], plus
            elif b == 2:
                far, seq = from_east[halo_at(i, kk, 23, 8), :], minus
            elif b == 4:
                far, seq = from_west[halo_at(i, kk, 26, 8), :], plus
            else:
                if b == 1:
                    pos = sub < 1
                    far_p, far_m = from_west[halo_at(i, kk, 24, 8), :], from_east[halo_at(i, kk, 15, 8), :]
                else:
                    pos = sub >= 3
                    far_p, far_m = from_west[halo_at(i, kk, 22, 8), :], from_east[halo_at(i, kk, 31, 8), :]
                far = jnp.where(pos, far_p, far_m)
                seq = [jnp.where(pos, p, m) for p, m in zip(plus, minus)]
            seq = [far, *seq]
            moved = [
                w0 * seq[c] + w1 * seq[c + 1] + w2 * seq[c + 2] + w3 * seq[c + 3] for c in range(CELLS)
            ]
            if b == 2:
                moved = moved[::-1]
            elif b in (1, 3):
                moved = [jnp.where(pos, p, m) for p, m in zip(moved, moved[::-1])]
            for c in range(CELLS):
                z = moved[c] * sea8[c]
                ghost = ghosts[k, c, b]
                s1 = pltpu.roll(jnp.where(lane == LANES - 1, ghost, z), 1, 1)
                n1 = pltpu.roll(jnp.where(lane == 0, ghost, z), LANES - 1, 1)
                if b <= 2:
                    s2 = pltpu.roll(jnp.where(lane >= LANES - 2, ghost, z), 2, 1)
                if b >= 2:
                    n2 = pltpu.roll(jnp.where(lane < 2, ghost, z), LANES - 2, 1)
                if b < 2:
                    up, down, far = s1, n1, s2
                elif b > 2:
                    up, down, far = n1, s1, n2
                else:
                    p = sub < 2
                    up, down = jnp.where(p, s1, n1), jnp.where(p, n1, s1)
                    far = jnp.where(p, s2, n2)
                z = (v0 * far + v1 * up + v2 * z + v3 * down) * sea8[c]
                zs[kk, c, pl.ds(8 + j0, 8), :] = z
        out_sums = []
        for c in range(CELLS):
            zs[kk, c, pl.ds(8 + DIRS, 1), :] = zs[kk, c, pl.ds(8, 1), :]
            for b, j0 in enumerate(BLOCKS):
                own = zs[kk, c, pl.ds(8 + j0, 8), :]
                nxt = zs[kk, c, pl.ds(9 + j0, 8), :]
                s = bend * turn[c, pl.ds(j0, 8), :]
                gs[kk, c, pl.ds(8 + j0, 8), :] = jnp.maximum(s, 0.0) * own + jnp.minimum(s, 0.0) * nxt
            gs[kk, c, pl.ds(7, 1), :] = gs[kk, c, pl.ds(7 + DIRS, 1), :]
            total = sums[c]
            for b, j0 in enumerate(BLOCKS):
                own = zs[kk, c, pl.ds(8 + j0, 8), :]
                flux = gs[kk, c, pl.ds(8 + j0, 8), :]
                prev = gs[kk, c, pl.ds(7 + j0, 8), :]
                refracted = own - (flux - prev)
                total = total + (jnp.where(sub >= 4, refracted, 0.0) if b == 4 else refracted)
                growth = rate * jnp.maximum(proj[c, pl.ds(j0, 8), :] * slow - 1.0, 0.0)
                out[out_first + i * GROUP + kk, pl.ds(c + 4 * j0, 8, stride=4), :] = refracted * jnp.exp(growth)
            out_sums.append(total)
        return tuple(out_sums)

    def body(i, sums):
        for kk in range(GROUP):
            sums = one(i, kk, sums)
        return sums

    zero = jnp.zeros((8, LANES), F32)
    return lax.fori_loop(0, count // GROUP, body, (zero,) * CELLS)


def main_body(
    first, count, scal, ang, x, west, east, ghosts, sea8, turn, proj, out, energy, zs, gs
):
    sums = chunk_pass(first, count, scal, ang, x, west, east, ghosts, sea8, turn, proj, zs, gs, out, 0)
    for c in range(CELLS):
        energy[c] = sums[c]


def pass_scratch():
    return [pltpu.VMEM((GROUP, CELLS, 56, LANES), F32), pltpu.VMEM((GROUP, CELLS, 56, LANES), F32)]


def main_chunk(first, count, x, west, east, ghosts, tables):
    return pl.pallas_call(
        lambda *refs: main_body(first, count, *refs),
        out_shape=(
            jax.ShapeDtypeStruct((count, ROWS, LANES), F32),
            jax.ShapeDtypeStruct((CELLS, 8, LANES), F32),
        ),
        in_specs=[smem_spec()] + [vmem_spec()] * 8,
        out_specs=(vmem_spec(), vmem_spec()),
        scratch_shapes=pass_scratch(),
        compiler_params=pltpu.CompilerParams(vmem_limit_bytes=VMEM),
        cost_estimate=pl.CostEstimate(flops=0, bytes_accessed=1000000, transcendentals=0),
        name="chunk",
    )(SCALARS, ANGLES, x, west, east, ghosts, *tables)


def tail_body(sizes, scal, ang, x, west, east, ghosts, sea8, turn, proj, *rest):
    done = len(sizes) - 1
    parts, energies = rest[:done], rest[done : 2 * done]
    out_hbm, obuf, zs, gs, out_sem = rest[2 * done :]
    count = sizes[-1]
    first = FREQS - count
    sums = chunk_pass(
        first, count, scal, ang, x, west, east, ghosts, sea8, turn, proj, zs, gs, obuf, first
    )
    sub = lax.broadcasted_iota(jnp.int32, (8, LANES), 0)
    pattern = jnp.zeros((8, LANES), F32)
    for c in range(CELLS):
        total = sums[c]
        for energy in energies:
            total = total + energy[c]
        mean = jnp.sum(total, axis=0, keepdims=True) * (1.0 / (FREQS * DIRS))
        level = mean * (1.0 / energy_ref)
        pattern = jnp.where(sub % CELLS == c, damping_rate * (level * level), pattern)
    stores, at = [], 0
    for n, size in enumerate(sizes):
        def body(i, _, at=at, n=n):
            scale = jnp.exp(-(scal[4, at + i] * pattern))
            source, k = (parts[n], i) if n < done else (obuf, at + i)
            for r in range(0, ROWS, 8):
                obuf[at + i, pl.ds(r, 8), :] = source[k, pl.ds(r, 8), :] * scale
            return 0

        lax.fori_loop(0, size, body, 0)
        span = pl.ds(at, size)
        stores.append(pltpu.make_async_copy(obuf.at[span], out_hbm.at[span], out_sem.at[n]))
        stores[-1].start()
        at += size
    for store in stores:
        store.wait()


def tail_chunk(sizes, x, west, east, ghosts, tables, parts, energies):
    done = len(sizes) - 1
    return pl.pallas_call(
        lambda *refs: tail_body(sizes, *refs),
        out_shape=jax.ShapeDtypeStruct((FREQS, ROWS, LANES), F32),
        in_specs=[smem_spec()] + [vmem_spec()] * (8 + 2 * done),
        out_specs=any_spec(),
        scratch_shapes=[
            pltpu.VMEM((FREQS, ROWS, LANES), F32),
            *pass_scratch(),
            pltpu.SemaphoreType.DMA((done + 1,)),
        ],
        compiler_params=pltpu.CompilerParams(vmem_limit_bytes=VMEM),
        cost_estimate=pl.CostEstimate(flops=0, bytes_accessed=6000000, transcendentals=0),
        name="last_chunk",
    )(SCALARS, ANGLES, x, west, east, ghosts, *tables, *parts, *energies)


def ring(axis, wrap):
    size = lax.axis_size(axis)
    up = [(i, (i + 1) % size) for i in range(size if wrap else size - 1)]
    return up, [(j, i) for i, j in up]


def local(
    spectrum, sea_mask, refraction, atm_wind, hour_fraction, send_cells, recv_slots, recv_weights
):
    east_way, west_way = ring("lon", True)
    north_way, south_way = ring("lat", False)
    x = spectrum.reshape(FREQS, ROWS, LANES)
    tiles = lax.axis_size("lon")
    cap = send_cells.shape[1] // tiles
    firsts = [sum(CHUNKS[:n]) for n in range(len(CHUNKS))]

    def exchange(to_east, to_west):
        return lax.ppermute(to_east, "lon", east_way), lax.ppermute(to_west, "lon", west_way)

    *sends, packed = first_halos(
        x, CHUNKS[0], hour_fraction, atm_wind.reshape(4, LANES), send_cells
    )
    halos = [exchange(*sends)]
    q = pack_edges(x, sea_mask, packed)
    south = lax.ppermute(q, "lat", north_way)
    north = lax.ppermute(q, "lat", south_way)
    *sends, merged = middle_halos(x, tuple(zip(firsts, CHUNKS))[1:3], south, north, halos[0])
    halos += [exchange(*sends[:2]), exchange(*sends[2:])]
    west, east = (side[-8:] for side in halos[0])
    lists = [jnp.concatenate([packed, jnp.where(lax.axis_index("lon") % 2 == 0, east, west)])]
    step = 2
    while step < tiles:
        held = lists[0] if len(lists) == 1 else jnp.concatenate(lists)
        lists.append(lax.ppermute(held, "lon", [(i, i ^ step) for i in range(tiles)]))
        step *= 2
    surface_wind, *tables = surface(
        cap,
        tiles,
        lists,
        recv_slots.reshape(4 * CELLS, LANES),
        recv_weights.reshape(4 * CELLS, LANES),
        sea_mask,
        refraction,
    )
    halos.append(exchange(*last_halos(x, firsts[3], CHUNKS[3], *halos[1], tables[0])))
    ghosts = move_ghosts(CHUNKS[1], merged, *halos[1])

    parts, energies = [], []
    for n, (first, count) in enumerate(zip(firsts, CHUNKS)):
        west, east = halos[n]
        if n < len(CHUNKS) - 1:
            part, energy = main_chunk(first, count, x, west, east, ghosts, tables)
            parts.append(part)
            energies.append(energy)
        else:
            out = tail_chunk(CHUNKS, x, west, east, ghosts, tables, parts, energies)
    return (out.reshape(spectrum.shape), surface_wind)


def solution(mesh):
    in_specs = (
        P(None, None, "lon", "lat"),
        P("lon", "lat"),
        P(None, "lon", "lat"),
        P(None, None, ("lon", "lat")),
        P(),
        P(("lon", "lat"), None),
        P(None, "lon", "lat"),
        P(None, "lon", "lat"),
    )
    out_specs = (P(None, None, "lon", "lat"), P(None, "lon", "lat"))
    return jax.shard_map(local, mesh=mesh, in_specs=in_specs, out_specs=out_specs, check_vma=False)
```

```python
import math

import jax
import jax.numpy as jnp
import numpy as np
from jax import lax
from jax.experimental import pallas as pl
from jax.experimental.pallas import tpu as pltpu
from jax.sharding import PartitionSpec as P

base_freq = 0.035
freq_step = 1.1
courant_max = 0.9
gravity = 9.81
input_rate = 0.05
damping_rate = 0.8
energy_ref = 0.5

F32 = jnp.float32
FREQS = 36
DIRS = 36
CELLS = 4
LANES = 128
ROWS = DIRS * CELLS
BLOCKS = (0, 8, 16, 24, 28)
GROUP = 4
HALO = DIRS + DIRS // 2
NEAR_SPLIT = 16
FAR = DIRS // 2
PACK = 6
CHUNKS = (12, 8, 12, 4)
GROUPS = FREQS // PACK
PIECE = 4
EDGE_ROWS = 2 * (FREQS // PACK) * 8
VMEM = 32 * 1024 * 1024
FIRST_VMEM = 63000000

freqs = base_freq * freq_step ** np.arange(FREQS, dtype=np.float64)
spacing = 2.0 * math.pi / DIRS
theta = (np.arange(DIRS) + 0.5) * spacing
phi = (np.arange(DIRS) + 1.0) * spacing
ratio = base_freq / freqs
SCALARS = np.stack(
    [
        courant_max * ratio,
        np.sqrt(ratio),
        input_rate * freqs / freqs[-1],
        2.0 * math.pi * freqs / gravity,
        freqs / freqs[-1],
    ]
).astype(np.float32)
SCALARS = np.ascontiguousarray(np.broadcast_to(SCALARS[:, :, None], (5, FREQS, LANES)))
ANGLES = np.broadcast_to(
    np.stack(
        [np.abs(np.cos(theta)), np.abs(np.sin(theta)), np.cos(theta), np.sin(theta), np.sin(phi), np.cos(phi)]
    )[:, :, None],
    (6, DIRS, LANES),
).astype(np.float32)


def stencil(a):
    one_m = 1.0 - a * a
    beyond = a * one_m * (-1.0 / 6.0)
    half = a * (0.5 - 0.5 * a)
    down = half + beyond
    up = a - half - 2.0 * beyond
    return beyond, up - beyond, 1.0 + down - up, -down


def packed_weights():
    out = np.zeros((5, FREQS // PACK, 8, LANES), np.float64)
    for k in range(FREQS):
        for b, j0 in enumerate(BLOCKS):
            c = courant_max * ratio[k] * np.cos(theta[j0 : j0 + 8])
            far, up, own, down = stencil(np.abs(c))
            zero = np.zeros(8)
            pos = c > 0
            five = [
                np.where(pos, far, zero),
                np.where(pos, up, down),
                own,
                np.where(pos, down, up),
                np.where(pos, zero, far),
            ]
            lane = 4 * ((k % PACK) * len(BLOCKS) + b)
            for d in range(5):
                out[d, k // PACK, :, lane : lane + 4] = five[d][:, None]
    return out.astype(np.float32)


PACKED = packed_weights()


def any_spec():
    return pl.BlockSpec(memory_space=pl.ANY)


def vmem_spec():
    return pl.BlockSpec(memory_space=pltpu.VMEM)


def smem_spec():
    return pl.BlockSpec(memory_space=pltpu.SMEM)


def halo_rows(x, start, right, left, low, high):
    def body(i, _):
        for kk in range(GROUP):
            k = start + i * GROUP + kk
            for ref, near, far in ((right, 3, 2), (left, 0, 1)):
                if far == 2:
                    runs = ((16, 0, 8), (24, 8, 1), (25, 27, 8), (33, 35, 1))
                else:
                    runs = ((16, 9, 8), (24, 17, 8), (32, 25, 2))
                for cell, rows in (
                    (near, ((0, 0, 8), (8, 8, 8), (34, 16, 8), (42, 24, 8), (50, 32, 4))),
                    (far, runs),
                ):
                    for row, j, n in rows:
                        ref[halo_at(i, kk, row, n), :] = x[k, pl.ds(cell + 4 * j, n, stride=4), :]
        return 0

    lax.fori_loop(low // GROUP, high // GROUP, body, 0)


def halo_at(i, kk, row, n):
    return pl.ds(pl.multiple_of(i * (GROUP * HALO), 8) + HALO * kk + row, n)


def lane_ids():
    return lax.broadcasted_iota(jnp.int32, (8, LANES), 1)


def first_body(
    count, x_hbm, hour_hbm, wind_hbm, cells_hbm, right, left, packed, x, hour, wind, cells, sem, small
):
    copies = []
    for n in range(count // GROUP):
        span = pl.ds(n * GROUP, GROUP)
        copies.append(pltpu.make_async_copy(x_hbm.at[span], x.at[span], sem.at[n]))
        copies[-1].start()
    few = [
        pltpu.make_async_copy(wind_hbm, wind, small.at[0]),
        pltpu.make_async_copy(cells_hbm, cells, small.at[1]),
        pltpu.make_async_copy(hour_hbm, hour, small.at[2]),
    ]
    for copy in few:
        copy.start()
    for copy in few:
        copy.wait()
    late = hour[...]
    now = (1.0 - late) * wind[pl.ds(0, 2), :] + late * wind[pl.ds(2, 2), :]
    width = cells.shape[1]
    index = jnp.concatenate([cells[:, :LANES], cells[:, width - LANES :]] * 4, axis=0)
    table = jnp.concatenate([now[:1]] * 2 + [now[1:]] * 2 + [now[:1]] * 4, axis=0)
    listed = jnp.take_along_axis(table, index, axis=1)
    for ref, row in ((packed, 0), (right, count * HALO), (left, count * HALO)):
        ref[pl.ds(row, 8), :] = listed
    for n in range(count // GROUP):
        copies[n].wait()
        halo_rows(x, 0, right, left, n * GROUP, (n + 1) * GROUP)


def message(count, extra=0):
    return pltpu.VMEM((count * HALO + extra, LANES), F32)


def first_halos(x, count, hour, wind, cells):
    return pl.pallas_call(
        lambda *refs: first_body(count, *refs),
        out_shape=(message(count, 8), message(count, 8), jax.ShapeDtypeStruct((8, LANES), F32)),
        in_specs=[any_spec()] * 4,
        out_specs=(vmem_spec(),) * 3,
        scratch_shapes=[
            pltpu.VMEM((count, *x.shape[1:]), F32),
            pltpu.VMEM(hour.shape, F32),
            pltpu.VMEM(wind.shape, F32),
            pltpu.VMEM(cells.shape, cells.dtype),
            pltpu.SemaphoreType.DMA((count // GROUP,)),
            pltpu.SemaphoreType.DMA((3,)),
        ],
        compiler_params=pltpu.CompilerParams(vmem_limit_bytes=FIRST_VMEM),
        cost_estimate=pl.CostEstimate(flops=0, bytes_accessed=2000000, transcendentals=0),
        name="first_halos",
    )(x, hour, wind, cells)


def edge_body(x, sea, after, q):
    lane = lane_ids()
    block = lane // 4

    def body(g, _):
        for cell in range(CELLS):
            acc = jnp.zeros((8, LANES), F32)
            for r in range(PACK):
                for b, j0 in enumerate(BLOCKS):
                    at = r * len(BLOCKS) + b
                    rows = x[g * PACK + r, pl.ds(cell + 4 * j0, 8, stride=4), :]
                    acc = jnp.where(block == at, pltpu.roll(rows, (4 * at + 2) % LANES, 1), acc)
            q[cell, g] = acc
        return 0

    lax.fori_loop(0, GROUPS, body, 0)
    for cell in range(CELLS):
        mask = jnp.zeros((8, LANES), F32)
        for n, at in enumerate((LANES - 2, LANES - 1, 0, 1)):
            mask = jnp.where(lane % 4 == n, sea[pl.ds(cell, 1), pl.ds(at, 1)].astype(F32), mask)
        q[cell, GROUPS] = mask


def pack_edges(x, sea, after):
    return pl.pallas_call(
        edge_body,
        out_shape=jax.ShapeDtypeStruct((CELLS, GROUPS + 1, 8, LANES), F32),
        in_specs=[vmem_spec()] * 3,
        out_specs=vmem_spec(),
        compiler_params=pltpu.CompilerParams(vmem_limit_bytes=VMEM),
        cost_estimate=pl.CostEstimate(flops=0, bytes_accessed=4000000, transcendentals=0),
        name="pack_edges",
    )(x, sea, after)


def second_body(start, count, x, south, north, right, left, merged):
    row = count * HALO
    pick = lane_ids() % 4 < 2
    for c in range(CELLS):
        side, slot = (left, c) if c < 2 else (right, c - 2)
        for g in range(GROUPS + 1):
            both = jnp.where(pick, south[c, g], north[c, g])
            merged[c, g] = both
            if g < GROUPS:
                side[pl.ds(row + (slot * GROUPS + g) * 8, 8), :] = both
    halo_rows(x, start, right, left, 0, count)


def second_halos(x, start, count, south, north):
    return pl.pallas_call(
        lambda *refs: second_body(start, count, *refs),
        out_shape=(
            message(count, EDGE_ROWS),
            message(count, EDGE_ROWS),
            jax.ShapeDtypeStruct((CELLS, GROUPS + 1, 8, LANES), F32),
        ),
        in_specs=[vmem_spec()] * 3,
        out_specs=(vmem_spec(),) * 3,
        compiler_params=pltpu.CompilerParams(vmem_limit_bytes=VMEM),
        cost_estimate=pl.CostEstimate(flops=0, bytes_accessed=2000000, transcendentals=0),
        name="second_halos",
    )(x, south, north)


def later_halos(x, start, count, *after):
    return pl.pallas_call(
        lambda x, *refs: halo_rows(x, start, *refs[-2:], 0, count),
        out_shape=(message(count), message(count)),
        in_specs=[vmem_spec()] * (1 + len(after)),
        out_specs=(vmem_spec(),) * 2,
        compiler_params=pltpu.CompilerParams(vmem_limit_bytes=VMEM),
        cost_estimate=pl.CostEstimate(flops=0, bytes_accessed=1000000, transcendentals=0),
        name="later_halos",
    )(x, *after)


def ghost_body(count, merged, west, east, weights, ghosts):
    def body(g, _):
        rows = [
            pl.ds(pl.multiple_of(count * HALO + (n * GROUPS + g) * 8, 8), 8) for n in range(2)
        ]
        ext = [west[rows[0], :], west[rows[1], :]] + [merged[c, g] for c in range(CELLS)]
        ext += [east[rows[0], :], east[rows[1], :]]
        for c in range(CELLS):
            total = weights[0, g] * ext[c]
            for d in range(1, 5):
                total = total + weights[d, g] * ext[c + d]
            total = total * merged[c, GROUPS]
            for r in range(PACK):
                for b in range(len(BLOCKS)):
                    shift = LANES - (4 * (r * len(BLOCKS) + b) + 2)
                    ghosts[g * PACK + r, c, b] = pltpu.roll(total, shift, 1)
        return 0

    lax.fori_loop(0, GROUPS, body, 0)


def move_ghosts(count, merged, west, east):
    return pl.pallas_call(
        lambda *refs: ghost_body(count, *refs),
        out_shape=jax.ShapeDtypeStruct((FREQS, CELLS, len(BLOCKS), 8, LANES), F32),
        in_specs=[vmem_spec()] * 4,
        out_specs=vmem_spec(),
        compiler_params=pltpu.CompilerParams(vmem_limit_bytes=VMEM),
        cost_estimate=pl.CostEstimate(flops=0, bytes_accessed=2000000, transcendentals=0),
        name="move_ghosts",
    )(merged, west, east, PACKED)


def wind_body(cap, sources, slots, weights, ang, sea, refr, *rest):
    picked = [[jnp.zeros((8, LANES), F32) for _ in range(2)] for _ in range(2)]
    pieces, (wind, sea8, turn, proj, table) = rest[:-5], rest[-5:]
    at = 0
    for piece in pieces:
        table[pl.ds(at, piece.shape[0]), :] = piece[...]
        at += piece.shape[0]
    width = cap * sources
    me = lax.axis_index("lon")
    mine = cap * me
    for half in range(2):
        index = slots[pl.ds(8 * half, 8), :]
        for s in range(sources):
            place = index - cap * s
            here = (place >= 0) & (place < cap)
            place = jnp.clip(place, 0, cap - 1) + mine
            low = place < LANES
            place = jnp.where(low, place, place - (width - LANES))
            for c in range(2):
                row = [
                    jnp.broadcast_to(table[pl.ds(8 * (s ^ me) + 2 * c + n, 1), :], (8, LANES)) for n in range(2)
                ]
                value = [jnp.take_along_axis(r, place, axis=1) for r in row]
                value = jnp.where(low, value[0], value[1])
                picked[half][c] = jnp.where(here, value, picked[half][c])
    for c in range(2):
        total = weights[pl.ds(0, 8), :] * picked[0][c]
        total = total + weights[pl.ds(8, 8), :] * picked[1][c]
        wind[c] = total[:CELLS] + total[CELLS:]
    for cell in range(CELLS):
        row = pl.ds(cell, 1)
        sea8[cell] = jnp.broadcast_to(sea[row, :], (8, LANES)).astype(F32)
        for j0 in BLOCKS:
            j = pl.ds(j0, 8)
            turn[cell, j, :] = refr[0, row, :] * ang[4, j, :] - refr[1, row, :] * ang[5, j, :]
            proj[cell, j, :] = wind[0, row, :] * ang[2, j, :] + wind[1, row, :] * ang[3, j, :]


def surface(cap, sources, pieces, slots, weights, sea, refr):
    return pl.pallas_call(
        lambda *refs: wind_body(cap, sources, *refs),
        out_shape=(
            jax.ShapeDtypeStruct((2, CELLS, LANES), F32),
            jax.ShapeDtypeStruct((CELLS, 8, LANES), F32),
            jax.ShapeDtypeStruct((CELLS, DIRS, LANES), F32),
            jax.ShapeDtypeStruct((CELLS, DIRS, LANES), F32),
        ),
        in_specs=[vmem_spec()] * (5 + len(pieces)),
        out_specs=(vmem_spec(),) * 4,
        scratch_shapes=[pltpu.VMEM((8 * sources, LANES), F32)],
        compiler_params=pltpu.CompilerParams(vmem_limit_bytes=VMEM),
        cost_estimate=pl.CostEstimate(flops=0, bytes_accessed=2000000, transcendentals=0),
        name="surface_wind",
    )(slots, weights, ANGLES, sea, refr, *pieces)


def chunk_pass(
    first, count, scal, ang, x, from_west, from_east, ghosts, sea8, turn, proj, zs, gs, out, out_first
):
    lane = lane_ids()
    sub = lax.broadcasted_iota(jnp.int32, (8, LANES), 0)
    near_rows = (0, 8, 34, 42, 46)

    def one(i, kk, sums):
        k = first + i * GROUP + kk
        cour, bend, rate, slow = (scal[n, pl.ds(k, 1), :] for n in range(4))
        for b, j0 in enumerate(BLOCKS):
            w0, w1, w2, w3 = stencil(cour * ang[0, pl.ds(j0, 8), :])
            v0, v1, v2, v3 = stencil(cour * ang[1, pl.ds(j0, 8), :])
            cells = [x[k, pl.ds(c + 4 * j0, 8, stride=4), :] for c in range(CELLS)]
            west = from_west[halo_at(i, kk, near_rows[b], 8), :]
            east = from_east[halo_at(i, kk, near_rows[b], 8), :]
            plus = [west, *cells, east]
            minus = plus[::-1]
            if b == 0:
                far, seq = from_west[halo_at(i, kk, 16, 8), :], plus
            elif b == 2:
                far, seq = from_east[halo_at(i, kk, 23, 8), :], minus
            elif b == 4:
                far, seq = from_west[halo_at(i, kk, 26, 8), :], plus
            else:
                if b == 1:
                    pos = sub < 1
                    far_p, far_m = from_west[halo_at(i, kk, 24, 8), :], from_east[halo_at(i, kk, 15, 8), :]
                else:
                    pos = sub >= 3
                    far_p, far_m = from_west[halo_at(i, kk, 22, 8), :], from_east[halo_at(i, kk, 31, 8), :]
                far = jnp.where(pos, far_p, far_m)
                seq = [jnp.where(pos, p, m) for p, m in zip(plus, minus)]
            seq = [far, *seq]
            moved = [
                w0 * seq[c] + w1 * seq[c + 1] + w2 * seq[c + 2] + w3 * seq[c + 3] for c in range(CELLS)
            ]
            if b == 2:
                moved = moved[::-1]
            elif b in (1, 3):
                moved = [jnp.where(pos, p, m) for p, m in zip(moved, moved[::-1])]
            for c in range(CELLS):
                z = moved[c] * sea8[c]
                ghost = ghosts[k, c, b]
                s1 = pltpu.roll(jnp.where(lane == LANES - 1, ghost, z), 1, 1)
                n1 = pltpu.roll(jnp.where(lane == 0, ghost, z), LANES - 1, 1)
                if b <= 2:
                    s2 = pltpu.roll(jnp.where(lane >= LANES - 2, ghost, z), 2, 1)
                if b >= 2:
                    n2 = pltpu.roll(jnp.where(lane < 2, ghost, z), LANES - 2, 1)
                if b < 2:
                    up, down, far = s1, n1, s2
                elif b > 2:
                    up, down, far = n1, s1, n2
                else:
                    p = sub < 2
                    up, down = jnp.where(p, s1, n1), jnp.where(p, n1, s1)
                    far = jnp.where(p, s2, n2)
                z = (v0 * far + v1 * up + v2 * z + v3 * down) * sea8[c]
                zs[kk, c, pl.ds(8 + j0, 8), :] = z
        out_sums = []
        for c in range(CELLS):
            zs[kk, c, pl.ds(8 + DIRS, 1), :] = zs[kk, c, pl.ds(8, 1), :]
            for b, j0 in enumerate(BLOCKS):
                own = zs[kk, c, pl.ds(8 + j0, 8), :]
                nxt = zs[kk, c, pl.ds(9 + j0, 8), :]
                s = bend * turn[c, pl.ds(j0, 8), :]
                gs[kk, c, pl.ds(8 + j0, 8), :] = jnp.maximum(s, 0.0) * own + jnp.minimum(s, 0.0) * nxt
            gs[kk, c, pl.ds(7, 1), :] = gs[kk, c, pl.ds(7 + DIRS, 1), :]
            total = sums[c]
            for b, j0 in enumerate(BLOCKS):
                own = zs[kk, c, pl.ds(8 + j0, 8), :]
                flux = gs[kk, c, pl.ds(8 + j0, 8), :]
                prev = gs[kk, c, pl.ds(7 + j0, 8), :]
                refracted = own - (flux - prev)
                total = total + (jnp.where(sub >= 4, refracted, 0.0) if b == 4 else refracted)
                growth = rate * jnp.maximum(proj[c, pl.ds(j0, 8), :] * slow - 1.0, 0.0)
                out[out_first + i * GROUP + kk, pl.ds(c + 4 * j0, 8, stride=4), :] = refracted * jnp.exp(growth)
            out_sums.append(total)
        return tuple(out_sums)

    def body(i, sums):
        for kk in range(GROUP):
            sums = one(i, kk, sums)
        return sums

    zero = jnp.zeros((8, LANES), F32)
    return lax.fori_loop(0, count // GROUP, body, (zero,) * CELLS)


def main_body(
    first, count, scal, ang, x, west, east, ghosts, sea8, turn, proj, out, energy, zs, gs
):
    sums = chunk_pass(first, count, scal, ang, x, west, east, ghosts, sea8, turn, proj, zs, gs, out, 0)
    for c in range(CELLS):
        energy[c] = sums[c]


def pass_scratch():
    return [pltpu.VMEM((GROUP, CELLS, 56, LANES), F32), pltpu.VMEM((GROUP, CELLS, 56, LANES), F32)]


def main_chunk(first, count, x, west, east, ghosts, tables):
    return pl.pallas_call(
        lambda *refs: main_body(first, count, *refs),
        out_shape=(
            jax.ShapeDtypeStruct((count, ROWS, LANES), F32),
            jax.ShapeDtypeStruct((CELLS, 8, LANES), F32),
        ),
        in_specs=[vmem_spec()] * 9,
        out_specs=(vmem_spec(), vmem_spec()),
        scratch_shapes=pass_scratch(),
        compiler_params=pltpu.CompilerParams(vmem_limit_bytes=VMEM),
        cost_estimate=pl.CostEstimate(flops=0, bytes_accessed=1000000, transcendentals=0),
        name="chunk",
    )(SCALARS, ANGLES, x, west, east, ghosts, *tables)


def tail_body(sizes, scal, ang, x, west, east, ghosts, sea8, turn, proj, *rest):
    done = len(sizes) - 1
    parts, energies = rest[:done], rest[done : 2 * done]
    out_hbm, obuf, zs, gs, out_sem = rest[2 * done :]
    count = sizes[-1]
    first = FREQS - count
    sums = chunk_pass(
        first, count, scal, ang, x, west, east, ghosts, sea8, turn, proj, zs, gs, obuf, first
    )
    sub = lax.broadcasted_iota(jnp.int32, (8, LANES), 0)
    pattern = jnp.zeros((8, LANES), F32)
    for c in range(CELLS):
        total = sums[c]
        for energy in energies:
            total = total + energy[c]
        mean = jnp.sum(total, axis=0, keepdims=True) * (1.0 / (FREQS * DIRS))
        level = mean * (1.0 / energy_ref)
        pattern = jnp.where(sub % CELLS == c, damping_rate * (level * level), pattern)
    stores, at = [], 0
    for n, size in enumerate(sizes):
        for low in range(0, size, PIECE):
            high = min(low + PIECE, size)

            def body(i, _, at=at, n=n):
                scale = jnp.exp(-(scal[4, pl.ds(at + i, 1), :] * pattern))
                source, k = (parts[n], i) if n < done else (obuf, at + i)
                for r in range(0, ROWS, 8):
                    obuf[at + i, pl.ds(r, 8), :] = source[k, pl.ds(r, 8), :] * scale
                return 0

            lax.fori_loop(low, high, body, 0)
            span = pl.ds(at + low, high - low)
            stores.append(
                pltpu.make_async_copy(obuf.at[span], out_hbm.at[span], out_sem.at[len(stores)])
            )
            stores[-1].start()
        at += size
    for store in stores:
        store.wait()


def tail_chunk(sizes, x, west, east, ghosts, tables, parts, energies):
    done = len(sizes) - 1
    return pl.pallas_call(
        lambda *refs: tail_body(sizes, *refs),
        out_shape=jax.ShapeDtypeStruct((FREQS, ROWS, LANES), F32),
        in_specs=[vmem_spec()] * (9 + 2 * done),
        out_specs=any_spec(),
        scratch_shapes=[
            pltpu.VMEM((FREQS, ROWS, LANES), F32),
            *pass_scratch(),
            pltpu.SemaphoreType.DMA((FREQS // PIECE,)),
        ],
        compiler_params=pltpu.CompilerParams(vmem_limit_bytes=VMEM),
        cost_estimate=pl.CostEstimate(flops=0, bytes_accessed=6000000, transcendentals=0),
        name="last_chunk",
    )(SCALARS, ANGLES, x, west, east, ghosts, *tables, *parts, *energies)


def ring(axis, wrap):
    size = lax.axis_size(axis)
    up = [(i, (i + 1) % size) for i in range(size if wrap else size - 1)]
    return up, [(j, i) for i, j in up]


def local(
    spectrum, sea_mask, refraction, atm_wind, hour_fraction, send_cells, recv_slots, recv_weights
):
    east_way, west_way = ring("lon", True)
    north_way, south_way = ring("lat", False)
    x = spectrum.reshape(FREQS, ROWS, LANES)
    tiles = lax.axis_size("lon")
    cap = send_cells.shape[1] // tiles
    firsts = [sum(CHUNKS[:n]) for n in range(len(CHUNKS))]

    def exchange(to_east, to_west):
        return lax.ppermute(to_east, "lon", east_way), lax.ppermute(to_west, "lon", west_way)

    *sends, packed = first_halos(
        x, CHUNKS[0], hour_fraction.reshape(1, 1), atm_wind.reshape(4, LANES), send_cells
    )
    halos = [exchange(*sends)]
    q = pack_edges(x, sea_mask, packed)
    south = lax.ppermute(q, "lat", north_way)
    north = lax.ppermute(q, "lat", south_way)
    *sends, merged = second_halos(x, firsts[1], CHUNKS[1], south, north)
    halos.append(exchange(*sends))
    halos.append(exchange(*later_halos(x, firsts[2], CHUNKS[2], *halos[0])))
    west, east = (side[-8:] for side in halos[0])
    lists = [jnp.concatenate([packed, jnp.where(lax.axis_index("lon") % 2 == 0, east, west)])]
    step = 2
    while step < tiles:
        held = lists[0] if len(lists) == 1 else jnp.concatenate(lists)
        lists.append(lax.ppermute(held, "lon", [(i, i ^ step) for i in range(tiles)]))
        step *= 2
    surface_wind, *tables = surface(
        cap,
        tiles,
        lists,
        recv_slots.reshape(4 * CELLS, LANES),
        recv_weights.reshape(4 * CELLS, LANES),
        sea_mask,
        refraction,
    )
    halos.append(exchange(*later_halos(x, firsts[3], CHUNKS[3], *halos[1], tables[0])))
    ghosts = move_ghosts(CHUNKS[1], merged, *halos[1])

    parts, energies = [], []
    for n, (first, count) in enumerate(zip(firsts, CHUNKS)):
        west, east = halos[n]
        if n < len(CHUNKS) - 1:
            part, energy = main_chunk(first, count, x, west, east, ghosts, tables)
            parts.append(part)
            energies.append(energy)
        else:
            out = tail_chunk(CHUNKS, x, west, east, ghosts, tables, parts, energies)
    return (out.reshape(spectrum.shape), surface_wind)


def solution(mesh):
    in_specs = (
        P(None, None, "lon", "lat"),
        P("lon", "lat"),
        P(None, "lon", "lat"),
        P(None, None, ("lon", "lat")),
        P(),
        P(("lon", "lat"), None),
        P(None, "lon", "lat"),
        P(None, "lon", "lat"),
    )
    out_specs = (P(None, None, "lon", "lat"), P(None, "lon", "lat"))
    return jax.shard_map(local, mesh=mesh, in_specs=in_specs, out_specs=out_specs, check_vma=False)
```

```python
import math

import jax
import jax.numpy as jnp
import numpy as np
from jax import lax
from jax.experimental import pallas as pl
from jax.experimental.pallas import tpu as pltpu
from jax.sharding import PartitionSpec as P

base_freq = 0.035
freq_step = 1.1
courant_max = 0.9
gravity = 9.81
input_rate = 0.05
damping_rate = 0.8
energy_ref = 0.5

F32 = jnp.float32
FREQS = 36
DIRS = 36
CELLS = 4
LANES = 128
ROWS = DIRS * CELLS
BLOCKS = (0, 8, 16, 24, 28)
GROUP = 4
HALO = DIRS + DIRS // 2
NEAR_SPLIT = 16
FAR = DIRS // 2
PACK = 6
CHUNKS = (12, 8, 12, 4)
GROUPS = FREQS // PACK
PIECE = 4
EDGE_ROWS = 2 * (FREQS // PACK) * 8
VMEM = 32 * 1024 * 1024
FIRST_VMEM = 63000000

freqs = base_freq * freq_step ** np.arange(FREQS, dtype=np.float64)
spacing = 2.0 * math.pi / DIRS
theta = (np.arange(DIRS) + 0.5) * spacing
phi = (np.arange(DIRS) + 1.0) * spacing
ratio = base_freq / freqs
SCALARS = np.stack(
    [
        courant_max * ratio,
        np.sqrt(ratio),
        input_rate * freqs / freqs[-1],
        2.0 * math.pi * freqs / gravity,
        freqs / freqs[-1],
    ]
).astype(np.float32)
SCALARS = np.ascontiguousarray(np.broadcast_to(SCALARS[:, :, None], (5, FREQS, LANES)))
ANGLES = np.broadcast_to(
    np.stack(
        [np.abs(np.cos(theta)), np.abs(np.sin(theta)), np.cos(theta), np.sin(theta), np.sin(phi), np.cos(phi)]
    )[:, :, None],
    (6, DIRS, LANES),
).astype(np.float32)


def stencil(a):
    one_m = 1.0 - a * a
    beyond = a * one_m * (-1.0 / 6.0)
    half = a * (0.5 - 0.5 * a)
    down = half + beyond
    up = a - half - 2.0 * beyond
    return beyond, up - beyond, 1.0 + down - up, -down


def packed_weights():
    out = np.zeros((5, FREQS // PACK, 8, LANES), np.float64)
    for k in range(FREQS):
        for b, j0 in enumerate(BLOCKS):
            c = courant_max * ratio[k] * np.cos(theta[j0 : j0 + 8])
            far, up, own, down = stencil(np.abs(c))
            zero = np.zeros(8)
            pos = c > 0
            five = [
                np.where(pos, far, zero),
                np.where(pos, up, down),
                own,
                np.where(pos, down, up),
                np.where(pos, zero, far),
            ]
            lane = 4 * ((k % PACK) * len(BLOCKS) + b)
            for d in range(5):
                out[d, k // PACK, :, lane : lane + 4] = five[d][:, None]
    return out.astype(np.float32)


PACKED = packed_weights()


def any_spec():
    return pl.BlockSpec(memory_space=pl.ANY)


def vmem_spec():
    return pl.BlockSpec(memory_space=pltpu.VMEM)


def smem_spec():
    return pl.BlockSpec(memory_space=pltpu.SMEM)


def is_even():
    return jnp.full((8, LANES), lax.axis_index("lon") % 2) == 0


def halo_rows(x, start, one, two, low, high):
    even = is_even()

    def body(i, _):
        for kk in range(GROUP):
            k = start + i * GROUP + kk
            near = ((0, 0, 0, 8), (8, 8, 8, 8), (34, 16, 16, 8), (42, 24, 24, 8), (50, 32, 32, 4))
            far = ((16, 0, 9, 8), (24, 8, 17, 1), (25, 27, 18, 8), (33, 35, 26, 1))
            for cell_e, cell_w, runs in ((3, 0, near), (2, 1, far)):
                for row, j_e, j_w, n in runs:
                    east = x[k, pl.ds(cell_e + 4 * j_e, n, stride=4), :]
                    west = x[k, pl.ds(cell_w + 4 * j_w, n, stride=4), :]
                    one[halo_at(i, kk, row, n), :] = jnp.where(even[:n], east, west)
                    two[halo_at(i, kk, row, n), :] = jnp.where(even[:n], west, east)
        return 0

    lax.fori_loop(low // GROUP, high // GROUP, body, 0)


def halo_at(i, kk, row, n):
    return pl.ds(pl.multiple_of(i * (GROUP * HALO), 8) + HALO * kk + row, n)


def lane_ids():
    return lax.broadcasted_iota(jnp.int32, (8, LANES), 1)


def first_body(
    count, x_hbm, hour_hbm, wind_hbm, cells_hbm, one, two, packed, x, hour, wind, cells, sem, small
):
    copies = []
    for n in range(count // GROUP):
        span = pl.ds(n * GROUP, GROUP)
        copies.append(pltpu.make_async_copy(x_hbm.at[span], x.at[span], sem.at[n]))
        copies[-1].start()
    few = [
        pltpu.make_async_copy(wind_hbm, wind, small.at[0]),
        pltpu.make_async_copy(cells_hbm, cells, small.at[1]),
        pltpu.make_async_copy(hour_hbm, hour, small.at[2]),
    ]
    for copy in few:
        copy.start()
    for copy in few:
        copy.wait()
    late = hour[...]
    now = (1.0 - late) * wind[pl.ds(0, 2), :] + late * wind[pl.ds(2, 2), :]
    width = cells.shape[1]
    index = jnp.concatenate([cells[:, :LANES], cells[:, width - LANES :]] * 4, axis=0)
    table = jnp.concatenate([now[:1]] * 2 + [now[1:]] * 2 + [now[:1]] * 4, axis=0)
    listed = jnp.take_along_axis(table, index, axis=1)
    packed[...] = listed
    one[pl.ds(count * HALO, 8), :] = listed
    for n in range(count // GROUP):
        copies[n].wait()
        halo_rows(x, 0, one, two, n * GROUP, (n + 1) * GROUP)


def message(count, extra=0):
    return pltpu.VMEM((count * HALO + extra, LANES), F32)


def first_halos(x, count, hour, wind, cells):
    return pl.pallas_call(
        lambda *refs: first_body(count, *refs),
        out_shape=(message(count, 8), message(count), jax.ShapeDtypeStruct((8, LANES), F32)),
        in_specs=[any_spec()] * 4,
        out_specs=(vmem_spec(),) * 3,
        scratch_shapes=[
            pltpu.VMEM((count, *x.shape[1:]), F32),
            pltpu.VMEM(hour.shape, F32),
            pltpu.VMEM(wind.shape, F32),
            pltpu.VMEM(cells.shape, cells.dtype),
            pltpu.SemaphoreType.DMA((count // GROUP,)),
            pltpu.SemaphoreType.DMA((3,)),
        ],
        compiler_params=pltpu.CompilerParams(vmem_limit_bytes=FIRST_VMEM),
        cost_estimate=pl.CostEstimate(flops=0, bytes_accessed=2000000, transcendentals=0),
        name="first_halos",
    )(x, hour, wind, cells)


def edge_body(x, sea, after, q):
    lane = lane_ids()
    block = lane // 4

    def body(g, _):
        for cell in range(CELLS):
            acc = jnp.zeros((8, LANES), F32)
            for r in range(PACK):
                for b, j0 in enumerate(BLOCKS):
                    at = r * len(BLOCKS) + b
                    rows = x[g * PACK + r, pl.ds(cell + 4 * j0, 8, stride=4), :]
                    acc = jnp.where(block == at, pltpu.roll(rows, (4 * at + 2) % LANES, 1), acc)
            q[cell, g] = acc
        return 0

    lax.fori_loop(0, GROUPS, body, 0)
    for cell in range(CELLS):
        mask = jnp.zeros((8, LANES), F32)
        for n, at in enumerate((LANES - 2, LANES - 1, 0, 1)):
            mask = jnp.where(lane % 4 == n, sea[pl.ds(cell, 1), pl.ds(at, 1)].astype(F32), mask)
        q[cell, GROUPS] = mask


def pack_edges(x, sea, after):
    return pl.pallas_call(
        edge_body,
        out_shape=jax.ShapeDtypeStruct((CELLS, GROUPS + 1, 8, LANES), F32),
        in_specs=[vmem_spec()] * 3,
        out_specs=vmem_spec(),
        compiler_params=pltpu.CompilerParams(vmem_limit_bytes=VMEM),
        cost_estimate=pl.CostEstimate(flops=0, bytes_accessed=4000000, transcendentals=0),
        name="pack_edges",
    )(x, sea, after)


def second_body(start, count, x, south, north, one, two, merged):
    pick = lane_ids() % 4 < 2
    even = is_even()

    def body(g, _):
        both = [jnp.where(pick, south[c, g], north[c, g]) for c in range(CELLS)]
        for c in range(CELLS):
            merged[c, g] = both[c]
        for n in range(2):
            row = pl.ds(pl.multiple_of(count * HALO + (n * GROUPS + g) * 8, 8), 8)
            one[row, :] = jnp.where(even, both[2 + n], both[n])
            two[row, :] = jnp.where(even, both[n], both[2 + n])
        return 0

    lax.fori_loop(0, GROUPS, body, 0)
    for c in range(CELLS):
        merged[c, GROUPS] = jnp.where(pick, south[c, GROUPS], north[c, GROUPS])
    halo_rows(x, start, one, two, 0, count)


def second_halos(x, start, count, south, north):
    return pl.pallas_call(
        lambda *refs: second_body(start, count, *refs),
        out_shape=(
            message(count, EDGE_ROWS),
            message(count, EDGE_ROWS),
            jax.ShapeDtypeStruct((CELLS, GROUPS + 1, 8, LANES), F32),
        ),
        in_specs=[vmem_spec()] * 3,
        out_specs=(vmem_spec(),) * 3,
        compiler_params=pltpu.CompilerParams(vmem_limit_bytes=VMEM),
        cost_estimate=pl.CostEstimate(flops=0, bytes_accessed=2000000, transcendentals=0),
        name="second_halos",
    )(x, south, north)


def later_halos(x, start, count, *after):
    return pl.pallas_call(
        lambda x, *refs: halo_rows(x, start, *refs[-2:], 0, count),
        out_shape=(message(count), message(count)),
        in_specs=[vmem_spec()] * (1 + len(after)),
        out_specs=(vmem_spec(),) * 2,
        compiler_params=pltpu.CompilerParams(vmem_limit_bytes=VMEM),
        cost_estimate=pl.CostEstimate(flops=0, bytes_accessed=1000000, transcendentals=0),
        name="later_halos",
    )(x, *after)


def ghost_body(count, merged, one, two, weights, ghosts):
    even = is_even()

    def body(g, _):
        rows = [
            pl.ds(pl.multiple_of(count * HALO + (n * GROUPS + g) * 8, 8), 8) for n in range(2)
        ]
        west = [jnp.where(even, two[row, :], one[row, :]) for row in rows]
        east = [jnp.where(even, one[row, :], two[row, :]) for row in rows]
        ext = west + [merged[c, g] for c in range(CELLS)] + east
        for c in range(CELLS):
            total = weights[0, g] * ext[c]
            for d in range(1, 5):
                total = total + weights[d, g] * ext[c + d]
            total = total * merged[c, GROUPS]
            for r in range(PACK):
                for b in range(len(BLOCKS)):
                    shift = LANES - (4 * (r * len(BLOCKS) + b) + 2)
                    ghosts[g * PACK + r, c, b] = pltpu.roll(total, shift, 1)
        return 0

    lax.fori_loop(0, GROUPS, body, 0)


def move_ghosts(count, merged, one, two):
    return pl.pallas_call(
        lambda *refs: ghost_body(count, *refs),
        out_shape=jax.ShapeDtypeStruct((FREQS, CELLS, len(BLOCKS), 8, LANES), F32),
        in_specs=[vmem_spec()] * 4,
        out_specs=vmem_spec(),
        compiler_params=pltpu.CompilerParams(vmem_limit_bytes=VMEM),
        cost_estimate=pl.CostEstimate(flops=0, bytes_accessed=2000000, transcendentals=0),
        name="move_ghosts",
    )(merged, one, two, PACKED)


def wind_body(cap, sources, slots, weights, ang, sea, refr, *rest):
    picked = [[jnp.zeros((8, LANES), F32) for _ in range(2)] for _ in range(2)]
    pieces, (wind, sea8, turn, proj, table) = rest[:-5], rest[-5:]
    at = 0
    for piece in pieces:
        table[pl.ds(at, piece.shape[0]), :] = piece[...]
        at += piece.shape[0]
    width = cap * sources
    me = lax.axis_index("lon")
    mine = cap * me
    for half in range(2):
        index = slots[pl.ds(8 * half, 8), :]
        for s in range(sources):
            place = index - cap * s
            here = (place >= 0) & (place < cap)
            place = jnp.clip(place, 0, cap - 1) + mine
            low = place < LANES
            place = jnp.where(low, place, place - (width - LANES))
            for c in range(2):
                row = [
                    jnp.broadcast_to(table[pl.ds(8 * (s ^ me) + 2 * c + n, 1), :], (8, LANES)) for n in range(2)
                ]
                value = [jnp.take_along_axis(r, place, axis=1) for r in row]
                value = jnp.where(low, value[0], value[1])
                picked[half][c] = jnp.where(here, value, picked[half][c])
    for c in range(2):
        total = weights[pl.ds(0, 8), :] * picked[0][c]
        total = total + weights[pl.ds(8, 8), :] * picked[1][c]
        wind[c] = total[:CELLS] + total[CELLS:]
    for cell in range(CELLS):
        row = pl.ds(cell, 1)
        sea8[cell] = jnp.broadcast_to(sea[row, :], (8, LANES)).astype(F32)
        for j0 in BLOCKS:
            j = pl.ds(j0, 8)
            turn[cell, j, :] = refr[0, row, :] * ang[4, j, :] - refr[1, row, :] * ang[5, j, :]
            proj[cell, j, :] = wind[0, row, :] * ang[2, j, :] + wind[1, row, :] * ang[3, j, :]


def surface(cap, sources, pieces, slots, weights, sea, refr):
    return pl.pallas_call(
        lambda *refs: wind_body(cap, sources, *refs),
        out_shape=(
            jax.ShapeDtypeStruct((2, CELLS, LANES), F32),
            jax.ShapeDtypeStruct((CELLS, 8, LANES), F32),
            jax.ShapeDtypeStruct((CELLS, DIRS, LANES), F32),
            jax.ShapeDtypeStruct((CELLS, DIRS, LANES), F32),
        ),
        in_specs=[vmem_spec()] * (5 + len(pieces)),
        out_specs=(vmem_spec(),) * 4,
        scratch_shapes=[pltpu.VMEM((8 * sources, LANES), F32)],
        compiler_params=pltpu.CompilerParams(vmem_limit_bytes=VMEM),
        cost_estimate=pl.CostEstimate(flops=0, bytes_accessed=2000000, transcendentals=0),
        name="surface_wind",
    )(slots, weights, ANGLES, sea, refr, *pieces)


def chunk_pass(
    first, count, scal, ang, x, one_ref, two_ref, ghosts, sea8, turn, proj, zs, gs, out, out_first
):
    lane = lane_ids()
    sub = lax.broadcasted_iota(jnp.int32, (8, LANES), 0)
    near_rows = (0, 8, 34, 42, 46)
    even = is_even()

    def from_west(rows):
        return jnp.where(even, two_ref[rows, :], one_ref[rows, :])

    def from_east(rows):
        return jnp.where(even, one_ref[rows, :], two_ref[rows, :])

    def one(i, kk, sums):
        k = first + i * GROUP + kk
        cour, bend, rate, slow = (scal[n, pl.ds(k, 1), :] for n in range(4))
        for b, j0 in enumerate(BLOCKS):
            w0, w1, w2, w3 = stencil(cour * ang[0, pl.ds(j0, 8), :])
            v0, v1, v2, v3 = stencil(cour * ang[1, pl.ds(j0, 8), :])
            cells = [x[k, pl.ds(c + 4 * j0, 8, stride=4), :] for c in range(CELLS)]
            west = from_west(halo_at(i, kk, near_rows[b], 8))
            east = from_east(halo_at(i, kk, near_rows[b], 8))
            plus = [west, *cells, east]
            minus = plus[::-1]
            if b == 0:
                far, seq = from_west(halo_at(i, kk, 16, 8)), plus
            elif b == 2:
                far, seq = from_east(halo_at(i, kk, 23, 8)), minus
            elif b == 4:
                far, seq = from_west(halo_at(i, kk, 26, 8)), plus
            else:
                if b == 1:
                    pos = sub < 1
                    far_p, far_m = from_west(halo_at(i, kk, 24, 8)), from_east(halo_at(i, kk, 15, 8))
                else:
                    pos = sub >= 3
                    far_p, far_m = from_west(halo_at(i, kk, 22, 8)), from_east(halo_at(i, kk, 31, 8))
                far = jnp.where(pos, far_p, far_m)
                seq = [jnp.where(pos, p, m) for p, m in zip(plus, minus)]
            seq = [far, *seq]
            moved = [
                w0 * seq[c] + w1 * seq[c + 1] + w2 * seq[c + 2] + w3 * seq[c + 3] for c in range(CELLS)
            ]
            if b == 2:
                moved = moved[::-1]
            elif b in (1, 3):
                moved = [jnp.where(pos, p, m) for p, m in zip(moved, moved[::-1])]
            for c in range(CELLS):
                z = moved[c] * sea8[c]
                ghost = ghosts[k, c, b]
                s1 = pltpu.roll(jnp.where(lane == LANES - 1, ghost, z), 1, 1)
                n1 = pltpu.roll(jnp.where(lane == 0, ghost, z), LANES - 1, 1)
                if b <= 2:
                    s2 = pltpu.roll(jnp.where(lane >= LANES - 2, ghost, z), 2, 1)
                if b >= 2:
                    n2 = pltpu.roll(jnp.where(lane < 2, ghost, z), LANES - 2, 1)
                if b < 2:
                    up, down, far = s1, n1, s2
                elif b > 2:
                    up, down, far = n1, s1, n2
                else:
                    p = sub < 2
                    up, down = jnp.where(p, s1, n1), jnp.where(p, n1, s1)
                    far = jnp.where(p, s2, n2)
                z = (v0 * far + v1 * up + v2 * z + v3 * down) * sea8[c]
                zs[kk, c, pl.ds(8 + j0, 8), :] = z
        out_sums = []
        for c in range(CELLS):
            zs[kk, c, pl.ds(8 + DIRS, 1), :] = zs[kk, c, pl.ds(8, 1), :]
            for b, j0 in enumerate(BLOCKS):
                own = zs[kk, c, pl.ds(8 + j0, 8), :]
                nxt = zs[kk, c, pl.ds(9 + j0, 8), :]
                s = bend * turn[c, pl.ds(j0, 8), :]
                gs[kk, c, pl.ds(8 + j0, 8), :] = jnp.maximum(s, 0.0) * own + jnp.minimum(s, 0.0) * nxt
            gs[kk, c, pl.ds(7, 1), :] = gs[kk, c, pl.ds(7 + DIRS, 1), :]
            total = sums[c]
            for b, j0 in enumerate(BLOCKS):
                own = zs[kk, c, pl.ds(8 + j0, 8), :]
                flux = gs[kk, c, pl.ds(8 + j0, 8), :]
                prev = gs[kk, c, pl.ds(7 + j0, 8), :]
                refracted = own - (flux - prev)
                total = total + (jnp.where(sub >= 4, refracted, 0.0) if b == 4 else refracted)
                growth = rate * jnp.maximum(proj[c, pl.ds(j0, 8), :] * slow - 1.0, 0.0)
                out[out_first + i * GROUP + kk, pl.ds(c + 4 * j0, 8, stride=4), :] = refracted * jnp.exp(growth)
            out_sums.append(total)
        return tuple(out_sums)

    def body(i, sums):
        for kk in range(GROUP):
            sums = one(i, kk, sums)
        return sums

    zero = jnp.zeros((8, LANES), F32)
    return lax.fori_loop(0, count // GROUP, body, (zero,) * CELLS)


def main_body(
    first, count, scal, ang, x, west, east, ghosts, sea8, turn, proj, out, energy, zs, gs
):
    sums = chunk_pass(first, count, scal, ang, x, west, east, ghosts, sea8, turn, proj, zs, gs, out, 0)
    for c in range(CELLS):
        energy[c] = sums[c]


def pass_scratch():
    return [pltpu.VMEM((GROUP, CELLS, 56, LANES), F32), pltpu.VMEM((GROUP, CELLS, 56, LANES), F32)]


def main_chunk(first, count, x, west, east, ghosts, tables):
    return pl.pallas_call(
        lambda *refs: main_body(first, count, *refs),
        out_shape=(
            jax.ShapeDtypeStruct((count, ROWS, LANES), F32),
            jax.ShapeDtypeStruct((CELLS, 8, LANES), F32),
        ),
        in_specs=[vmem_spec()] * 9,
        out_specs=(vmem_spec(), vmem_spec()),
        scratch_shapes=pass_scratch(),
        compiler_params=pltpu.CompilerParams(vmem_limit_bytes=VMEM),
        cost_estimate=pl.CostEstimate(flops=0, bytes_accessed=1000000, transcendentals=0),
        name="chunk",
    )(SCALARS, ANGLES, x, west, east, ghosts, *tables)


def tail_body(sizes, scal, ang, x, west, east, ghosts, sea8, turn, proj, *rest):
    done = len(sizes) - 1
    parts, energies = rest[:done], rest[done : 2 * done]
    out_hbm, obuf, zs, gs, out_sem = rest[2 * done :]
    count = sizes[-1]
    first = FREQS - count
    sums = chunk_pass(
        first, count, scal, ang, x, west, east, ghosts, sea8, turn, proj, zs, gs, obuf, first
    )
    sub = lax.broadcasted_iota(jnp.int32, (8, LANES), 0)
    pattern = jnp.zeros((8, LANES), F32)
    for c in range(CELLS):
        total = sums[c]
        for energy in energies:
            total = total + energy[c]
        mean = jnp.sum(total, axis=0, keepdims=True) * (1.0 / (FREQS * DIRS))
        level = mean * (1.0 / energy_ref)
        pattern = jnp.where(sub % CELLS == c, damping_rate * (level * level), pattern)
    stores, at = [], 0
    for n, size in enumerate(sizes):
        for low in range(0, size, PIECE):
            high = min(low + PIECE, size)

            def body(i, _, at=at, n=n):
                scale = jnp.exp(-(scal[4, pl.ds(at + i, 1), :] * pattern))
                source, k = (parts[n], i) if n < done else (obuf, at + i)
                for r in range(0, ROWS, 8):
                    obuf[at + i, pl.ds(r, 8), :] = source[k, pl.ds(r, 8), :] * scale
                return 0

            lax.fori_loop(low, high, body, 0)
            span = pl.ds(at + low, high - low)
            stores.append(
                pltpu.make_async_copy(obuf.at[span], out_hbm.at[span], out_sem.at[len(stores)])
            )
            stores[-1].start()
        at += size
    for store in stores:
        store.wait()


def tail_chunk(sizes, x, west, east, ghosts, tables, parts, energies):
    done = len(sizes) - 1
    return pl.pallas_call(
        lambda *refs: tail_body(sizes, *refs),
        out_shape=jax.ShapeDtypeStruct((FREQS, ROWS, LANES), F32),
        in_specs=[vmem_spec()] * (9 + 2 * done),
        out_specs=any_spec(),
        scratch_shapes=[
            pltpu.VMEM((FREQS, ROWS, LANES), F32),
            *pass_scratch(),
            pltpu.SemaphoreType.DMA((FREQS // PIECE,)),
        ],
        compiler_params=pltpu.CompilerParams(vmem_limit_bytes=VMEM),
        cost_estimate=pl.CostEstimate(flops=0, bytes_accessed=6000000, transcendentals=0),
        name="last_chunk",
    )(SCALARS, ANGLES, x, west, east, ghosts, *tables, *parts, *energies)


def line(axis):
    up = [(i, i + 1) for i in range(lax.axis_size(axis) - 1)]
    return up, [(j, i) for i, j in up]


def local(
    spectrum, sea_mask, refraction, atm_wind, hour_fraction, send_cells, recv_slots, recv_weights
):
    north_way, south_way = line("lat")
    x = spectrum.reshape(FREQS, ROWS, LANES)
    tiles = lax.axis_size("lon")
    swap_one = [(i, i ^ 1) for i in range(tiles)]
    swap_two = [(i, (i + 1 if i % 2 else i - 1) % tiles) for i in range(tiles)]
    cap = send_cells.shape[1] // tiles
    firsts = [sum(CHUNKS[:n]) for n in range(len(CHUNKS))]

    def exchange(one, two):
        return lax.ppermute(one, "lon", swap_one), lax.ppermute(two, "lon", swap_two)

    *sends, packed = first_halos(
        x, CHUNKS[0], hour_fraction.reshape(1, 1), atm_wind.reshape(4, LANES), send_cells
    )
    halos = [exchange(*sends)]
    q = pack_edges(x, sea_mask, packed)
    south = lax.ppermute(q, "lat", north_way)
    north = lax.ppermute(q, "lat", south_way)
    *sends, merged = second_halos(x, firsts[1], CHUNKS[1], south, north)
    halos.append(exchange(*sends))
    halos.append(exchange(*later_halos(x, firsts[2], CHUNKS[2], *halos[0])))
    ghosts = move_ghosts(CHUNKS[1], merged, *halos[1])

    lists = [jnp.concatenate([packed, halos[0][0][-8:]])]
    step = 2
    while step < tiles:
        held = lists[0] if len(lists) == 1 else jnp.concatenate(lists)
        lists.append(lax.ppermute(held, "lon", [(i, i ^ step) for i in range(tiles)]))
        step *= 2
    surface_wind, *tables = surface(
        cap,
        tiles,
        lists,
        recv_slots.reshape(4 * CELLS, LANES),
        recv_weights.reshape(4 * CELLS, LANES),
        sea_mask,
        refraction,
    )
    halos.append(exchange(*later_halos(x, firsts[3], CHUNKS[3], *halos[1], tables[0])))

    parts, energies = [], []
    for n, (first, count) in enumerate(zip(firsts, CHUNKS)):
        west, east = halos[n]
        if n < len(CHUNKS) - 1:
            part, energy = main_chunk(first, count, x, west, east, ghosts, tables)
            parts.append(part)
            energies.append(energy)
        else:
            out = tail_chunk(CHUNKS, x, west, east, ghosts, tables, parts, energies)
    return (out.reshape(spectrum.shape), surface_wind)


def solution(mesh):
    in_specs = (
        P(None, None, "lon", "lat"),
        P("lon", "lat"),
        P(None, "lon", "lat"),
        P(None, None, ("lon", "lat")),
        P(),
        P(("lon", "lat"), None),
        P(None, "lon", "lat"),
        P(None, "lon", "lat"),
    )
    out_specs = (P(None, None, "lon", "lat"), P(None, "lon", "lat"))
    return jax.shard_map(local, mesh=mesh, in_specs=in_specs, out_specs=out_specs, check_vma=False)
```

```python
import math

import jax
import jax.numpy as jnp
import numpy as np
from jax import lax
from jax.experimental import pallas as pl
from jax.experimental.pallas import tpu as pltpu
from jax.sharding import PartitionSpec as P

base_freq = 0.035
freq_step = 1.1
courant_max = 0.9
gravity = 9.81
input_rate = 0.05
damping_rate = 0.8
energy_ref = 0.5

F32 = jnp.float32
FREQS = 36
DIRS = 36
CELLS = 4
LANES = 128
ROWS = DIRS * CELLS
BLOCKS = (0, 8, 16, 24, 28)
GROUP = 4
HALO = DIRS + DIRS // 2
NEAR_SPLIT = 16
FAR = DIRS // 2
PACK = 6
CHUNKS = (12, 8, 12, 4)
GROUPS = FREQS // PACK
PIECE = 4
EDGE_ROWS = 2 * (FREQS // PACK) * 8
VMEM = 32 * 1024 * 1024
FIRST_VMEM = 63000000

freqs = base_freq * freq_step ** np.arange(FREQS, dtype=np.float64)
spacing = 2.0 * math.pi / DIRS
theta = (np.arange(DIRS) + 0.5) * spacing
phi = (np.arange(DIRS) + 1.0) * spacing
ratio = base_freq / freqs
log2_e = 1.0 / math.log(2.0)
rate = input_rate * freqs / freqs[-1] * log2_e
SCALARS = np.stack(
    [
        courant_max * ratio,
        np.sqrt(ratio),
        rate * 2.0 * math.pi * freqs / gravity,
        rate,
        damping_rate * freqs / freqs[-1] * log2_e,
    ]
).astype(np.float32)
SCALARS = np.ascontiguousarray(np.broadcast_to(SCALARS[:, :, None], (5, FREQS, LANES)))
ANGLES = np.broadcast_to(
    np.stack(
        [np.abs(np.cos(theta)), np.abs(np.sin(theta)), np.cos(theta), np.sin(theta), np.sin(phi), np.cos(phi)]
    )[:, :, None],
    (6, DIRS, LANES),
).astype(np.float32)


def stencil(a):
    one_m = 1.0 - a * a
    beyond = a * one_m * (-1.0 / 6.0)
    half = a * (0.5 - 0.5 * a)
    down = half + beyond
    up = a - half - 2.0 * beyond
    return beyond, up - beyond, 1.0 + down - up, -down


def packed_weights():
    out = np.zeros((5, FREQS // PACK, 8, LANES), np.float64)
    for k in range(FREQS):
        for b, j0 in enumerate(BLOCKS):
            c = courant_max * ratio[k] * np.cos(theta[j0 : j0 + 8])
            far, up, own, down = stencil(np.abs(c))
            zero = np.zeros(8)
            pos = c > 0
            five = [
                np.where(pos, far, zero),
                np.where(pos, up, down),
                own,
                np.where(pos, down, up),
                np.where(pos, zero, far),
            ]
            lane = 4 * ((k % PACK) * len(BLOCKS) + b)
            for d in range(5):
                out[d, k // PACK, :, lane : lane + 4] = five[d][:, None]
    return out.astype(np.float32)


PACKED = packed_weights()


def any_spec():
    return pl.BlockSpec(memory_space=pl.ANY)


def vmem_spec():
    return pl.BlockSpec(memory_space=pltpu.VMEM)


def smem_spec():
    return pl.BlockSpec(memory_space=pltpu.SMEM)


def is_even():
    return jnp.full((8, LANES), lax.axis_index("lon") % 2) == 0


def halo_rows(x, start, one, two, low, high):
    even = is_even()

    def body(i, _):
        for kk in range(GROUP):
            k = start + i * GROUP + kk
            near = ((0, 0, 0, 8), (8, 8, 8, 8), (34, 16, 16, 8), (42, 24, 24, 8), (50, 32, 32, 4))
            far = ((16, 0, 9, 8), (24, 8, 17, 1), (25, 27, 18, 8), (33, 35, 26, 1))
            for cell_e, cell_w, runs in ((3, 0, near), (2, 1, far)):
                for row, j_e, j_w, n in runs:
                    east = x[k, pl.ds(cell_e + 4 * j_e, n, stride=4), :]
                    west = x[k, pl.ds(cell_w + 4 * j_w, n, stride=4), :]
                    one[halo_at(i, kk, row, n), :] = jnp.where(even[:n], east, west)
                    two[halo_at(i, kk, row, n), :] = jnp.where(even[:n], west, east)
        return 0

    lax.fori_loop(low // GROUP, high // GROUP, body, 0)


def halo_at(i, kk, row, n):
    return pl.ds(pl.multiple_of(i * (GROUP * HALO), 8) + HALO * kk + row, n)


def lane_ids():
    return lax.broadcasted_iota(jnp.int32, (8, LANES), 1)


def first_body(count, x_hbm, wind_hbm, cells_hbm, one, two, packed, x, wind, cells, sem, small):
    few = [
        pltpu.make_async_copy(wind_hbm, wind, small.at[0]),
        pltpu.make_async_copy(cells_hbm, cells, small.at[1]),
    ]
    for copy in few:
        copy.start()
    copies = []
    for n in range(count // GROUP):
        span = pl.ds(n * GROUP, GROUP)
        copies.append(pltpu.make_async_copy(x_hbm.at[span], x.at[span], sem.at[n]))
        copies[-1].start()
    for copy in few:
        copy.wait()
    width = cells.shape[1]
    index = jnp.concatenate([cells[:, :LANES], cells[:, width - LANES :]] * 4, axis=0)
    table = jnp.concatenate([wind[pl.ds(n // 2, 1), :] for n in range(8)], axis=0)
    listed = jnp.take_along_axis(table, index, axis=1)
    packed[...] = listed
    one[pl.ds(count * HALO, 8), :] = listed
    for n in range(count // GROUP):
        copies[n].wait()
        halo_rows(x, 0, one, two, n * GROUP, (n + 1) * GROUP)


def message(count, extra=0):
    return pltpu.VMEM((count * HALO + extra, LANES), F32)


def first_halos(x, count, wind, cells):
    return pl.pallas_call(
        lambda *refs: first_body(count, *refs),
        out_shape=(message(count, 8), message(count), pltpu.VMEM((8, LANES), F32)),
        in_specs=[any_spec()] * 3,
        out_specs=(vmem_spec(),) * 3,
        scratch_shapes=[
            pltpu.VMEM((count, *x.shape[1:]), F32),
            pltpu.VMEM(wind.shape, F32),
            pltpu.VMEM(cells.shape, cells.dtype),
            pltpu.SemaphoreType.DMA((count // GROUP,)),
            pltpu.SemaphoreType.DMA((2,)),
        ],
        compiler_params=pltpu.CompilerParams(vmem_limit_bytes=FIRST_VMEM),
        cost_estimate=pl.CostEstimate(flops=0, bytes_accessed=2000000, transcendentals=0),
        name="first_halos",
    )(x, wind, cells)


def edge_body(x, sea, after, q):
    lane = lane_ids()
    block = lane // 4

    def body(g, _):
        for cell in range(CELLS):
            acc = jnp.zeros((8, LANES), F32)
            for r in range(PACK):
                for b, j0 in enumerate(BLOCKS):
                    at = r * len(BLOCKS) + b
                    rows = x[g * PACK + r, pl.ds(cell + 4 * j0, 8, stride=4), :]
                    acc = jnp.where(block == at, pltpu.roll(rows, (4 * at + 2) % LANES, 1), acc)
            q[cell, g] = acc
        return 0

    lax.fori_loop(0, GROUPS, body, 0)
    for cell in range(CELLS):
        mask = jnp.zeros((8, LANES), F32)
        for n, at in enumerate((LANES - 2, LANES - 1, 0, 1)):
            mask = jnp.where(lane % 4 == n, sea[pl.ds(cell, 1), pl.ds(at, 1)].astype(F32), mask)
        q[cell, GROUPS] = mask


def pack_edges(x, sea, after):
    return pl.pallas_call(
        edge_body,
        out_shape=pltpu.VMEM((CELLS, GROUPS + 1, 8, LANES), F32),
        in_specs=[vmem_spec()] * 3,
        out_specs=vmem_spec(),
        compiler_params=pltpu.CompilerParams(vmem_limit_bytes=VMEM),
        cost_estimate=pl.CostEstimate(flops=0, bytes_accessed=4000000, transcendentals=0),
        name="pack_edges",
    )(x, sea, after)


def second_body(start, count, x, south, north, one, two, merged):
    pick = lane_ids() % 4 < 2
    even = is_even()

    def body(g, _):
        both = [jnp.where(pick, south[c, g], north[c, g]) for c in range(CELLS)]
        for c in range(CELLS):
            merged[c, g] = both[c]
        for n in range(2):
            row = pl.ds(pl.multiple_of(count * HALO + (n * GROUPS + g) * 8, 8), 8)
            one[row, :] = jnp.where(even, both[2 + n], both[n])
            two[row, :] = jnp.where(even, both[n], both[2 + n])
        return 0

    lax.fori_loop(0, GROUPS, body, 0)
    for c in range(CELLS):
        merged[c, GROUPS] = jnp.where(pick, south[c, GROUPS], north[c, GROUPS])
    halo_rows(x, start, one, two, 0, count)


def second_halos(x, start, count, south, north):
    return pl.pallas_call(
        lambda *refs: second_body(start, count, *refs),
        out_shape=(
            message(count, EDGE_ROWS),
            message(count, EDGE_ROWS),
            pltpu.VMEM((CELLS, GROUPS + 1, 8, LANES), F32),
        ),
        in_specs=[vmem_spec()] * 3,
        out_specs=(vmem_spec(),) * 3,
        compiler_params=pltpu.CompilerParams(vmem_limit_bytes=VMEM),
        cost_estimate=pl.CostEstimate(flops=0, bytes_accessed=2000000, transcendentals=0),
        name="second_halos",
    )(x, south, north)


def later_halos(x, start, count, *after):
    return pl.pallas_call(
        lambda x, *refs: halo_rows(x, start, *refs[-2:], 0, count),
        out_shape=(message(count), message(count)),
        in_specs=[vmem_spec()] * (1 + len(after)),
        out_specs=(vmem_spec(),) * 2,
        compiler_params=pltpu.CompilerParams(vmem_limit_bytes=VMEM),
        cost_estimate=pl.CostEstimate(flops=0, bytes_accessed=1000000, transcendentals=0),
        name="later_halos",
    )(x, *after)


def ghost_body(count, merged, one, two, weights, ghosts):
    even = is_even()

    def body(g, _):
        rows = [
            pl.ds(pl.multiple_of(count * HALO + (n * GROUPS + g) * 8, 8), 8) for n in range(2)
        ]
        west = [jnp.where(even, two[row, :], one[row, :]) for row in rows]
        east = [jnp.where(even, one[row, :], two[row, :]) for row in rows]
        ext = west + [merged[c, g] for c in range(CELLS)] + east
        for c in range(CELLS):
            total = weights[0, g] * ext[c]
            for d in range(1, 5):
                total = total + weights[d, g] * ext[c + d]
            total = total * merged[c, GROUPS]
            for r in range(PACK):
                for b in range(len(BLOCKS)):
                    shift = LANES - (4 * (r * len(BLOCKS) + b) + 2)
                    ghosts[g * PACK + r, c, b] = pltpu.roll(total, shift, 1)
        return 0

    lax.fori_loop(0, GROUPS, body, 0)


def move_ghosts(count, merged, one, two):
    return pl.pallas_call(
        lambda *refs: ghost_body(count, *refs),
        out_shape=pltpu.VMEM((FREQS, CELLS, len(BLOCKS), 8, LANES), F32),
        in_specs=[vmem_spec()] * 4,
        out_specs=vmem_spec(),
        compiler_params=pltpu.CompilerParams(vmem_limit_bytes=VMEM),
        cost_estimate=pl.CostEstimate(flops=0, bytes_accessed=2000000, transcendentals=0),
        name="move_ghosts",
    )(merged, one, two, PACKED)


def wind_body(cap, sources, hour, slots, weights, ang, sea, refr, *rest):
    picked = [[jnp.zeros((8, LANES), F32) for _ in range(2)] for _ in range(2)]
    pieces, (wind, sea8, turn, proj, table) = rest[:-5], rest[-5:]
    at = 0
    for piece in pieces:
        table[pl.ds(at, piece.shape[0]), :] = piece[...]
        at += piece.shape[0]
    late = hour[...]
    width = cap * sources
    me = lax.axis_index("lon")
    mine = cap * me
    for half in range(2):
        index = slots[pl.ds(8 * half, 8), :]
        for s in range(sources):
            place = index - cap * s
            here = (place >= 0) & (place < cap)
            place = jnp.clip(place, 0, cap - 1) + mine
            low = place < LANES
            place = jnp.where(low, place, place - (width - LANES))
            for c in range(2):
                at = 8 * (s ^ me) + 2 * c
                row = [
                    (1.0 - late) * table[pl.ds(at + n, 1), :] + late * table[pl.ds(at + 4 + n, 1), :]
                    for n in range(2)
                ]
                row = [jnp.broadcast_to(r, (8, LANES)) for r in row]
                value = [jnp.take_along_axis(r, place, axis=1) for r in row]
                value = jnp.where(low, value[0], value[1])
                picked[half][c] = jnp.where(here, value, picked[half][c])
    for c in range(2):
        total = weights[pl.ds(0, 8), :] * picked[0][c]
        total = total + weights[pl.ds(8, 8), :] * picked[1][c]
        wind[c] = total[:CELLS] + total[CELLS:]
    for cell in range(CELLS):
        row = pl.ds(cell, 1)
        sea8[cell] = jnp.broadcast_to(sea[row, :], (8, LANES)).astype(F32)
        for j0 in BLOCKS:
            j = pl.ds(j0, 8)
            turn[cell, j, :] = refr[0, row, :] * ang[4, j, :] - refr[1, row, :] * ang[5, j, :]
            proj[cell, j, :] = wind[0, row, :] * ang[2, j, :] + wind[1, row, :] * ang[3, j, :]


def surface(cap, sources, hour, pieces, slots, weights, sea, refr):
    return pl.pallas_call(
        lambda *refs: wind_body(cap, sources, *refs),
        out_shape=(
            jax.ShapeDtypeStruct((2, CELLS, LANES), F32),
            pltpu.VMEM((CELLS, 8, LANES), F32),
            pltpu.VMEM((CELLS, DIRS, LANES), F32),
            pltpu.VMEM((CELLS, DIRS, LANES), F32),
        ),
        in_specs=[vmem_spec()] * (6 + len(pieces)),
        out_specs=(vmem_spec(),) * 4,
        scratch_shapes=[pltpu.VMEM((8 * sources, LANES), F32)],
        compiler_params=pltpu.CompilerParams(vmem_limit_bytes=VMEM),
        cost_estimate=pl.CostEstimate(flops=0, bytes_accessed=2000000, transcendentals=0),
        name="surface_wind",
    )(hour, slots, weights, ANGLES, sea, refr, *pieces)


def weight_body(scal, ang, after, table):
    def body(k, _):
        cour = scal[0, pl.ds(k, 1), :]
        for b, j0 in enumerate(BLOCKS):
            both = stencil(cour * ang[0, pl.ds(j0, 8), :]) + stencil(cour * ang[1, pl.ds(j0, 8), :])
            for n, weight in enumerate(both):
                table[k, b, n] = weight
        return 0

    lax.fori_loop(0, FREQS, body, 0)


def stencil_weights(after):
    return pl.pallas_call(
        weight_body,
        out_shape=pltpu.VMEM((FREQS, len(BLOCKS), 8, 8, LANES), F32),
        in_specs=[vmem_spec()] * 3,
        out_specs=vmem_spec(),
        compiler_params=pltpu.CompilerParams(vmem_limit_bytes=VMEM),
        cost_estimate=pl.CostEstimate(flops=0, bytes_accessed=2000000, transcendentals=0),
        name="stencil_weights",
    )(SCALARS, ANGLES, after)


def chunk_pass(
    first, count, scal, weights, x, one_ref, two_ref, ghosts, sea8, turn, proj, zs, gs, out, out_first
):
    lane = lane_ids()
    sub = lax.broadcasted_iota(jnp.int32, (8, LANES), 0)
    near_rows = (0, 8, 34, 42, 46)
    even = is_even()

    def from_west(rows):
        return jnp.where(even, two_ref[rows, :], one_ref[rows, :])

    def from_east(rows):
        return jnp.where(even, one_ref[rows, :], two_ref[rows, :])

    def one(i, kk, sums):
        k = first + i * GROUP + kk
        bend, gain, floor = (scal[n, pl.ds(k, 1), :] for n in range(1, 4))
        for b, j0 in enumerate(BLOCKS):
            w0, w1, w2, w3, v0, v1, v2, v3 = (weights[k, b, n] for n in range(8))
            cells = [x[k, pl.ds(c + 4 * j0, 8, stride=4), :] for c in range(CELLS)]
            west = from_west(halo_at(i, kk, near_rows[b], 8))
            east = from_east(halo_at(i, kk, near_rows[b], 8))
            plus = [west, *cells, east]
            minus = plus[::-1]
            if b == 0:
                far, seq = from_west(halo_at(i, kk, 16, 8)), plus
            elif b == 2:
                far, seq = from_east(halo_at(i, kk, 23, 8)), minus
            elif b == 4:
                far, seq = from_west(halo_at(i, kk, 26, 8)), plus
            else:
                if b == 1:
                    pos = sub < 1
                    far_p, far_m = from_west(halo_at(i, kk, 24, 8)), from_east(halo_at(i, kk, 15, 8))
                else:
                    pos = sub >= 3
                    far_p, far_m = from_west(halo_at(i, kk, 22, 8)), from_east(halo_at(i, kk, 31, 8))
                far = jnp.where(pos, far_p, far_m)
                seq = [jnp.where(pos, p, m) for p, m in zip(plus, minus)]
            seq = [far, *seq]
            moved = [
                w0 * seq[c] + w1 * seq[c + 1] + w2 * seq[c + 2] + w3 * seq[c + 3] for c in range(CELLS)
            ]
            if b == 2:
                moved = moved[::-1]
            elif b in (1, 3):
                moved = [jnp.where(pos, p, m) for p, m in zip(moved, moved[::-1])]
            for c in range(CELLS):
                z = moved[c] * sea8[c]
                ghost = ghosts[k, c, b]
                s1 = pltpu.roll(jnp.where(lane == LANES - 1, ghost, z), 1, 1)
                n1 = pltpu.roll(jnp.where(lane == 0, ghost, z), LANES - 1, 1)
                if b <= 2:
                    s2 = pltpu.roll(jnp.where(lane >= LANES - 2, ghost, z), 2, 1)
                if b >= 2:
                    n2 = pltpu.roll(jnp.where(lane < 2, ghost, z), LANES - 2, 1)
                if b < 2:
                    up, down, far = s1, n1, s2
                elif b > 2:
                    up, down, far = n1, s1, n2
                else:
                    p = sub < 2
                    up, down = jnp.where(p, s1, n1), jnp.where(p, n1, s1)
                    far = jnp.where(p, s2, n2)
                z = v0 * far + v1 * up + v2 * z + v3 * down
                zs[kk, c, pl.ds(8 + j0, 8), :] = z
        out_sums = []
        for c in range(CELLS):
            zs[kk, c, pl.ds(8 + DIRS, 1), :] = zs[kk, c, pl.ds(8, 1), :]
            for b, j0 in enumerate(BLOCKS):
                own = zs[kk, c, pl.ds(8 + j0, 8), :]
                nxt = zs[kk, c, pl.ds(9 + j0, 8), :]
                s = bend * turn[c, pl.ds(j0, 8), :]
                gs[kk, c, pl.ds(8 + j0, 8), :] = s * jnp.where(s > 0, own, nxt)
            gs[kk, c, pl.ds(7, 1), :] = gs[kk, c, pl.ds(7 + DIRS, 1), :]
            total = sums[c]
            for b, j0 in enumerate(BLOCKS):
                own = zs[kk, c, pl.ds(8 + j0, 8), :]
                flux = gs[kk, c, pl.ds(8 + j0, 8), :]
                prev = gs[kk, c, pl.ds(7 + j0, 8), :]
                refracted = own - (flux - prev)
                total = total + (jnp.where(sub >= 4, refracted, 0.0) if b == 4 else refracted)
                growth = jnp.maximum(proj[c, pl.ds(j0, 8), :] * gain - floor, 0.0)
                out[out_first + i * GROUP + kk, pl.ds(c + 4 * j0, 8, stride=4), :] = refracted * jnp.exp2(growth)
            out_sums.append(total)
        return tuple(out_sums)

    def body(i, sums):
        for kk in range(GROUP):
            sums = one(i, kk, sums)
        return sums

    zero = jnp.zeros((8, LANES), F32)
    return lax.fori_loop(0, count // GROUP, body, (zero,) * CELLS)


def main_body(
    first, count, scal, weights, x, west, east, ghosts, sea8, turn, proj, out, energy, zs, gs
):
    sums = chunk_pass(first, count, scal, weights, x, west, east, ghosts, sea8, turn, proj, zs, gs, out, 0)
    for c in range(CELLS):
        energy[c] = sums[c]


def pass_scratch():
    return [pltpu.VMEM((GROUP, CELLS, 56, LANES), F32), pltpu.VMEM((GROUP, CELLS, 56, LANES), F32)]


def main_chunk(first, count, weights, x, west, east, ghosts, tables):
    return pl.pallas_call(
        lambda *refs: main_body(first, count, *refs),
        out_shape=(
            pltpu.VMEM((count, ROWS, LANES), F32),
            pltpu.VMEM((CELLS, 8, LANES), F32),
        ),
        in_specs=[vmem_spec()] * 9,
        out_specs=(vmem_spec(), vmem_spec()),
        scratch_shapes=pass_scratch(),
        compiler_params=pltpu.CompilerParams(vmem_limit_bytes=VMEM),
        cost_estimate=pl.CostEstimate(flops=0, bytes_accessed=1000000, transcendentals=0),
        name="chunk",
    )(SCALARS, weights, x, west, east, ghosts, *tables)


def tail_body(sizes, scal, weights, x, west, east, ghosts, sea8, turn, proj, *rest):
    done = len(sizes) - 1
    parts, energies = rest[:done], rest[done : 2 * done]
    out_hbm, obuf, zs, gs, out_sem = rest[2 * done :]
    count = sizes[-1]
    first = FREQS - count
    sums = chunk_pass(
        first, count, scal, weights, x, west, east, ghosts, sea8, turn, proj, zs, gs, obuf, first
    )
    sub = lax.broadcasted_iota(jnp.int32, (8, LANES), 0)
    pattern = mask = jnp.zeros((8, LANES), F32)
    for c in range(CELLS):
        total = sums[c]
        for energy in energies:
            total = total + energy[c]
        mean = sea8[c] * (jnp.sum(total, axis=0, keepdims=True) * (1.0 / (FREQS * DIRS)))
        level = mean * (1.0 / energy_ref)
        pattern = jnp.where(sub % CELLS == c, level * level, pattern)
        mask = jnp.where(sub % CELLS == c, sea8[c], mask)
    stores, at = [], 0
    for n, size in enumerate(sizes):
        for low in range(0, size, PIECE):
            high = min(low + PIECE, size)

            def body(i, _, at=at, n=n):
                scale = jnp.exp2(-(scal[4, pl.ds(at + i, 1), :] * pattern)) * mask
                source, k = (parts[n], i) if n < done else (obuf, at + i)
                for r in range(0, ROWS, 8):
                    obuf[at + i, pl.ds(r, 8), :] = source[k, pl.ds(r, 8), :] * scale
                return 0

            lax.fori_loop(low, high, body, 0)
            span = pl.ds(at + low, high - low)
            stores.append(
                pltpu.make_async_copy(obuf.at[span], out_hbm.at[span], out_sem.at[len(stores)])
            )
            stores[-1].start()
        at += size
    for store in stores:
        store.wait()


def tail_chunk(sizes, weights, x, west, east, ghosts, tables, parts, energies):
    done = len(sizes) - 1
    return pl.pallas_call(
        lambda *refs: tail_body(sizes, *refs),
        out_shape=jax.ShapeDtypeStruct((FREQS, ROWS, LANES), F32),
        in_specs=[vmem_spec()] * (9 + 2 * done),
        out_specs=any_spec(),
        scratch_shapes=[
            pltpu.VMEM((FREQS, ROWS, LANES), F32),
            *pass_scratch(),
            pltpu.SemaphoreType.DMA((FREQS // PIECE,)),
        ],
        compiler_params=pltpu.CompilerParams(vmem_limit_bytes=VMEM),
        cost_estimate=pl.CostEstimate(flops=0, bytes_accessed=6000000, transcendentals=0),
        name="last_chunk",
    )(SCALARS, weights, x, west, east, ghosts, *tables, *parts, *energies)


def line(axis):
    up = [(i, i + 1) for i in range(lax.axis_size(axis) - 1)]
    return up, [(j, i) for i, j in up]


def local(
    spectrum, sea_mask, refraction, atm_wind, hour_fraction, send_cells, recv_slots, recv_weights
):
    north_way, south_way = line("lat")
    x = spectrum.reshape(FREQS, ROWS, LANES)
    tiles = lax.axis_size("lon")
    swap_one = [(i, i ^ 1) for i in range(tiles)]
    swap_two = [(i, (i + 1 if i % 2 else i - 1) % tiles) for i in range(tiles)]
    cap = send_cells.shape[1] // tiles
    firsts = [sum(CHUNKS[:n]) for n in range(len(CHUNKS))]

    def exchange(one, two):
        return lax.ppermute(one, "lon", swap_one), lax.ppermute(two, "lon", swap_two)

    *sends, packed = first_halos(
        x, CHUNKS[0], atm_wind.reshape(4, LANES), send_cells
    )
    halos = [exchange(*sends)]
    q = pack_edges(x, sea_mask, packed)
    weights = stencil_weights(packed)
    south = lax.ppermute(q, "lat", north_way)
    north = lax.ppermute(q, "lat", south_way)
    *sends, merged = second_halos(x, firsts[1], CHUNKS[1], south, north)
    halos.append(exchange(*sends))
    halos.append(exchange(*later_halos(x, firsts[2], CHUNKS[2], *halos[0], weights)))
    ghosts = move_ghosts(CHUNKS[1], merged, *halos[1])

    lists = [jnp.concatenate([packed, halos[0][0][-8:]])]
    step = 2
    while step < tiles:
        held = lists[0] if len(lists) == 1 else jnp.concatenate(lists)
        lists.append(lax.ppermute(held, "lon", [(i, i ^ step) for i in range(tiles)]))
        step *= 2
    surface_wind, *tables = surface(
        cap,
        tiles,
        hour_fraction.reshape(1, 1),
        lists,
        recv_slots.reshape(4 * CELLS, LANES),
        recv_weights.reshape(4 * CELLS, LANES),
        sea_mask,
        refraction,
    )
    halos.append(exchange(*later_halos(x, firsts[3], CHUNKS[3], *halos[1], tables[0])))

    parts, energies = [], []
    for n, (first, count) in enumerate(zip(firsts, CHUNKS)):
        west, east = halos[n]
        if n < len(CHUNKS) - 1:
            part, energy = main_chunk(first, count, weights, x, west, east, ghosts, tables)
            parts.append(part)
            energies.append(energy)
        else:
            out = tail_chunk(CHUNKS, weights, x, west, east, ghosts, tables, parts, energies)
    return (out.reshape(spectrum.shape), surface_wind)


def solution(mesh):
    in_specs = (
        P(None, None, "lon", "lat"),
        P("lon", "lat"),
        P(None, "lon", "lat"),
        P(None, None, ("lon", "lat")),
        P(),
        P(("lon", "lat"), None),
        P(None, "lon", "lat"),
        P(None, "lon", "lat"),
    )
    out_specs = (P(None, None, "lon", "lat"), P(None, "lon", "lat"))
    return jax.shard_map(local, mesh=mesh, in_specs=in_specs, out_specs=out_specs, check_vma=False)
```

```python
import math

import jax
import jax.numpy as jnp
import numpy as np
from jax import lax
from jax.experimental import pallas as pl
from jax.experimental.pallas import tpu as pltpu
from jax.sharding import PartitionSpec as P

base_freq = 0.035
freq_step = 1.1
courant_max = 0.9
gravity = 9.81
input_rate = 0.05
damping_rate = 0.8
energy_ref = 0.5

F32 = jnp.float32
FREQS = 36
DIRS = 36
CELLS = 4
LANES = 128
ROWS = DIRS * CELLS
BLOCKS = (0, 8, 16, 24, 28)
GROUP = 4
HALO = DIRS + DIRS // 2
NEAR_SPLIT = 16
FAR = DIRS // 2
PACK = 8
SPAN = LANES // PACK
OFFSETS, WIDTHS, EDGES = (0, 3, 6, 10, 13), (3, 3, 4, 3, 3), (0, 0, 0, 1, 1)
CHUNKS = (12, 8, 12, 4)
GROUPS = -(-FREQS // PACK)
PIECE = 4
EDGE_ROWS = 2 * (-(-FREQS // PACK)) * 8
VMEM = 32 * 1024 * 1024
FIRST_VMEM = 63000000

freqs = base_freq * freq_step ** np.arange(FREQS, dtype=np.float64)
spacing = 2.0 * math.pi / DIRS
theta = (np.arange(DIRS) + 0.5) * spacing
phi = (np.arange(DIRS) + 1.0) * spacing
ratio = base_freq / freqs
log2_e = 1.0 / math.log(2.0)
rate = input_rate * freqs / freqs[-1] * log2_e
SCALARS = np.stack(
    [
        courant_max * ratio,
        np.sqrt(ratio),
        rate * 2.0 * math.pi * freqs / gravity,
        rate,
        damping_rate * freqs / freqs[-1] * log2_e,
    ]
).astype(np.float32)
SCALARS = np.ascontiguousarray(np.broadcast_to(SCALARS[:, :, None], (5, FREQS, LANES)))
ANGLES = np.broadcast_to(
    np.stack(
        [np.abs(np.cos(theta)), np.abs(np.sin(theta)), np.cos(theta), np.sin(theta), np.sin(phi), np.cos(phi)]
    )[:, :, None],
    (6, DIRS, LANES),
).astype(np.float32)


def stencil(a):
    one_m = 1.0 - a * a
    beyond = a * one_m * (-1.0 / 6.0)
    half = a * (0.5 - 0.5 * a)
    down = half + beyond
    up = a - half - 2.0 * beyond
    return beyond, up - beyond, 1.0 + down - up, -down


def packed_weights():
    out = np.zeros((5, GROUPS, 8, LANES), np.float64)
    for k in range(FREQS):
        for b, j0 in enumerate(BLOCKS):
            c = courant_max * ratio[k] * np.cos(theta[j0 : j0 + 8])
            far, up, own, down = stencil(np.abs(c))
            zero = np.zeros(8)
            pos = c > 0
            five = [
                np.where(pos, far, zero),
                np.where(pos, up, down),
                own,
                np.where(pos, down, up),
                np.where(pos, zero, far),
            ]
            lane = (k % PACK) * SPAN + OFFSETS[b]
            for d in range(5):
                out[d, k // PACK, :, lane : lane + WIDTHS[b]] = five[d][:, None]
    return out.astype(np.float32)


PACKED = packed_weights()


def any_spec():
    return pl.BlockSpec(memory_space=pl.ANY)


def vmem_spec():
    return pl.BlockSpec(memory_space=pltpu.VMEM)


def smem_spec():
    return pl.BlockSpec(memory_space=pltpu.SMEM)


def is_even():
    return jnp.full((8, LANES), lax.axis_index("lon") % 2) == 0


def halo_rows(x, start, one, two, low, high):
    even = is_even()

    def body(i, _):
        for kk in range(GROUP):
            k = start + i * GROUP + kk
            near = ((0, 0, 0, 8), (8, 8, 8, 8), (34, 16, 16, 8), (42, 24, 24, 8), (50, 32, 32, 4))
            far = ((16, 0, 9, 8), (24, 8, 17, 1), (25, 27, 18, 8), (33, 35, 26, 1))
            for cell_e, cell_w, runs in ((3, 0, near), (2, 1, far)):
                for row, j_e, j_w, n in runs:
                    east = x[k, pl.ds(cell_e + 4 * j_e, n, stride=4), :]
                    west = x[k, pl.ds(cell_w + 4 * j_w, n, stride=4), :]
                    one[halo_at(i, kk, row, n), :] = jnp.where(even[:n], east, west)
                    two[halo_at(i, kk, row, n), :] = jnp.where(even[:n], west, east)
        return 0

    lax.fori_loop(low // GROUP, high // GROUP, body, 0)


def halo_at(i, kk, row, n):
    return pl.ds(pl.multiple_of(i * (GROUP * HALO), 8) + HALO * kk + row, n)


def lane_ids():
    return lax.broadcasted_iota(jnp.int32, (8, LANES), 1)


def first_body(count, x_hbm, wind_hbm, cells_hbm, one, two, packed, x, wind, cells, sem, small):
    few = [
        pltpu.make_async_copy(wind_hbm, wind, small.at[0]),
        pltpu.make_async_copy(cells_hbm, cells, small.at[1]),
    ]
    for copy in few:
        copy.start()
    copies = []
    for n in range(count // GROUP):
        span = pl.ds(n * GROUP, GROUP)
        copies.append(pltpu.make_async_copy(x_hbm.at[span], x.at[span], sem.at[n]))
        copies[-1].start()
    for copy in few:
        copy.wait()
    width = cells.shape[1]
    index = jnp.concatenate([cells[:, :LANES], cells[:, width - LANES :]] * 4, axis=0)
    table = jnp.concatenate([wind[pl.ds(n // 2, 1), :] for n in range(8)], axis=0)
    listed = jnp.take_along_axis(table, index, axis=1)
    packed[...] = listed
    one[pl.ds(count * HALO, 8), :] = listed
    for n in range(count // GROUP):
        copies[n].wait()
        halo_rows(x, 0, one, two, n * GROUP, (n + 1) * GROUP)


def message(count, extra=0):
    return pltpu.VMEM((count * HALO + extra, LANES), F32)


def first_halos(x, count, wind, cells):
    return pl.pallas_call(
        lambda *refs: first_body(count, *refs),
        out_shape=(message(count, 8), message(count), pltpu.VMEM((8, LANES), F32)),
        in_specs=[any_spec()] * 3,
        out_specs=(vmem_spec(),) * 3,
        scratch_shapes=[
            pltpu.VMEM((count, *x.shape[1:]), F32),
            pltpu.VMEM(wind.shape, F32),
            pltpu.VMEM(cells.shape, cells.dtype),
            pltpu.SemaphoreType.DMA((count // GROUP,)),
            pltpu.SemaphoreType.DMA((2,)),
        ],
        compiler_params=pltpu.CompilerParams(vmem_limit_bytes=FIRST_VMEM),
        cost_estimate=pl.CostEstimate(flops=0, bytes_accessed=2000000, transcendentals=0),
        name="first_halos",
    )(x, wind, cells)


def edge_ids():
    place = lane_ids() % SPAN
    edge = place
    for offset, first in zip(OFFSETS[1:], EDGES[1:]):
        edge = jnp.where(place >= offset, place - (offset - first), edge)
    return edge


def edge_shift(r, b):
    return (r * SPAN + OFFSETS[b] + 2 - EDGES[b]) % LANES


def edge_body(x, sea, after, q):
    lane = lane_ids()
    edge = edge_ids()

    def pack(g, count):
        for cell in range(CELLS):
            acc = jnp.zeros((8, LANES), F32)
            for r in range(count):
                for b, j0 in enumerate(BLOCKS):
                    rows = x[g * PACK + r, pl.ds(cell + 4 * j0, 8, stride=4), :]
                    rows = pltpu.roll(rows, edge_shift(r, b), 1)
                    acc = jnp.where(lane >= r * SPAN + OFFSETS[b], rows, acc)
            q[cell, g] = acc

    def body(g, _):
        pack(g, PACK)
        return 0

    lax.fori_loop(0, FREQS // PACK, body, 0)
    pack(GROUPS - 1, FREQS - (GROUPS - 1) * PACK)
    for cell in range(CELLS):
        mask = jnp.zeros((8, LANES), F32)
        for n, at in enumerate((LANES - 2, LANES - 1, 0, 1)):
            mask = jnp.where(edge == n, sea[pl.ds(cell, 1), pl.ds(at, 1)].astype(F32), mask)
        q[cell, GROUPS] = mask


def pack_edges(x, sea, after):
    return pl.pallas_call(
        edge_body,
        out_shape=pltpu.VMEM((CELLS, GROUPS + 1, 8, LANES), F32),
        in_specs=[vmem_spec()] * 3,
        out_specs=vmem_spec(),
        compiler_params=pltpu.CompilerParams(vmem_limit_bytes=VMEM),
        cost_estimate=pl.CostEstimate(flops=0, bytes_accessed=4000000, transcendentals=0),
        name="pack_edges",
    )(x, sea, after)


def second_body(start, count, x, south, north, one, two, merged):
    pick = edge_ids() < 2
    even = is_even()

    def body(g, _):
        both = [jnp.where(pick, south[c, g], north[c, g]) for c in range(CELLS)]
        for c in range(CELLS):
            merged[c, g] = both[c]
        for n in range(2):
            row = pl.ds(pl.multiple_of(count * HALO + (n * GROUPS + g) * 8, 8), 8)
            one[row, :] = jnp.where(even, both[2 + n], both[n])
            two[row, :] = jnp.where(even, both[n], both[2 + n])
        return 0

    lax.fori_loop(0, GROUPS, body, 0)
    for c in range(CELLS):
        merged[c, GROUPS] = jnp.where(pick, south[c, GROUPS], north[c, GROUPS])
    halo_rows(x, start, one, two, 0, count)


def second_halos(x, start, count, south, north):
    return pl.pallas_call(
        lambda *refs: second_body(start, count, *refs),
        out_shape=(
            message(count, EDGE_ROWS),
            message(count, EDGE_ROWS),
            pltpu.VMEM((CELLS, GROUPS + 1, 8, LANES), F32),
        ),
        in_specs=[vmem_spec()] * 3,
        out_specs=(vmem_spec(),) * 3,
        compiler_params=pltpu.CompilerParams(vmem_limit_bytes=VMEM),
        cost_estimate=pl.CostEstimate(flops=0, bytes_accessed=2000000, transcendentals=0),
        name="second_halos",
    )(x, south, north)


def later_halos(x, start, count, *after):
    return pl.pallas_call(
        lambda x, *refs: halo_rows(x, start, *refs[-2:], 0, count),
        out_shape=(message(count), message(count)),
        in_specs=[vmem_spec()] * (1 + len(after)),
        out_specs=(vmem_spec(),) * 2,
        compiler_params=pltpu.CompilerParams(vmem_limit_bytes=VMEM),
        cost_estimate=pl.CostEstimate(flops=0, bytes_accessed=1000000, transcendentals=0),
        name="later_halos",
    )(x, *after)


def ghost_body(count, merged, one, two, weights, ghosts, token):
    even = is_even()
    token[...] = jnp.zeros_like(token)

    def spread(g, freqs):
        rows = [
            pl.ds(pl.multiple_of(count * HALO + (n * GROUPS + g) * 8, 8), 8) for n in range(2)
        ]
        west = [jnp.where(even, two[row, :], one[row, :]) for row in rows]
        east = [jnp.where(even, one[row, :], two[row, :]) for row in rows]
        ext = west + [merged[c, g] for c in range(CELLS)] + east
        for c in range(CELLS):
            total = weights[0, g] * ext[c]
            for d in range(1, 5):
                total = total + weights[d, g] * ext[c + d]
            total = total * merged[c, GROUPS]
            for r in range(freqs):
                for b in range(len(BLOCKS)):
                    ghosts[g * PACK + r, c, b] = pltpu.roll(total, (LANES - edge_shift(r, b)) % LANES, 1)

    def body(g, _):
        spread(g, PACK)
        return 0

    lax.fori_loop(0, FREQS // PACK, body, 0)
    spread(GROUPS - 1, FREQS - (GROUPS - 1) * PACK)


def move_ghosts(count, merged, one, two):
    return pl.pallas_call(
        lambda *refs: ghost_body(count, *refs),
        out_shape=(
            pltpu.VMEM((FREQS, CELLS, len(BLOCKS), 8, LANES), F32),
            pltpu.VMEM((8, LANES), F32),
        ),
        in_specs=[vmem_spec()] * 4,
        out_specs=(vmem_spec(),) * 2,
        compiler_params=pltpu.CompilerParams(vmem_limit_bytes=VMEM),
        cost_estimate=pl.CostEstimate(flops=0, bytes_accessed=2000000, transcendentals=0),
        name="move_ghosts",
    )(merged, one, two, PACKED)


def wind_body(cap, sources, after, hour, slots, weights, ang, sea, refr, *rest):
    picked = [[jnp.zeros((8, LANES), F32) for _ in range(2)] for _ in range(2)]
    pieces, (wind, sea8, turn, proj, table) = rest[:-5], rest[-5:]
    at = 0
    for piece in pieces:
        table[pl.ds(at, piece.shape[0]), :] = piece[...]
        at += piece.shape[0]
    late = hour[...]
    width = cap * sources
    me = lax.axis_index("lon")
    mine = cap * me
    for half in range(2):
        index = slots[pl.ds(8 * half, 8), :]
        for s in range(sources):
            place = index - cap * s
            here = (place >= 0) & (place < cap)
            place = jnp.clip(place, 0, cap - 1) + mine
            low = place < LANES
            place = jnp.where(low, place, place - (width - LANES))
            for c in range(2):
                at = 8 * (s ^ me) + 2 * c
                row = [
                    (1.0 - late) * table[pl.ds(at + n, 1), :] + late * table[pl.ds(at + 4 + n, 1), :]
                    for n in range(2)
                ]
                row = [jnp.broadcast_to(r, (8, LANES)) for r in row]
                value = [jnp.take_along_axis(r, place, axis=1) for r in row]
                value = jnp.where(low, value[0], value[1])
                picked[half][c] = jnp.where(here, value, picked[half][c])
    for c in range(2):
        total = weights[pl.ds(0, 8), :] * picked[0][c]
        total = total + weights[pl.ds(8, 8), :] * picked[1][c]
        wind[c] = total[:CELLS] + total[CELLS:]
    for cell in range(CELLS):
        row = pl.ds(cell, 1)
        sea8[cell] = jnp.broadcast_to(sea[row, :], (8, LANES)).astype(F32)
        for j0 in BLOCKS:
            j = pl.ds(j0, 8)
            turn[cell, j, :] = refr[0, row, :] * ang[4, j, :] - refr[1, row, :] * ang[5, j, :]
            proj[cell, j, :] = wind[0, row, :] * ang[2, j, :] + wind[1, row, :] * ang[3, j, :]


def surface(cap, sources, after, hour, pieces, slots, weights, sea, refr):
    return pl.pallas_call(
        lambda *refs: wind_body(cap, sources, *refs),
        out_shape=(
            jax.ShapeDtypeStruct((2, CELLS, LANES), F32),
            pltpu.VMEM((CELLS, 8, LANES), F32),
            pltpu.VMEM((CELLS, DIRS, LANES), F32),
            pltpu.VMEM((CELLS, DIRS, LANES), F32),
        ),
        in_specs=[vmem_spec()] * (7 + len(pieces)),
        out_specs=(vmem_spec(),) * 4,
        scratch_shapes=[pltpu.VMEM((8 * sources, LANES), F32)],
        compiler_params=pltpu.CompilerParams(vmem_limit_bytes=VMEM),
        cost_estimate=pl.CostEstimate(flops=0, bytes_accessed=2000000, transcendentals=0),
        name="surface_wind",
    )(after, hour, slots, weights, ANGLES, sea, refr, *pieces)


def weight_body(scal, ang, after, table):
    def body(k, _):
        cour = scal[0, pl.ds(k, 1), :]
        for b, j0 in enumerate(BLOCKS):
            both = stencil(cour * ang[0, pl.ds(j0, 8), :]) + stencil(cour * ang[1, pl.ds(j0, 8), :])
            for n, weight in enumerate(both):
                table[k, b, n] = weight
        return 0

    lax.fori_loop(0, FREQS, body, 0)


def stencil_weights(after):
    return pl.pallas_call(
        weight_body,
        out_shape=pltpu.VMEM((FREQS, len(BLOCKS), 8, 8, LANES), F32),
        in_specs=[vmem_spec()] * 3,
        out_specs=vmem_spec(),
        compiler_params=pltpu.CompilerParams(vmem_limit_bytes=VMEM),
        cost_estimate=pl.CostEstimate(flops=0, bytes_accessed=2000000, transcendentals=0),
        name="stencil_weights",
    )(SCALARS, ANGLES, after)


def chunk_pass(
    first, count, scal, weights, x, one_ref, two_ref, ghosts, sea8, turn, proj, zs, gs, out, out_first
):
    lane = lane_ids()
    sub = lax.broadcasted_iota(jnp.int32, (8, LANES), 0)
    near_rows = (0, 8, 34, 42, 46)
    even = is_even()

    def from_west(rows):
        return jnp.where(even, two_ref[rows, :], one_ref[rows, :])

    def from_east(rows):
        return jnp.where(even, one_ref[rows, :], two_ref[rows, :])

    def one(i, kk, sums):
        k = first + i * GROUP + kk
        bend, gain, floor = (scal[n, pl.ds(k, 1), :] for n in range(1, 4))
        for b, j0 in enumerate(BLOCKS):
            w0, w1, w2, w3, v0, v1, v2, v3 = (weights[k, b, n] for n in range(8))
            cells = [x[k, pl.ds(c + 4 * j0, 8, stride=4), :] for c in range(CELLS)]
            west = from_west(halo_at(i, kk, near_rows[b], 8))
            east = from_east(halo_at(i, kk, near_rows[b], 8))
            plus = [west, *cells, east]
            minus = plus[::-1]
            if b == 0:
                far, seq = from_west(halo_at(i, kk, 16, 8)), plus
            elif b == 2:
                far, seq = from_east(halo_at(i, kk, 23, 8)), minus
            elif b == 4:
                far, seq = from_west(halo_at(i, kk, 26, 8)), plus
            else:
                if b == 1:
                    pos = sub < 1
                    far_p, far_m = from_west(halo_at(i, kk, 24, 8)), from_east(halo_at(i, kk, 15, 8))
                else:
                    pos = sub >= 3
                    far_p, far_m = from_west(halo_at(i, kk, 22, 8)), from_east(halo_at(i, kk, 31, 8))
                far = jnp.where(pos, far_p, far_m)
                seq = [jnp.where(pos, p, m) for p, m in zip(plus, minus)]
            seq = [far, *seq]
            moved = [
                w0 * seq[c] + w1 * seq[c + 1] + w2 * seq[c + 2] + w3 * seq[c + 3] for c in range(CELLS)
            ]
            if b == 2:
                moved = moved[::-1]
            elif b in (1, 3):
                moved = [jnp.where(pos, p, m) for p, m in zip(moved, moved[::-1])]
            for c in range(CELLS):
                z = moved[c] * sea8[c]
                ghost = ghosts[k, c, b]
                s1 = pltpu.roll(jnp.where(lane == LANES - 1, ghost, z), 1, 1)
                n1 = pltpu.roll(jnp.where(lane == 0, ghost, z), LANES - 1, 1)
                if b <= 2:
                    s2 = pltpu.roll(jnp.where(lane >= LANES - 2, ghost, z), 2, 1)
                if b >= 2:
                    n2 = pltpu.roll(jnp.where(lane < 2, ghost, z), LANES - 2, 1)
                if b < 2:
                    up, down, far = s1, n1, s2
                elif b > 2:
                    up, down, far = n1, s1, n2
                else:
                    p = sub < 2
                    up, down = jnp.where(p, s1, n1), jnp.where(p, n1, s1)
                    far = jnp.where(p, s2, n2)
                z = v0 * far + v1 * up + v2 * z + v3 * down
                zs[kk, c, pl.ds(8 + j0, 8), :] = z
        out_sums = []
        for c in range(CELLS):
            zs[kk, c, pl.ds(8 + DIRS, 1), :] = zs[kk, c, pl.ds(8, 1), :]
            for b, j0 in enumerate(BLOCKS):
                own = zs[kk, c, pl.ds(8 + j0, 8), :]
                nxt = zs[kk, c, pl.ds(9 + j0, 8), :]
                s = bend * turn[c, pl.ds(j0, 8), :]
                gs[kk, c, pl.ds(8 + j0, 8), :] = s * jnp.where(s > 0, own, nxt)
            gs[kk, c, pl.ds(7, 1), :] = gs[kk, c, pl.ds(7 + DIRS, 1), :]
            total = sums[c]
            for b, j0 in enumerate(BLOCKS):
                own = zs[kk, c, pl.ds(8 + j0, 8), :]
                flux = gs[kk, c, pl.ds(8 + j0, 8), :]
                prev = gs[kk, c, pl.ds(7 + j0, 8), :]
                refracted = own - (flux - prev)
                total = total + (jnp.where(sub >= 4, refracted, 0.0) if b == 4 else refracted)
                growth = jnp.maximum(proj[c, pl.ds(j0, 8), :] * gain - floor, 0.0)
                out[out_first + i * GROUP + kk, pl.ds(c + 4 * j0, 8, stride=4), :] = refracted * jnp.exp2(growth)
            out_sums.append(total)
        return tuple(out_sums)

    def body(i, sums):
        for kk in range(GROUP):
            sums = one(i, kk, sums)
        return sums

    zero = jnp.zeros((8, LANES), F32)
    return lax.fori_loop(0, count // GROUP, body, (zero,) * CELLS)


def main_body(
    first, count, scal, weights, x, west, east, ghosts, sea8, turn, proj, out, energy, zs, gs
):
    sums = chunk_pass(first, count, scal, weights, x, west, east, ghosts, sea8, turn, proj, zs, gs, out, 0)
    for c in range(CELLS):
        energy[c] = sums[c]


def pass_scratch():
    return [pltpu.VMEM((GROUP, CELLS, 56, LANES), F32), pltpu.VMEM((GROUP, CELLS, 56, LANES), F32)]


def main_chunk(first, count, weights, x, west, east, ghosts, tables):
    return pl.pallas_call(
        lambda *refs: main_body(first, count, *refs),
        out_shape=(
            pltpu.VMEM((count, ROWS, LANES), F32),
            pltpu.VMEM((CELLS, 8, LANES), F32),
        ),
        in_specs=[vmem_spec()] * 9,
        out_specs=(vmem_spec(), vmem_spec()),
        scratch_shapes=pass_scratch(),
        compiler_params=pltpu.CompilerParams(vmem_limit_bytes=VMEM),
        cost_estimate=pl.CostEstimate(flops=0, bytes_accessed=1000000, transcendentals=0),
        name="chunk",
    )(SCALARS, weights, x, west, east, ghosts, *tables)


def tail_body(sizes, scal, weights, x, west, east, ghosts, sea8, turn, proj, *rest):
    done = len(sizes) - 1
    parts, energies = rest[:done], rest[done : 2 * done]
    out_hbm, obuf, zs, gs, out_sem = rest[2 * done :]
    count = sizes[-1]
    first = FREQS - count
    sums = chunk_pass(
        first, count, scal, weights, x, west, east, ghosts, sea8, turn, proj, zs, gs, obuf, first
    )
    sub = lax.broadcasted_iota(jnp.int32, (8, LANES), 0)
    pattern = mask = jnp.zeros((8, LANES), F32)
    for c in range(CELLS):
        total = sums[c]
        for energy in energies:
            total = total + energy[c]
        mean = sea8[c] * (jnp.sum(total, axis=0, keepdims=True) * (1.0 / (FREQS * DIRS)))
        level = mean * (1.0 / energy_ref)
        pattern = jnp.where(sub % CELLS == c, level * level, pattern)
        mask = jnp.where(sub % CELLS == c, sea8[c], mask)
    stores, at = [], 0
    for n, size in enumerate(sizes):
        for low in range(0, size, PIECE):
            high = min(low + PIECE, size)

            def body(i, _, at=at, n=n):
                scale = jnp.exp2(-(scal[4, pl.ds(at + i, 1), :] * pattern)) * mask
                source, k = (parts[n], i) if n < done else (obuf, at + i)
                for r in range(0, ROWS, 8):
                    obuf[at + i, pl.ds(r, 8), :] = source[k, pl.ds(r, 8), :] * scale
                return 0

            lax.fori_loop(low, high, body, 0)
            span = pl.ds(at + low, high - low)
            stores.append(
                pltpu.make_async_copy(obuf.at[span], out_hbm.at[span], out_sem.at[len(stores)])
            )
            stores[-1].start()
        at += size
    for store in stores:
        store.wait()


def tail_chunk(sizes, weights, x, west, east, ghosts, tables, parts, energies):
    done = len(sizes) - 1
    return pl.pallas_call(
        lambda *refs: tail_body(sizes, *refs),
        out_shape=jax.ShapeDtypeStruct((FREQS, ROWS, LANES), F32),
        in_specs=[vmem_spec()] * (9 + 2 * done),
        out_specs=any_spec(),
        scratch_shapes=[
            pltpu.VMEM((FREQS, ROWS, LANES), F32),
            *pass_scratch(),
            pltpu.SemaphoreType.DMA((FREQS // PIECE,)),
        ],
        compiler_params=pltpu.CompilerParams(vmem_limit_bytes=VMEM),
        cost_estimate=pl.CostEstimate(flops=0, bytes_accessed=6000000, transcendentals=0),
        name="last_chunk",
    )(SCALARS, weights, x, west, east, ghosts, *tables, *parts, *energies)


def line(axis):
    up = [(i, i + 1) for i in range(lax.axis_size(axis) - 1)]
    return up, [(j, i) for i, j in up]


def local(
    spectrum, sea_mask, refraction, atm_wind, hour_fraction, send_cells, recv_slots, recv_weights
):
    north_way, south_way = line("lat")
    x = spectrum.reshape(FREQS, ROWS, LANES)
    tiles = lax.axis_size("lon")
    swap_one = [(i, i ^ 1) for i in range(tiles)]
    swap_two = [(i, (i + 1 if i % 2 else i - 1) % tiles) for i in range(tiles)]
    cap = send_cells.shape[1] // tiles
    firsts = [sum(CHUNKS[:n]) for n in range(len(CHUNKS))]

    def exchange(one, two):
        return lax.ppermute(one, "lon", swap_one), lax.ppermute(two, "lon", swap_two)

    *sends, packed = first_halos(
        x, CHUNKS[0], atm_wind.reshape(4, LANES), send_cells
    )
    halos = [exchange(*sends)]
    q = pack_edges(x, sea_mask, packed)
    weights = stencil_weights(packed)
    south = lax.ppermute(q, "lat", north_way)
    north = lax.ppermute(q, "lat", south_way)
    *sends, merged = second_halos(x, firsts[1], CHUNKS[1], south, north)
    halos.append(exchange(*sends))
    halos.append(exchange(*later_halos(x, firsts[2], CHUNKS[2], *halos[0], weights)))

    lists = [jnp.concatenate([packed, halos[0][0][-8:]])]
    step = 2
    while step < tiles:
        held = lists[0] if len(lists) == 1 else jnp.concatenate(lists)
        lists.append(lax.ppermute(held, "lon", [(i, i ^ step) for i in range(tiles)]))
        step *= 2
    ghosts, token = move_ghosts(CHUNKS[1], merged, *halos[1])
    surface_wind, *tables = surface(
        cap,
        tiles,
        token,
        hour_fraction.reshape(1, 1),
        lists,
        recv_slots.reshape(4 * CELLS, LANES),
        recv_weights.reshape(4 * CELLS, LANES),
        sea_mask,
        refraction,
    )
    halos.append(exchange(*later_halos(x, firsts[3], CHUNKS[3], *halos[1], tables[0])))

    parts, energies = [], []
    for n, (first, count) in enumerate(zip(firsts, CHUNKS)):
        west, east = halos[n]
        if n < len(CHUNKS) - 1:
            part, energy = main_chunk(first, count, weights, x, west, east, ghosts, tables)
            parts.append(part)
            energies.append(energy)
        else:
            out = tail_chunk(CHUNKS, weights, x, west, east, ghosts, tables, parts, energies)
    return (out.reshape(spectrum.shape), surface_wind)


def solution(mesh):
    in_specs = (
        P(None, None, "lon", "lat"),
        P("lon", "lat"),
        P(None, "lon", "lat"),
        P(None, None, ("lon", "lat")),
        P(),
        P(("lon", "lat"), None),
        P(None, "lon", "lat"),
        P(None, "lon", "lat"),
    )
    out_specs = (P(None, None, "lon", "lat"), P(None, "lon", "lat"))
    return jax.shard_map(local, mesh=mesh, in_specs=in_specs, out_specs=out_specs, check_vma=False)
```

```python
import math

import jax
import jax.numpy as jnp
import numpy as np
from jax import lax
from jax.experimental import pallas as pl
from jax.experimental.pallas import tpu as pltpu
from jax.sharding import PartitionSpec as P

base_freq = 0.035
freq_step = 1.1
courant_max = 0.9
gravity = 9.81
input_rate = 0.05
damping_rate = 0.8
energy_ref = 0.5

F32 = jnp.float32
FREQS = 36
DIRS = 36
CELLS = 4
LANES = 128
ROWS = DIRS * CELLS
BLOCKS = (0, 8, 16, 24, 28)
GROUP = 4
HALO = DIRS + DIRS // 2
NEAR_SPLIT = 16
FAR = DIRS // 2
PACK = 8
SPAN = LANES // PACK
OFFSETS, WIDTHS, EDGES = (0, 3, 6, 10, 13), (3, 3, 4, 3, 3), (0, 0, 0, 1, 1)
CHUNKS = (12, 8, 12, 4)
GROUPS = -(-FREQS // PACK)
PIECE = 4
EDGE_ROWS = 2 * (-(-FREQS // PACK)) * 8
VMEM = 32 * 1024 * 1024
FIRST_VMEM = 63000000

freqs = base_freq * freq_step ** np.arange(FREQS, dtype=np.float64)
spacing = 2.0 * math.pi / DIRS
theta = (np.arange(DIRS) + 0.5) * spacing
phi = (np.arange(DIRS) + 1.0) * spacing
ratio = base_freq / freqs
log2_e = 1.0 / math.log(2.0)
rate = input_rate * freqs / freqs[-1] * log2_e
SCALARS = np.stack(
    [
        courant_max * ratio,
        np.sqrt(ratio),
        rate * 2.0 * math.pi * freqs / gravity,
        rate,
        damping_rate * freqs / freqs[-1] * log2_e,
    ]
).astype(np.float32)
SCALARS = np.ascontiguousarray(np.broadcast_to(SCALARS[:, :, None], (5, FREQS, LANES)))
ANGLES = np.broadcast_to(
    np.stack(
        [np.abs(np.cos(theta)), np.abs(np.sin(theta)), np.cos(theta), np.sin(theta), np.sin(phi), np.cos(phi)]
    )[:, :, None],
    (6, DIRS, LANES),
).astype(np.float32)


def stencil(a):
    one_m = 1.0 - a * a
    beyond = a * one_m * (-1.0 / 6.0)
    half = a * (0.5 - 0.5 * a)
    down = half + beyond
    up = a - half - 2.0 * beyond
    return beyond, up - beyond, 1.0 + down - up, -down


def packed_weights():
    out = np.zeros((5, GROUPS, 8, LANES), np.float64)
    for k in range(FREQS):
        for b, j0 in enumerate(BLOCKS):
            c = courant_max * ratio[k] * np.cos(theta[j0 : j0 + 8])
            far, up, own, down = stencil(np.abs(c))
            zero = np.zeros(8)
            pos = c > 0
            five = [
                np.where(pos, far, zero),
                np.where(pos, up, down),
                own,
                np.where(pos, down, up),
                np.where(pos, zero, far),
            ]
            lane = (k % PACK) * SPAN + OFFSETS[b]
            for d in range(5):
                out[d, k // PACK, :, lane : lane + WIDTHS[b]] = five[d][:, None]
    return out.astype(np.float32)


PACKED = packed_weights()


def any_spec():
    return pl.BlockSpec(memory_space=pl.ANY)


def vmem_spec():
    return pl.BlockSpec(memory_space=pltpu.VMEM)


def smem_spec():
    return pl.BlockSpec(memory_space=pltpu.SMEM)


def is_even():
    return jnp.full((8, LANES), lax.axis_index("lon") % 2) == 0


def halo_rows(x, start, one, two, low, high):
    even = is_even()

    def body(i, _):
        for kk in range(GROUP):
            k = start + i * GROUP + kk
            near = ((0, 0, 0, 8), (8, 8, 8, 8), (34, 16, 16, 8), (42, 24, 24, 8), (50, 32, 32, 4))
            far = ((16, 0, 9, 8), (24, 8, 17, 1), (25, 27, 18, 8), (33, 35, 26, 1))
            for cell_e, cell_w, runs in ((3, 0, near), (2, 1, far)):
                for row, j_e, j_w, n in runs:
                    east = x[k, pl.ds(cell_e + 4 * j_e, n, stride=4), :]
                    west = x[k, pl.ds(cell_w + 4 * j_w, n, stride=4), :]
                    one[halo_at(i, kk, row, n), :] = jnp.where(even[:n], east, west)
                    two[halo_at(i, kk, row, n), :] = jnp.where(even[:n], west, east)
        return 0

    lax.fori_loop(low // GROUP, high // GROUP, body, 0)


def halo_at(i, kk, row, n):
    return pl.ds(pl.multiple_of(i * (GROUP * HALO), 8) + HALO * kk + row, n)


def lane_ids():
    return lax.broadcasted_iota(jnp.int32, (8, LANES), 1)


def first_body(count, x_hbm, wind_hbm, cells_hbm, one, two, packed, x, wind, cells, sem, small):
    few = [
        pltpu.make_async_copy(wind_hbm, wind, small.at[0]),
        pltpu.make_async_copy(cells_hbm, cells, small.at[1]),
    ]
    for copy in few:
        copy.start()
    copies = []
    for n in range(count // GROUP):
        span = pl.ds(n * GROUP, GROUP)
        copies.append(pltpu.make_async_copy(x_hbm.at[span], x.at[span], sem.at[n]))
        copies[-1].start()
    for copy in few:
        copy.wait()
    width = cells.shape[1]
    index = jnp.concatenate([cells[:, :LANES], cells[:, width - LANES :]] * 4, axis=0)
    table = jnp.concatenate([wind[pl.ds(n // 2, 1), :] for n in range(8)], axis=0)
    listed = jnp.take_along_axis(table, index, axis=1)
    packed[...] = listed
    one[pl.ds(count * HALO, 8), :] = listed
    for n in range(count // GROUP):
        copies[n].wait()
        halo_rows(x, 0, one, two, n * GROUP, (n + 1) * GROUP)


def message(count, extra=0):
    return pltpu.VMEM((count * HALO + extra, LANES), F32)


def first_halos(x, count, wind, cells):
    return pl.pallas_call(
        lambda *refs: first_body(count, *refs),
        out_shape=(message(count, 8), message(count), pltpu.VMEM((8, LANES), F32)),
        in_specs=[any_spec()] * 3,
        out_specs=(vmem_spec(),) * 3,
        scratch_shapes=[
            pltpu.VMEM((count, *x.shape[1:]), F32),
            pltpu.VMEM(wind.shape, F32),
            pltpu.VMEM(cells.shape, cells.dtype),
            pltpu.SemaphoreType.DMA((count // GROUP,)),
            pltpu.SemaphoreType.DMA((2,)),
        ],
        compiler_params=pltpu.CompilerParams(vmem_limit_bytes=FIRST_VMEM),
        cost_estimate=pl.CostEstimate(flops=0, bytes_accessed=2000000, transcendentals=0),
        name="first_halos",
    )(x, wind, cells)


def edge_ids():
    place = lane_ids() % SPAN
    edge = place
    for offset, first in zip(OFFSETS[1:], EDGES[1:]):
        edge = jnp.where(place >= offset, place - (offset - first), edge)
    return edge


def edge_shift(r, b):
    return (r * SPAN + OFFSETS[b] + 2 - EDGES[b]) % LANES


def edge_body(x, sea, after, q):
    lane = lane_ids()
    edge = edge_ids()

    def pack(g, count):
        for cell in range(CELLS):
            acc = jnp.zeros((8, LANES), F32)
            for r in range(count):
                for b, j0 in enumerate(BLOCKS):
                    rows = x[g * PACK + r, pl.ds(cell + 4 * j0, 8, stride=4), :]
                    rows = pltpu.roll(rows, edge_shift(r, b), 1)
                    acc = jnp.where(lane >= r * SPAN + OFFSETS[b], rows, acc)
            q[cell, g] = acc

    def body(g, _):
        pack(g, PACK)
        return 0

    lax.fori_loop(0, FREQS // PACK, body, 0)
    pack(GROUPS - 1, FREQS - (GROUPS - 1) * PACK)
    for cell in range(CELLS):
        mask = jnp.zeros((8, LANES), F32)
        for n, at in enumerate((LANES - 2, LANES - 1, 0, 1)):
            mask = jnp.where(edge == n, sea[pl.ds(cell, 1), pl.ds(at, 1)].astype(F32), mask)
        q[cell, GROUPS] = mask


def pack_edges(x, sea, after):
    return pl.pallas_call(
        edge_body,
        out_shape=pltpu.VMEM((CELLS, GROUPS + 1, 8, LANES), F32),
        in_specs=[vmem_spec()] * 3,
        out_specs=vmem_spec(),
        compiler_params=pltpu.CompilerParams(vmem_limit_bytes=VMEM),
        cost_estimate=pl.CostEstimate(flops=0, bytes_accessed=4000000, transcendentals=0),
        name="pack_edges",
    )(x, sea, after)


def second_body(start, count, x, south, north, one, two, merged):
    pick = edge_ids() < 2
    even = is_even()

    def body(g, _):
        both = [jnp.where(pick, south[c, g], north[c, g]) for c in range(CELLS)]
        for c in range(CELLS):
            merged[c, g] = both[c]
        for n in range(2):
            row = pl.ds(pl.multiple_of(count * HALO + (n * GROUPS + g) * 8, 8), 8)
            one[row, :] = jnp.where(even, both[2 + n], both[n])
            two[row, :] = jnp.where(even, both[n], both[2 + n])
        return 0

    lax.fori_loop(0, GROUPS, body, 0)
    for c in range(CELLS):
        merged[c, GROUPS] = jnp.where(pick, south[c, GROUPS], north[c, GROUPS])
    halo_rows(x, start, one, two, 0, count)


def second_halos(x, start, count, south, north):
    return pl.pallas_call(
        lambda *refs: second_body(start, count, *refs),
        out_shape=(
            message(count, EDGE_ROWS),
            message(count, EDGE_ROWS),
            pltpu.VMEM((CELLS, GROUPS + 1, 8, LANES), F32),
        ),
        in_specs=[vmem_spec()] * 3,
        out_specs=(vmem_spec(),) * 3,
        compiler_params=pltpu.CompilerParams(vmem_limit_bytes=VMEM),
        cost_estimate=pl.CostEstimate(flops=0, bytes_accessed=2000000, transcendentals=0),
        name="second_halos",
    )(x, south, north)


def later_halos(x, start, count, *after):
    return pl.pallas_call(
        lambda x, *refs: halo_rows(x, start, *refs[-2:], 0, count),
        out_shape=(message(count), message(count)),
        in_specs=[vmem_spec()] * (1 + len(after)),
        out_specs=(vmem_spec(),) * 2,
        compiler_params=pltpu.CompilerParams(vmem_limit_bytes=VMEM),
        cost_estimate=pl.CostEstimate(flops=0, bytes_accessed=1000000, transcendentals=0),
        name="later_halos",
    )(x, *after)


def ghost_body(count, merged, one, two, weights, ghosts, token):
    even = is_even()
    token[...] = jnp.zeros_like(token)

    def spread(g, freqs):
        rows = [
            pl.ds(pl.multiple_of(count * HALO + (n * GROUPS + g) * 8, 8), 8) for n in range(2)
        ]
        west = [jnp.where(even, two[row, :], one[row, :]) for row in rows]
        east = [jnp.where(even, one[row, :], two[row, :]) for row in rows]
        ext = west + [merged[c, g] for c in range(CELLS)] + east
        for c in range(CELLS):
            total = weights[0, g] * ext[c]
            for d in range(1, 5):
                total = total + weights[d, g] * ext[c + d]
            total = total * merged[c, GROUPS]
            for r in range(freqs):
                for b in range(len(BLOCKS)):
                    ghosts[g * PACK + r, c, b] = pltpu.roll(total, (LANES - edge_shift(r, b)) % LANES, 1)

    def body(g, _):
        spread(g, PACK)
        return 0

    lax.fori_loop(0, FREQS // PACK, body, 0)
    spread(GROUPS - 1, FREQS - (GROUPS - 1) * PACK)


def move_ghosts(count, merged, one, two):
    return pl.pallas_call(
        lambda *refs: ghost_body(count, *refs),
        out_shape=(
            pltpu.VMEM((FREQS, CELLS, len(BLOCKS), 8, LANES), F32),
            pltpu.VMEM((8, LANES), F32),
        ),
        in_specs=[vmem_spec()] * 4,
        out_specs=(vmem_spec(),) * 2,
        compiler_params=pltpu.CompilerParams(vmem_limit_bytes=VMEM),
        cost_estimate=pl.CostEstimate(flops=0, bytes_accessed=2000000, transcendentals=0),
        name="move_ghosts",
    )(merged, one, two, PACKED)


def wind_body(cap, sources, after, hour, slots, weights, ang, sea, refr, *rest):
    pieces, (wind, sea8, turn, proj, table) = rest[:-5], rest[-5:]
    at = 0
    for piece in pieces:
        table[pl.ds(at, piece.shape[0]), :] = piece[...]
        at += piece.shape[0]
    late = hour[...]
    width = cap * sources
    me = lax.axis_index("lon")
    mine = cap * me
    high = mine + cap > LANES
    begin = jnp.where(high, mine - (width - LANES), mine)
    lane = lane_ids()
    rows = [jnp.zeros((8, LANES), F32)] * 2
    for s in range(sources):
        block = table[pl.ds(pl.multiple_of(8 * (s ^ me), 8), 8), :]
        for n, to in enumerate((cap * s, cap * s - (width - LANES))):
            if to < LANES and to + cap > 0:
                moved = pltpu.roll(block, (to + 2 * LANES - begin) % LANES, 1)
                rows[n] = jnp.where((lane >= to) & (lane < to + cap), moved, rows[n])

    def entries(n, c):
        now = [jnp.where(high, rows[n][r + 1 : r + 2], rows[n][r : r + 1]) for r in (2 * c, 2 * c + 4)]
        return jnp.broadcast_to((1.0 - late) * now[0] + late * now[1], (8, LANES))

    lists = [[entries(n, c) for n in range(2)] for c in range(2)]
    picked = [[None, None], [None, None]]
    for half in range(2):
        index = slots[pl.ds(8 * half, 8), :]
        low = index < LANES
        place = jnp.where(low, index, index - (width - LANES))
        for c in range(2):
            value = [jnp.take_along_axis(row, place, axis=1) for row in lists[c]]
            picked[half][c] = jnp.where(low, value[0], value[1])
    for c in range(2):
        total = weights[pl.ds(0, 8), :] * picked[0][c]
        total = total + weights[pl.ds(8, 8), :] * picked[1][c]
        wind[c] = total[:CELLS] + total[CELLS:]
    for cell in range(CELLS):
        row = pl.ds(cell, 1)
        sea8[cell] = jnp.broadcast_to(sea[row, :], (8, LANES)).astype(F32)
        for j0 in BLOCKS:
            j = pl.ds(j0, 8)
            turn[cell, j, :] = refr[0, row, :] * ang[4, j, :] - refr[1, row, :] * ang[5, j, :]
            proj[cell, j, :] = wind[0, row, :] * ang[2, j, :] + wind[1, row, :] * ang[3, j, :]


def surface(cap, sources, after, hour, pieces, slots, weights, sea, refr):
    return pl.pallas_call(
        lambda *refs: wind_body(cap, sources, *refs),
        out_shape=(
            pltpu.VMEM((2, CELLS, LANES), F32),
            pltpu.VMEM((CELLS, 8, LANES), F32),
            pltpu.VMEM((CELLS, DIRS, LANES), F32),
            pltpu.VMEM((CELLS, DIRS, LANES), F32),
        ),
        in_specs=[vmem_spec()] * (7 + len(pieces)),
        out_specs=(vmem_spec(),) * 4,
        scratch_shapes=[pltpu.VMEM((8 * sources, LANES), F32)],
        compiler_params=pltpu.CompilerParams(vmem_limit_bytes=VMEM),
        cost_estimate=pl.CostEstimate(flops=0, bytes_accessed=2000000, transcendentals=0),
        name="surface_wind",
    )(after, hour, slots, weights, ANGLES, sea, refr, *pieces)


def weight_body(scal, ang, after, table):
    def body(k, _):
        cour = scal[0, pl.ds(k, 1), :]
        for b, j0 in enumerate(BLOCKS):
            both = stencil(cour * ang[0, pl.ds(j0, 8), :]) + stencil(cour * ang[1, pl.ds(j0, 8), :])
            for n, weight in enumerate(both):
                table[k, b, n] = weight
        return 0

    lax.fori_loop(0, FREQS, body, 0)


def stencil_weights(after):
    return pl.pallas_call(
        weight_body,
        out_shape=pltpu.VMEM((FREQS, len(BLOCKS), 8, 8, LANES), F32),
        in_specs=[vmem_spec()] * 3,
        out_specs=vmem_spec(),
        compiler_params=pltpu.CompilerParams(vmem_limit_bytes=VMEM),
        cost_estimate=pl.CostEstimate(flops=0, bytes_accessed=2000000, transcendentals=0),
        name="stencil_weights",
    )(SCALARS, ANGLES, after)


def chunk_steps(
    first, scal, weights, x, one_ref, two_ref, ghosts, sea8, turn, proj, zs, gs, out, out_first
):
    lane = lane_ids()
    sub = lax.broadcasted_iota(jnp.int32, (8, LANES), 0)
    near_rows = (0, 8, 34, 42, 46)
    even = is_even()

    def from_west(rows):
        return jnp.where(even, two_ref[rows, :], one_ref[rows, :])

    def from_east(rows):
        return jnp.where(even, one_ref[rows, :], two_ref[rows, :])

    def advect(i, kk, sums):
        k = first + i * GROUP + kk
        sums = list(sums)
        for b, j0 in enumerate(BLOCKS):
            w0, w1, w2, w3, v0, v1, v2, v3 = (weights[k, b, n] for n in range(8))
            cells = [x[k, pl.ds(c + 4 * j0, 8, stride=4), :] for c in range(CELLS)]
            west = from_west(halo_at(i, kk, near_rows[b], 8))
            east = from_east(halo_at(i, kk, near_rows[b], 8))
            plus = [west, *cells, east]
            minus = plus[::-1]
            if b == 0:
                far, seq = from_west(halo_at(i, kk, 16, 8)), plus
            elif b == 2:
                far, seq = from_east(halo_at(i, kk, 23, 8)), minus
            elif b == 4:
                far, seq = from_west(halo_at(i, kk, 26, 8)), plus
            else:
                if b == 1:
                    pos = sub < 1
                    far_p, far_m = from_west(halo_at(i, kk, 24, 8)), from_east(halo_at(i, kk, 15, 8))
                else:
                    pos = sub >= 3
                    far_p, far_m = from_west(halo_at(i, kk, 22, 8)), from_east(halo_at(i, kk, 31, 8))
                far = jnp.where(pos, far_p, far_m)
                seq = [jnp.where(pos, p, m) for p, m in zip(plus, minus)]
            seq = [far, *seq]
            moved = [
                w0 * seq[c] + w1 * seq[c + 1] + w2 * seq[c + 2] + w3 * seq[c + 3] for c in range(CELLS)
            ]
            if b == 2:
                moved = moved[::-1]
            elif b in (1, 3):
                moved = [jnp.where(pos, p, m) for p, m in zip(moved, moved[::-1])]
            for c in range(CELLS):
                z = moved[c] * sea8[c]
                ghost = ghosts[k, c, b]
                s1 = pltpu.roll(jnp.where(lane == LANES - 1, ghost, z), 1, 1)
                n1 = pltpu.roll(jnp.where(lane == 0, ghost, z), LANES - 1, 1)
                if b <= 2:
                    s2 = pltpu.roll(jnp.where(lane >= LANES - 2, ghost, z), 2, 1)
                if b >= 2:
                    n2 = pltpu.roll(jnp.where(lane < 2, ghost, z), LANES - 2, 1)
                if b < 2:
                    up, down, far = s1, n1, s2
                elif b > 2:
                    up, down, far = n1, s1, n2
                else:
                    p = sub < 2
                    up, down = jnp.where(p, s1, n1), jnp.where(p, n1, s1)
                    far = jnp.where(p, s2, n2)
                z = v0 * far + v1 * up + v2 * z + v3 * down
                zs[kk, c, pl.ds(8 + j0, 8), :] = z
                sums[c] = sums[c] + (jnp.where(sub >= 4, z, 0.0) if b == 4 else z)
        return tuple(sums)

    def bend_grow(i, kk):
        k = first + i * GROUP + kk
        bend, gain, floor = (scal[n, pl.ds(k, 1), :] for n in range(1, 4))
        for c in range(CELLS):
            zs[kk, c, pl.ds(8 + DIRS, 1), :] = zs[kk, c, pl.ds(8, 1), :]
            for b, j0 in enumerate(BLOCKS):
                own = zs[kk, c, pl.ds(8 + j0, 8), :]
                nxt = zs[kk, c, pl.ds(9 + j0, 8), :]
                s = bend * turn[c, pl.ds(j0, 8), :]
                gs[kk, c, pl.ds(8 + j0, 8), :] = s * jnp.where(s > 0, own, nxt)
            gs[kk, c, pl.ds(7, 1), :] = gs[kk, c, pl.ds(7 + DIRS, 1), :]
            for b, j0 in enumerate(BLOCKS):
                own = zs[kk, c, pl.ds(8 + j0, 8), :]
                flux = gs[kk, c, pl.ds(8 + j0, 8), :]
                prev = gs[kk, c, pl.ds(7 + j0, 8), :]
                refracted = own - (flux - prev)
                growth = jnp.maximum(proj[c, pl.ds(j0, 8), :] * gain - floor, 0.0)
                out[out_first + i * GROUP + kk, pl.ds(c + 4 * j0, 8, stride=4), :] = refracted * jnp.exp2(growth)

    return advect, bend_grow


def no_sums():
    return (jnp.zeros((8, LANES), F32),) * CELLS


def main_body(
    first, count, scal, weights, x, west, east, ghosts, sea8, turn, proj, out, energy, zs, gs
):
    advect, bend_grow = chunk_steps(
        first, scal, weights, x, west, east, ghosts, sea8, turn, proj, zs, gs, out, 0
    )

    def body(i, sums):
        for kk in range(GROUP):
            sums = advect(i, kk, sums)
            bend_grow(i, kk)
        return sums

    for c, total in enumerate(lax.fori_loop(0, count // GROUP, body, no_sums())):
        energy[c] = total


def pass_scratch():
    return [pltpu.VMEM((GROUP, CELLS, 56, LANES), F32), pltpu.VMEM((GROUP, CELLS, 56, LANES), F32)]


def main_chunk(first, count, weights, x, west, east, ghosts, tables):
    return pl.pallas_call(
        lambda *refs: main_body(first, count, *refs),
        out_shape=(
            pltpu.VMEM((count, ROWS, LANES), F32),
            pltpu.VMEM((CELLS, 8, LANES), F32),
        ),
        in_specs=[vmem_spec()] * 9,
        out_specs=(vmem_spec(), vmem_spec()),
        scratch_shapes=pass_scratch(),
        compiler_params=pltpu.CompilerParams(vmem_limit_bytes=VMEM),
        cost_estimate=pl.CostEstimate(flops=0, bytes_accessed=1000000, transcendentals=0),
        name="chunk",
    )(SCALARS, weights, x, west, east, ghosts, *tables)


def tail_body(sizes, scal, weights, x, west, east, ghosts, wind, sea8, turn, proj, *rest):
    done = len(sizes) - 1
    parts, energies = rest[:done], rest[done : 2 * done]
    out_hbm, wind_hbm, obuf, zs, gs, out_sem, wind_sem = rest[2 * done :]
    stores, at = [pltpu.make_async_copy(wind, wind_hbm, wind_sem)], 0
    stores[0].start()
    count = sizes[-1]
    first = FREQS - count
    advect, bend_grow = chunk_steps(
        first, scal, weights, x, west, east, ghosts, sea8, turn, proj, zs, gs, obuf, first
    )
    assert count == GROUP
    sums = no_sums()
    for kk in range(GROUP):
        sums = advect(0, kk, sums)
    sub = lax.broadcasted_iota(jnp.int32, (8, LANES), 0)
    pattern = mask = jnp.zeros((8, LANES), F32)
    for c in range(CELLS):
        total = sums[c]
        for energy in energies:
            total = total + energy[c]
        mean = sea8[c] * (jnp.sum(total, axis=0, keepdims=True) * (1.0 / (FREQS * DIRS)))
        level = mean * (1.0 / energy_ref)
        pattern = jnp.where(sub % CELLS == c, level * level, pattern)
        mask = jnp.where(sub % CELLS == c, sea8[c], mask)
    for n, size in enumerate(sizes):
        if n == done:
            for kk in range(GROUP):
                bend_grow(0, kk)
        for low in range(0, size, PIECE):
            high = min(low + PIECE, size)

            def body(i, _, at=at, n=n):
                scale = jnp.exp2(-(scal[4, pl.ds(at + i, 1), :] * pattern)) * mask
                source, k = (parts[n], i) if n < done else (obuf, at + i)
                for r in range(0, ROWS, 8):
                    obuf[at + i, pl.ds(r, 8), :] = source[k, pl.ds(r, 8), :] * scale
                return 0

            lax.fori_loop(low, high, body, 0)
            span = pl.ds(at + low, high - low)
            stores.append(
                pltpu.make_async_copy(obuf.at[span], out_hbm.at[span], out_sem.at[len(stores) - 1])
            )
            stores[-1].start()
        at += size
    for store in stores:
        store.wait()


def tail_chunk(sizes, weights, x, west, east, ghosts, wind, tables, parts, energies):
    done = len(sizes) - 1
    return pl.pallas_call(
        lambda *refs: tail_body(sizes, *refs),
        out_shape=(
            jax.ShapeDtypeStruct((FREQS, ROWS, LANES), F32),
            jax.ShapeDtypeStruct((2, CELLS, LANES), F32),
        ),
        in_specs=[vmem_spec()] * (10 + 2 * done),
        out_specs=(any_spec(), any_spec()),
        scratch_shapes=[
            pltpu.VMEM((FREQS, ROWS, LANES), F32),
            *pass_scratch(),
            pltpu.SemaphoreType.DMA((FREQS // PIECE,)),
            pltpu.SemaphoreType.DMA,
        ],
        compiler_params=pltpu.CompilerParams(vmem_limit_bytes=VMEM),
        cost_estimate=pl.CostEstimate(flops=0, bytes_accessed=6000000, transcendentals=0),
        name="last_chunk",
    )(SCALARS, weights, x, west, east, ghosts, wind, *tables, *parts, *energies)


def line(axis):
    up = [(i, i + 1) for i in range(lax.axis_size(axis) - 1)]
    return up, [(j, i) for i, j in up]


def local(
    spectrum, sea_mask, refraction, atm_wind, hour_fraction, send_cells, recv_slots, recv_weights
):
    north_way, south_way = line("lat")
    x = spectrum.reshape(FREQS, ROWS, LANES)
    tiles = lax.axis_size("lon")
    swap_one = [(i, i ^ 1) for i in range(tiles)]
    swap_two = [(i, (i + 1 if i % 2 else i - 1) % tiles) for i in range(tiles)]
    cap = send_cells.shape[1] // tiles
    firsts = [sum(CHUNKS[:n]) for n in range(len(CHUNKS))]

    def exchange(one, two):
        return lax.ppermute(one, "lon", swap_one), lax.ppermute(two, "lon", swap_two)

    *sends, packed = first_halos(
        x, CHUNKS[0], atm_wind.reshape(4, LANES), send_cells
    )
    halos = [exchange(*sends)]
    q = pack_edges(x, sea_mask, packed)
    weights = stencil_weights(packed)
    south = lax.ppermute(q, "lat", north_way)
    north = lax.ppermute(q, "lat", south_way)
    *sends, merged = second_halos(x, firsts[1], CHUNKS[1], south, north)
    halos.append(exchange(*sends))
    halos.append(exchange(*later_halos(x, firsts[2], CHUNKS[2], *halos[0], weights)))

    lists = [jnp.concatenate([packed, halos[0][0][-8:]])]
    step = 2
    while step < tiles:
        held = lists[0] if len(lists) == 1 else jnp.concatenate(lists)
        lists.append(lax.ppermute(held, "lon", [(i, i ^ step) for i in range(tiles)]))
        step *= 2
    ghosts, token = move_ghosts(CHUNKS[1], merged, *halos[1])
    surface_wind, *tables = surface(
        cap,
        tiles,
        token,
        hour_fraction.reshape(1, 1),
        lists,
        recv_slots.reshape(4 * CELLS, LANES),
        recv_weights.reshape(4 * CELLS, LANES),
        sea_mask,
        refraction,
    )
    halos.append(exchange(*later_halos(x, firsts[3], CHUNKS[3], *halos[1], tables[0])))

    parts, energies = [], []
    for n, (first, count) in enumerate(zip(firsts, CHUNKS)):
        west, east = halos[n]
        if n < len(CHUNKS) - 1:
            part, energy = main_chunk(first, count, weights, x, west, east, ghosts, tables)
            parts.append(part)
            energies.append(energy)
        else:
            out, surface_wind = tail_chunk(
                CHUNKS, weights, x, west, east, ghosts, surface_wind, tables, parts, energies
            )
    return (out.reshape(spectrum.shape), surface_wind)


def solution(mesh):
    in_specs = (
        P(None, None, "lon", "lat"),
        P("lon", "lat"),
        P(None, "lon", "lat"),
        P(None, None, ("lon", "lat")),
        P(),
        P(("lon", "lat"), None),
        P(None, "lon", "lat"),
        P(None, "lon", "lat"),
    )
    out_specs = (P(None, None, "lon", "lat"), P(None, "lon", "lat"))
    return jax.shard_map(local, mesh=mesh, in_specs=in_specs, out_specs=out_specs, check_vma=False)
```

```python
import math

import jax
import jax.numpy as jnp
import numpy as np
from jax import lax
from jax.experimental import pallas as pl
from jax.experimental.pallas import tpu as pltpu
from jax.sharding import PartitionSpec as P

base_freq = 0.035
freq_step = 1.1
courant_max = 0.9
gravity = 9.81
input_rate = 0.05
damping_rate = 0.8
energy_ref = 0.5

F32 = jnp.float32
FREQS = 36
DIRS = 36
CELLS = 4
LANES = 128
ROWS = DIRS * CELLS
BLOCKS = (0, 8, 16, 24, 28)
GROUP = 4
HALO = DIRS + DIRS // 2
NEAR_SPLIT = 16
FAR = DIRS // 2
PACK = 8
SPAN = LANES // PACK
OFFSETS, WIDTHS, EDGES = (0, 3, 6, 10, 13), (3, 3, 4, 3, 3), (0, 0, 0, 1, 1)
CHUNKS = (12, 8, 12, 4)
GROUPS = -(-FREQS // PACK)
PIECE = 4
EDGE_ROWS = (2 * (-(-FREQS // PACK)) - 1) * 8
VMEM = 32 * 1024 * 1024
FIRST_VMEM = 63000000

freqs = base_freq * freq_step ** np.arange(FREQS, dtype=np.float64)
spacing = 2.0 * math.pi / DIRS
theta = (np.arange(DIRS) + 0.5) * spacing
phi = (np.arange(DIRS) + 1.0) * spacing
ratio = base_freq / freqs
log2_e = 1.0 / math.log(2.0)
rate = input_rate * freqs / freqs[-1] * log2_e
SCALARS = np.stack(
    [
        courant_max * ratio,
        np.sqrt(ratio),
        rate * 2.0 * math.pi * freqs / gravity,
        rate,
        damping_rate * freqs / freqs[-1] * log2_e,
    ]
).astype(np.float32)
SCALARS = np.ascontiguousarray(np.broadcast_to(SCALARS[:, :, None], (5, FREQS, LANES)))
ANGLES = np.broadcast_to(
    np.stack(
        [np.abs(np.cos(theta)), np.abs(np.sin(theta)), np.cos(theta), np.sin(theta), np.sin(phi), np.cos(phi)]
    )[:, :, None],
    (6, DIRS, LANES),
).astype(np.float32)


def stencil(a):
    one_m = 1.0 - a * a
    beyond = a * one_m * (-1.0 / 6.0)
    half = a * (0.5 - 0.5 * a)
    down = half + beyond
    up = a - half - 2.0 * beyond
    return beyond, up - beyond, 1.0 + down - up, -down


def packed_weights():
    out = np.zeros((5, GROUPS, 8, LANES), np.float64)
    for k in range(FREQS):
        for b, j0 in enumerate(BLOCKS):
            c = courant_max * ratio[k] * np.cos(theta[j0 : j0 + 8])
            far, up, own, down = stencil(np.abs(c))
            zero = np.zeros(8)
            pos = c > 0
            five = [
                np.where(pos, far, zero),
                np.where(pos, up, down),
                own,
                np.where(pos, down, up),
                np.where(pos, zero, far),
            ]
            lane = (k % PACK) * SPAN + OFFSETS[b]
            for d in range(5):
                out[d, k // PACK, :, lane : lane + WIDTHS[b]] = five[d][:, None]
    return out.astype(np.float32)


PACKED = packed_weights()


def any_spec():
    return pl.BlockSpec(memory_space=pl.ANY)


def vmem_spec():
    return pl.BlockSpec(memory_space=pltpu.VMEM)


def smem_spec():
    return pl.BlockSpec(memory_space=pltpu.SMEM)


def is_even():
    return jnp.full((8, LANES), lax.axis_index("lon") % 2) == 0


def halo_rows(x, start, one, two, low, high):
    even = is_even()

    def body(i, _):
        for kk in range(GROUP):
            k = start + i * GROUP + kk
            near = ((0, 0, 0, 8), (8, 8, 8, 8), (34, 16, 16, 8), (42, 24, 24, 8), (50, 32, 32, 4))
            far = ((16, 0, 9, 8), (24, 8, 17, 1), (25, 27, 18, 8), (33, 35, 26, 1))
            for cell_e, cell_w, runs in ((3, 0, near), (2, 1, far)):
                for row, j_e, j_w, n in runs:
                    east = x[k, pl.ds(cell_e + 4 * j_e, n, stride=4), :]
                    west = x[k, pl.ds(cell_w + 4 * j_w, n, stride=4), :]
                    one[halo_at(i, kk, row, n), :] = jnp.where(even[:n], east, west)
                    two[halo_at(i, kk, row, n), :] = jnp.where(even[:n], west, east)
        return 0

    lax.fori_loop(low // GROUP, high // GROUP, body, 0)


def halo_at(i, kk, row, n):
    return pl.ds(pl.multiple_of(i * (GROUP * HALO), 8) + HALO * kk + row, n)


def lane_ids():
    return lax.broadcasted_iota(jnp.int32, (8, LANES), 1)


def first_body(count, x_hbm, wind_hbm, cells_hbm, one, two, packed, x, wind, cells, sem, small):
    few = [
        pltpu.make_async_copy(wind_hbm, wind, small.at[0]),
        pltpu.make_async_copy(cells_hbm, cells, small.at[1]),
    ]
    for copy in few:
        copy.start()
    copies = []
    for n in range(count // GROUP):
        span = pl.ds(n * GROUP, GROUP)
        copies.append(pltpu.make_async_copy(x_hbm.at[span], x.at[span], sem.at[n]))
        copies[-1].start()
    for copy in few:
        copy.wait()
    width = cells.shape[1]
    index = jnp.concatenate([cells[:, :LANES], cells[:, width - LANES :]] * 4, axis=0)
    table = jnp.concatenate([wind[pl.ds(n // 2, 1), :] for n in range(8)], axis=0)
    listed = jnp.take_along_axis(table, index, axis=1)
    packed[...] = listed
    one[pl.ds(count * HALO, 8), :] = listed
    for n in range(count // GROUP):
        copies[n].wait()
        halo_rows(x, 0, one, two, n * GROUP, (n + 1) * GROUP)


def message(count, extra=0):
    return pltpu.VMEM((count * HALO + extra, LANES), F32)


def first_halos(x, count, wind, cells):
    return pl.pallas_call(
        lambda *refs: first_body(count, *refs),
        out_shape=(message(count, 8), message(count), pltpu.VMEM((8, LANES), F32)),
        in_specs=[any_spec()] * 3,
        out_specs=(vmem_spec(),) * 3,
        scratch_shapes=[
            pltpu.VMEM((count, *x.shape[1:]), F32),
            pltpu.VMEM(wind.shape, F32),
            pltpu.VMEM(cells.shape, cells.dtype),
            pltpu.SemaphoreType.DMA((count // GROUP,)),
            pltpu.SemaphoreType.DMA((2,)),
        ],
        compiler_params=pltpu.CompilerParams(vmem_limit_bytes=FIRST_VMEM),
        cost_estimate=pl.CostEstimate(flops=0, bytes_accessed=2000000, transcendentals=0),
        name="first_halos",
    )(x, wind, cells)


def edge_ids():
    place = lane_ids() % SPAN
    edge = place
    for offset, first in zip(OFFSETS[1:], EDGES[1:]):
        edge = jnp.where(place >= offset, place - (offset - first), edge)
    return edge


def edge_slot(n, g, joined):
    return 2 * (GROUPS - 1) if joined else n * (GROUPS - 1) + g


def edge_shift(r, b):
    return (r * SPAN + OFFSETS[b] + 2 - EDGES[b]) % LANES


def edge_body(x, sea, after, q):
    lane = lane_ids()
    edge = edge_ids()

    def pack(g, count):
        for cell in range(CELLS):
            acc = jnp.zeros((8, LANES), F32)
            for r in range(count):
                for b, j0 in enumerate(BLOCKS):
                    rows = x[g * PACK + r, pl.ds(cell + 4 * j0, 8, stride=4), :]
                    rows = pltpu.roll(rows, edge_shift(r, b), 1)
                    acc = jnp.where(lane >= r * SPAN + OFFSETS[b], rows, acc)
            q[cell, g] = acc

    def body(g, _):
        pack(g, PACK)
        return 0

    lax.fori_loop(0, FREQS // PACK, body, 0)
    pack(GROUPS - 1, FREQS - (GROUPS - 1) * PACK)
    for cell in range(CELLS):
        mask = jnp.zeros((8, LANES), F32)
        for n, at in enumerate((LANES - 2, LANES - 1, 0, 1)):
            mask = jnp.where(edge == n, sea[pl.ds(cell, 1), pl.ds(at, 1)].astype(F32), mask)
        q[cell, GROUPS] = mask


def pack_edges(x, sea, after):
    return pl.pallas_call(
        edge_body,
        out_shape=pltpu.VMEM((CELLS, GROUPS + 1, 8, LANES), F32),
        in_specs=[vmem_spec()] * 3,
        out_specs=vmem_spec(),
        compiler_params=pltpu.CompilerParams(vmem_limit_bytes=VMEM),
        cost_estimate=pl.CostEstimate(flops=0, bytes_accessed=4000000, transcendentals=0),
        name="pack_edges",
    )(x, sea, after)


def second_body(start, count, x, south, north, one, two, merged):
    pick = edge_ids() < 2
    even = is_even()

    def group(g, joined):
        both = [jnp.where(pick, south[c, g], north[c, g]) for c in range(CELLS)]
        for c in range(CELLS):
            merged[c, g] = both[c]
        east, west = both[2:], both[:2]
        if joined:
            half = lane_ids() < LANES // 2
            east, west = ([jnp.where(half, a, pltpu.roll(b, LANES // 2, 1))] for a, b in (east, west))
        for n, (e, w) in enumerate(zip(east, west)):
            row = pl.ds(pl.multiple_of(count * HALO + edge_slot(n, g, joined) * 8, 8), 8)
            one[row, :] = jnp.where(even, e, w)
            two[row, :] = jnp.where(even, w, e)

    def body(g, _):
        group(g, False)
        return 0

    lax.fori_loop(0, GROUPS - 1, body, 0)
    group(GROUPS - 1, True)
    for c in range(CELLS):
        merged[c, GROUPS] = jnp.where(pick, south[c, GROUPS], north[c, GROUPS])
    halo_rows(x, start, one, two, 0, count)


def second_halos(x, start, count, south, north):
    return pl.pallas_call(
        lambda *refs: second_body(start, count, *refs),
        out_shape=(
            message(count, EDGE_ROWS),
            message(count, EDGE_ROWS),
            pltpu.VMEM((CELLS, GROUPS + 1, 8, LANES), F32),
        ),
        in_specs=[vmem_spec()] * 3,
        out_specs=(vmem_spec(),) * 3,
        compiler_params=pltpu.CompilerParams(vmem_limit_bytes=VMEM),
        cost_estimate=pl.CostEstimate(flops=0, bytes_accessed=2000000, transcendentals=0),
        name="second_halos",
    )(x, south, north)


def later_halos(x, start, count, *after):
    return pl.pallas_call(
        lambda x, *refs: halo_rows(x, start, *refs[-2:], 0, count),
        out_shape=(message(count), message(count)),
        in_specs=[vmem_spec()] * (1 + len(after)),
        out_specs=(vmem_spec(),) * 2,
        compiler_params=pltpu.CompilerParams(vmem_limit_bytes=VMEM),
        cost_estimate=pl.CostEstimate(flops=0, bytes_accessed=1000000, transcendentals=0),
        name="later_halos",
    )(x, *after)


def ghost_body(count, merged, one, two, weights, ghosts, token):
    even = is_even()
    token[...] = jnp.zeros_like(token)

    def spread(g, freqs, joined):
        rows = [
            pl.ds(pl.multiple_of(count * HALO + edge_slot(n, g, joined) * 8, 8), 8)
            for n in range(1 if joined else 2)
        ]
        west = [jnp.where(even, two[row, :], one[row, :]) for row in rows]
        east = [jnp.where(even, one[row, :], two[row, :]) for row in rows]
        if joined:
            west, east = ([a, pltpu.roll(a, LANES // 2, 1)] for (a,) in (west, east))
        ext = west + [merged[c, g] for c in range(CELLS)] + east
        for c in range(CELLS):
            total = weights[0, g] * ext[c]
            for d in range(1, 5):
                total = total + weights[d, g] * ext[c + d]
            total = total * merged[c, GROUPS]
            for r in range(freqs):
                for b in range(len(BLOCKS)):
                    ghosts[g * PACK + r, c, b] = pltpu.roll(total, (LANES - edge_shift(r, b)) % LANES, 1)

    def body(g, _):
        spread(g, PACK, False)
        return 0

    lax.fori_loop(0, FREQS // PACK, body, 0)
    spread(GROUPS - 1, FREQS - (GROUPS - 1) * PACK, True)


def move_ghosts(count, merged, one, two):
    return pl.pallas_call(
        lambda *refs: ghost_body(count, *refs),
        out_shape=(
            pltpu.VMEM((FREQS, CELLS, len(BLOCKS), 8, LANES), F32),
            pltpu.VMEM((8, LANES), F32),
        ),
        in_specs=[vmem_spec()] * 4,
        out_specs=(vmem_spec(),) * 2,
        compiler_params=pltpu.CompilerParams(vmem_limit_bytes=VMEM),
        cost_estimate=pl.CostEstimate(flops=0, bytes_accessed=2000000, transcendentals=0),
        name="move_ghosts",
    )(merged, one, two, PACKED)


def wind_body(cap, sources, after, hour, slots, weights, ang, sea, refr, *rest):
    pieces, (wind, sea8, turn, proj, table) = rest[:-5], rest[-5:]
    at = 0
    for piece in pieces:
        table[pl.ds(at, piece.shape[0]), :] = piece[...]
        at += piece.shape[0]
    late = hour[...]
    width = cap * sources
    me = lax.axis_index("lon")
    mine = cap * me
    high = mine + cap > LANES
    begin = jnp.where(high, mine - (width - LANES), mine)
    lane = lane_ids()
    rows = [jnp.zeros((8, LANES), F32)] * 2
    for s in range(sources):
        block = table[pl.ds(pl.multiple_of(8 * (s ^ me), 8), 8), :]
        for n, to in enumerate((cap * s, cap * s - (width - LANES))):
            if to < LANES and to + cap > 0:
                moved = pltpu.roll(block, (to + 2 * LANES - begin) % LANES, 1)
                rows[n] = jnp.where((lane >= to) & (lane < to + cap), moved, rows[n])

    def entries(n, c):
        now = [jnp.where(high, rows[n][r + 1 : r + 2], rows[n][r : r + 1]) for r in (2 * c, 2 * c + 4)]
        return jnp.broadcast_to((1.0 - late) * now[0] + late * now[1], (8, LANES))

    lists = [[entries(n, c) for n in range(2)] for c in range(2)]
    picked = [[None, None], [None, None]]
    for half in range(2):
        index = slots[pl.ds(8 * half, 8), :]
        low = index < LANES
        place = jnp.where(low, index, index - (width - LANES))
        for c in range(2):
            value = [jnp.take_along_axis(row, place, axis=1) for row in lists[c]]
            picked[half][c] = jnp.where(low, value[0], value[1])
    for c in range(2):
        total = weights[pl.ds(0, 8), :] * picked[0][c]
        total = total + weights[pl.ds(8, 8), :] * picked[1][c]
        wind[c] = total[:CELLS] + total[CELLS:]
    for cell in range(CELLS):
        row = pl.ds(cell, 1)
        sea8[cell] = jnp.broadcast_to(sea[row, :], (8, LANES)).astype(F32)
        for j0 in BLOCKS:
            j = pl.ds(j0, 8)
            turn[cell, j, :] = refr[0, row, :] * ang[4, j, :] - refr[1, row, :] * ang[5, j, :]
            proj[cell, j, :] = wind[0, row, :] * ang[2, j, :] + wind[1, row, :] * ang[3, j, :]


def surface(cap, sources, after, hour, pieces, slots, weights, sea, refr):
    return pl.pallas_call(
        lambda *refs: wind_body(cap, sources, *refs),
        out_shape=(
            pltpu.VMEM((2, CELLS, LANES), F32),
            pltpu.VMEM((CELLS, 8, LANES), F32),
            pltpu.VMEM((CELLS, DIRS, LANES), F32),
            pltpu.VMEM((CELLS, DIRS, LANES), F32),
        ),
        in_specs=[vmem_spec()] * (7 + len(pieces)),
        out_specs=(vmem_spec(),) * 4,
        scratch_shapes=[pltpu.VMEM((8 * sources, LANES), F32)],
        compiler_params=pltpu.CompilerParams(vmem_limit_bytes=VMEM),
        cost_estimate=pl.CostEstimate(flops=0, bytes_accessed=2000000, transcendentals=0),
        name="surface_wind",
    )(after, hour, slots, weights, ANGLES, sea, refr, *pieces)


def weight_body(scal, ang, after, table):
    def body(k, _):
        cour = scal[0, pl.ds(k, 1), :]
        for b, j0 in enumerate(BLOCKS):
            both = stencil(cour * ang[0, pl.ds(j0, 8), :]) + stencil(cour * ang[1, pl.ds(j0, 8), :])
            for n, weight in enumerate(both):
                table[k, b, n] = weight
        return 0

    lax.fori_loop(0, FREQS, body, 0)


def stencil_weights(after):
    return pl.pallas_call(
        weight_body,
        out_shape=pltpu.VMEM((FREQS, len(BLOCKS), 8, 8, LANES), F32),
        in_specs=[vmem_spec()] * 3,
        out_specs=vmem_spec(),
        compiler_params=pltpu.CompilerParams(vmem_limit_bytes=VMEM),
        cost_estimate=pl.CostEstimate(flops=0, bytes_accessed=2000000, transcendentals=0),
        name="stencil_weights",
    )(SCALARS, ANGLES, after)


def chunk_steps(
    first, scal, weights, x, one_ref, two_ref, ghosts, sea8, turn, proj, zs, gs, out, out_first
):
    lane = lane_ids()
    sub = lax.broadcasted_iota(jnp.int32, (8, LANES), 0)
    near_rows = (0, 8, 34, 42, 46)
    even = is_even()

    def from_west(rows):
        return jnp.where(even, two_ref[rows, :], one_ref[rows, :])

    def from_east(rows):
        return jnp.where(even, one_ref[rows, :], two_ref[rows, :])

    def advect(i, kk, sums):
        k = first + i * GROUP + kk
        sums = list(sums)
        for b, j0 in enumerate(BLOCKS):
            w0, w1, w2, w3, v0, v1, v2, v3 = (weights[k, b, n] for n in range(8))
            cells = [x[k, pl.ds(c + 4 * j0, 8, stride=4), :] for c in range(CELLS)]
            west = from_west(halo_at(i, kk, near_rows[b], 8))
            east = from_east(halo_at(i, kk, near_rows[b], 8))
            plus = [west, *cells, east]
            minus = plus[::-1]
            if b == 0:
                far, seq = from_west(halo_at(i, kk, 16, 8)), plus
            elif b == 2:
                far, seq = from_east(halo_at(i, kk, 23, 8)), minus
            elif b == 4:
                far, seq = from_west(halo_at(i, kk, 26, 8)), plus
            else:
                if b == 1:
                    pos = sub < 1
                    far_p, far_m = from_west(halo_at(i, kk, 24, 8)), from_east(halo_at(i, kk, 15, 8))
                else:
                    pos = sub >= 3
                    far_p, far_m = from_west(halo_at(i, kk, 22, 8)), from_east(halo_at(i, kk, 31, 8))
                far = jnp.where(pos, far_p, far_m)
                seq = [jnp.where(pos, p, m) for p, m in zip(plus, minus)]
            seq = [far, *seq]
            moved = [
                w0 * seq[c] + w1 * seq[c + 1] + w2 * seq[c + 2] + w3 * seq[c + 3] for c in range(CELLS)
            ]
            if b == 2:
                moved = moved[::-1]
            elif b in (1, 3):
                moved = [jnp.where(pos, p, m) for p, m in zip(moved, moved[::-1])]
            for c in range(CELLS):
                z = moved[c] * sea8[c]
                ghost = ghosts[k, c, b]
                s1 = pltpu.roll(jnp.where(lane == LANES - 1, ghost, z), 1, 1)
                n1 = pltpu.roll(jnp.where(lane == 0, ghost, z), LANES - 1, 1)
                if b <= 2:
                    s2 = pltpu.roll(jnp.where(lane >= LANES - 2, ghost, z), 2, 1)
                if b >= 2:
                    n2 = pltpu.roll(jnp.where(lane < 2, ghost, z), LANES - 2, 1)
                if b < 2:
                    up, down, far = s1, n1, s2
                elif b > 2:
                    up, down, far = n1, s1, n2
                else:
                    p = sub < 2
                    up, down = jnp.where(p, s1, n1), jnp.where(p, n1, s1)
                    far = jnp.where(p, s2, n2)
                z = v0 * far + v1 * up + v2 * z + v3 * down
                zs[kk, c, pl.ds(8 + j0, 8), :] = z
                sums[c] = sums[c] + (jnp.where(sub >= 4, z, 0.0) if b == 4 else z)
        return tuple(sums)

    def bend_grow(i, kk):
        k = first + i * GROUP + kk
        bend, gain, floor = (scal[n, pl.ds(k, 1), :] for n in range(1, 4))
        for c in range(CELLS):
            zs[kk, c, pl.ds(8 + DIRS, 1), :] = zs[kk, c, pl.ds(8, 1), :]
            for b, j0 in enumerate(BLOCKS):
                own = zs[kk, c, pl.ds(8 + j0, 8), :]
                nxt = zs[kk, c, pl.ds(9 + j0, 8), :]
                s = bend * turn[c, pl.ds(j0, 8), :]
                gs[kk, c, pl.ds(8 + j0, 8), :] = s * jnp.where(s > 0, own, nxt)
            gs[kk, c, pl.ds(7, 1), :] = gs[kk, c, pl.ds(7 + DIRS, 1), :]
            for b, j0 in enumerate(BLOCKS):
                own = zs[kk, c, pl.ds(8 + j0, 8), :]
                flux = gs[kk, c, pl.ds(8 + j0, 8), :]
                prev = gs[kk, c, pl.ds(7 + j0, 8), :]
                refracted = own - (flux - prev)
                growth = jnp.maximum(proj[c, pl.ds(j0, 8), :] * gain - floor, 0.0)
                out[out_first + i * GROUP + kk, pl.ds(c + 4 * j0, 8, stride=4), :] = refracted * jnp.exp2(growth)

    return advect, bend_grow


def no_sums():
    return (jnp.zeros((8, LANES), F32),) * CELLS


def main_body(
    first, count, scal, weights, x, west, east, ghosts, sea8, turn, proj, out, energy, zs, gs
):
    advect, bend_grow = chunk_steps(
        first, scal, weights, x, west, east, ghosts, sea8, turn, proj, zs, gs, out, 0
    )

    def body(i, sums):
        for kk in range(GROUP):
            sums = advect(i, kk, sums)
            bend_grow(i, kk)
        return sums

    for c, total in enumerate(lax.fori_loop(0, count // GROUP, body, no_sums())):
        energy[c] = total


def pass_scratch():
    return [pltpu.VMEM((GROUP, CELLS, 56, LANES), F32), pltpu.VMEM((GROUP, CELLS, 56, LANES), F32)]


def main_chunk(first, count, weights, x, west, east, ghosts, tables):
    return pl.pallas_call(
        lambda *refs: main_body(first, count, *refs),
        out_shape=(
            pltpu.VMEM((count, ROWS, LANES), F32),
            pltpu.VMEM((CELLS, 8, LANES), F32),
        ),
        in_specs=[vmem_spec()] * 9,
        out_specs=(vmem_spec(), vmem_spec()),
        scratch_shapes=pass_scratch(),
        compiler_params=pltpu.CompilerParams(vmem_limit_bytes=VMEM),
        cost_estimate=pl.CostEstimate(flops=0, bytes_accessed=1000000, transcendentals=0),
        name="chunk",
    )(SCALARS, weights, x, west, east, ghosts, *tables)


def tail_body(sizes, scal, weights, x, west, east, ghosts, wind, sea8, turn, proj, *rest):
    done = len(sizes) - 1
    parts, energies = rest[:done], rest[done : 2 * done]
    out_hbm, wind_hbm, obuf, zs, gs, out_sem, wind_sem = rest[2 * done :]
    stores, at = [pltpu.make_async_copy(wind, wind_hbm, wind_sem)], 0
    stores[0].start()
    count = sizes[-1]
    first = FREQS - count
    advect, bend_grow = chunk_steps(
        first, scal, weights, x, west, east, ghosts, sea8, turn, proj, zs, gs, obuf, first
    )
    assert count == GROUP
    sums = no_sums()
    for kk in range(GROUP):
        sums = advect(0, kk, sums)
    sub = lax.broadcasted_iota(jnp.int32, (8, LANES), 0)
    pattern = mask = jnp.zeros((8, LANES), F32)
    for c in range(CELLS):
        total = sums[c]
        for energy in energies:
            total = total + energy[c]
        mean = sea8[c] * (jnp.sum(total, axis=0, keepdims=True) * (1.0 / (FREQS * DIRS)))
        level = mean * (1.0 / energy_ref)
        pattern = jnp.where(sub % CELLS == c, level * level, pattern)
        mask = jnp.where(sub % CELLS == c, sea8[c], mask)
    for n, size in enumerate(sizes):
        if n == done:
            for kk in range(GROUP):
                bend_grow(0, kk)
        for low in range(0, size, PIECE):
            high = min(low + PIECE, size)

            def body(i, _, at=at, n=n):
                scale = jnp.exp2(-(scal[4, pl.ds(at + i, 1), :] * pattern)) * mask
                source, k = (parts[n], i) if n < done else (obuf, at + i)
                for r in range(0, ROWS, 8):
                    obuf[at + i, pl.ds(r, 8), :] = source[k, pl.ds(r, 8), :] * scale
                return 0

            lax.fori_loop(low, high, body, 0)
            span = pl.ds(at + low, high - low)
            stores.append(
                pltpu.make_async_copy(obuf.at[span], out_hbm.at[span], out_sem.at[len(stores) - 1])
            )
            stores[-1].start()
        at += size
    for store in stores:
        store.wait()


def tail_chunk(sizes, weights, x, west, east, ghosts, wind, tables, parts, energies):
    done = len(sizes) - 1
    return pl.pallas_call(
        lambda *refs: tail_body(sizes, *refs),
        out_shape=(
            jax.ShapeDtypeStruct((FREQS, ROWS, LANES), F32),
            jax.ShapeDtypeStruct((2, CELLS, LANES), F32),
        ),
        in_specs=[vmem_spec()] * (10 + 2 * done),
        out_specs=(any_spec(), any_spec()),
        scratch_shapes=[
            pltpu.VMEM((FREQS, ROWS, LANES), F32),
            *pass_scratch(),
            pltpu.SemaphoreType.DMA((FREQS // PIECE,)),
            pltpu.SemaphoreType.DMA,
        ],
        compiler_params=pltpu.CompilerParams(vmem_limit_bytes=VMEM),
        cost_estimate=pl.CostEstimate(flops=0, bytes_accessed=6000000, transcendentals=0),
        name="last_chunk",
    )(SCALARS, weights, x, west, east, ghosts, wind, *tables, *parts, *energies)


def line(axis):
    up = [(i, i + 1) for i in range(lax.axis_size(axis) - 1)]
    return up, [(j, i) for i, j in up]


def local(
    spectrum, sea_mask, refraction, atm_wind, hour_fraction, send_cells, recv_slots, recv_weights
):
    north_way, south_way = line("lat")
    x = spectrum.reshape(FREQS, ROWS, LANES)
    tiles = lax.axis_size("lon")
    swap_one = [(i, i ^ 1) for i in range(tiles)]
    swap_two = [(i, (i + 1 if i % 2 else i - 1) % tiles) for i in range(tiles)]
    cap = send_cells.shape[1] // tiles
    firsts = [sum(CHUNKS[:n]) for n in range(len(CHUNKS))]

    def exchange(one, two):
        return lax.ppermute(one, "lon", swap_one), lax.ppermute(two, "lon", swap_two)

    *sends, packed = first_halos(
        x, CHUNKS[0], atm_wind.reshape(4, LANES), send_cells
    )
    halos = [exchange(*sends)]
    q = pack_edges(x, sea_mask, packed)
    weights = stencil_weights(packed)
    south = lax.ppermute(q, "lat", north_way)
    north = lax.ppermute(q, "lat", south_way)
    *sends, merged = second_halos(x, firsts[1], CHUNKS[1], south, north)
    halos.append(exchange(*sends))
    halos.append(exchange(*later_halos(x, firsts[2], CHUNKS[2], *halos[0], weights)))

    lists = [jnp.concatenate([packed, halos[0][0][-8:]])]
    step = 2
    while step < tiles:
        held = lists[0] if len(lists) == 1 else jnp.concatenate(lists)
        lists.append(lax.ppermute(held, "lon", [(i, i ^ step) for i in range(tiles)]))
        step *= 2
    ghosts, token = move_ghosts(CHUNKS[1], merged, *halos[1])
    surface_wind, *tables = surface(
        cap,
        tiles,
        token,
        hour_fraction.reshape(1, 1),
        lists,
        recv_slots.reshape(4 * CELLS, LANES),
        recv_weights.reshape(4 * CELLS, LANES),
        sea_mask,
        refraction,
    )
    halos.append(exchange(*later_halos(x, firsts[3], CHUNKS[3], *halos[1], tables[0])))

    parts, energies = [], []
    for n, (first, count) in enumerate(zip(firsts, CHUNKS)):
        west, east = halos[n]
        if n < len(CHUNKS) - 1:
            part, energy = main_chunk(first, count, weights, x, west, east, ghosts, tables)
            parts.append(part)
            energies.append(energy)
        else:
            out, surface_wind = tail_chunk(
                CHUNKS, weights, x, west, east, ghosts, surface_wind, tables, parts, energies
            )
    return (out.reshape(spectrum.shape), surface_wind)


def solution(mesh):
    in_specs = (
        P(None, None, "lon", "lat"),
        P("lon", "lat"),
        P(None, "lon", "lat"),
        P(None, None, ("lon", "lat")),
        P(),
        P(("lon", "lat"), None),
        P(None, "lon", "lat"),
        P(None, "lon", "lat"),
    )
    out_specs = (P(None, None, "lon", "lat"), P(None, "lon", "lat"))
    return jax.shard_map(local, mesh=mesh, in_specs=in_specs, out_specs=out_specs, check_vma=False)
```

```python
import math

import jax
import jax.numpy as jnp
import numpy as np
from jax import lax
from jax.experimental import pallas as pl
from jax.experimental.pallas import tpu as pltpu
from jax.sharding import PartitionSpec as P

base_freq = 0.035
freq_step = 1.1
courant_max = 0.9
gravity = 9.81
input_rate = 0.05
damping_rate = 0.8
energy_ref = 0.5

F32 = jnp.float32
FREQS = 36
DIRS = 36
CELLS = 4
LANES = 128
ROWS = DIRS * CELLS
BLOCKS = (0, 8, 16, 24, 28)
GROUP = 4
HALO = DIRS + DIRS // 2
NEAR_SPLIT = 16
FAR = DIRS // 2
PACK = 8
SPAN = LANES // PACK
OFFSETS, WIDTHS, EDGES = (0, 3, 6, 10, 13), (3, 3, 4, 3, 3), (0, 0, 0, 1, 1)
CHUNKS = (12, 8, 12, 4)
GROUPS = -(-FREQS // PACK)
PIECE = 4
EDGE_ROWS = (2 * (-(-FREQS // PACK)) - 1) * 8
VMEM = 32 * 1024 * 1024
FIRST_VMEM = 63000000

freqs = base_freq * freq_step ** np.arange(FREQS, dtype=np.float64)
spacing = 2.0 * math.pi / DIRS
theta = (np.arange(DIRS) + 0.5) * spacing
phi = (np.arange(DIRS) + 1.0) * spacing
ratio = base_freq / freqs
log2_e = 1.0 / math.log(2.0)
rate = input_rate * freqs / freqs[-1] * log2_e
SCALARS = np.stack(
    [
        courant_max * ratio,
        np.sqrt(ratio),
        rate * 2.0 * math.pi * freqs / gravity,
        rate,
        damping_rate * freqs / freqs[-1] * log2_e,
    ]
).astype(np.float32)
SCALARS = np.ascontiguousarray(np.broadcast_to(SCALARS[:, :, None], (5, FREQS, LANES)))
ANGLES = np.broadcast_to(
    np.stack(
        [np.abs(np.cos(theta)), np.abs(np.sin(theta)), np.cos(theta), np.sin(theta), np.sin(phi), np.cos(phi)]
    )[:, :, None],
    (6, DIRS, LANES),
).astype(np.float32)


def stencil(a):
    one_m = 1.0 - a * a
    beyond = a * one_m * (-1.0 / 6.0)
    half = a * (0.5 - 0.5 * a)
    down = half + beyond
    up = a - half - 2.0 * beyond
    return beyond, up - beyond, 1.0 + down - up, -down


def packed_weights():
    out = np.zeros((5, GROUPS, 8, LANES), np.float64)
    for k in range(FREQS):
        for b, j0 in enumerate(BLOCKS):
            c = courant_max * ratio[k] * np.cos(theta[j0 : j0 + 8])
            far, up, own, down = stencil(np.abs(c))
            zero = np.zeros(8)
            pos = c > 0
            five = [
                np.where(pos, far, zero),
                np.where(pos, up, down),
                own,
                np.where(pos, down, up),
                np.where(pos, zero, far),
            ]
            lane = (k % PACK) * SPAN + OFFSETS[b]
            for d in range(5):
                out[d, k // PACK, :, lane : lane + WIDTHS[b]] = five[d][:, None]
    return out.astype(np.float32)


PACKED = packed_weights()


def any_spec():
    return pl.BlockSpec(memory_space=pl.ANY)


def vmem_spec():
    return pl.BlockSpec(memory_space=pltpu.VMEM)


def smem_spec():
    return pl.BlockSpec(memory_space=pltpu.SMEM)


def is_even():
    return jnp.full((8, LANES), lax.axis_index("lon") % 2) == 0


def halo_rows(x, start, one, two, low, high):
    even = is_even()

    def body(i, _):
        for kk in range(GROUP):
            k = start + i * GROUP + kk
            near = ((0, 0, 0, 8), (8, 8, 8, 8), (34, 16, 16, 8), (42, 24, 24, 8), (50, 32, 32, 4))
            far = ((16, 0, 9, 8), (24, 8, 17, 1), (25, 27, 18, 8), (33, 35, 26, 1))
            for cell_e, cell_w, runs in ((3, 0, near), (2, 1, far)):
                for row, j_e, j_w, n in runs:
                    east = x[k, pl.ds(cell_e + 4 * j_e, n, stride=4), :]
                    west = x[k, pl.ds(cell_w + 4 * j_w, n, stride=4), :]
                    one[halo_at(i, kk, row, n), :] = jnp.where(even[:n], east, west)
                    two[halo_at(i, kk, row, n), :] = jnp.where(even[:n], west, east)
        return 0

    lax.fori_loop(low // GROUP, high // GROUP, body, 0)


def halo_at(i, kk, row, n):
    return pl.ds(pl.multiple_of(i * (GROUP * HALO), 8) + HALO * kk + row, n)


def lane_ids():
    return lax.broadcasted_iota(jnp.int32, (8, LANES), 1)


def first_body(count, x_hbm, wind_hbm, cells_hbm, one, two, packed, x, wind, cells, sem, small):
    few = [
        pltpu.make_async_copy(wind_hbm, wind, small.at[0]),
        pltpu.make_async_copy(cells_hbm, cells, small.at[1]),
    ]
    copies = []
    for n in range(count // GROUP):
        span = pl.ds(n * GROUP, GROUP)
        copies.append(pltpu.make_async_copy(x_hbm.at[span], x.at[span], sem.at[n]))
        copies[-1].start()
        if n == 0:
            for copy in few:
                copy.start()
    for n in range(count // GROUP - 1):
        copies[n].wait()
        halo_rows(x, 0, one, two, n * GROUP, (n + 1) * GROUP)
    for copy in few:
        copy.wait()
    width = cells.shape[1]
    index = jnp.concatenate([cells[:, :LANES], cells[:, width - LANES :]] * 4, axis=0)
    table = jnp.concatenate([wind[pl.ds(n // 2, 1), :] for n in range(8)], axis=0)
    listed = jnp.take_along_axis(table, index, axis=1)
    packed[...] = listed
    one[pl.ds(count * HALO, 8), :] = listed
    copies[-1].wait()
    halo_rows(x, 0, one, two, count - GROUP, count)


def message(count, extra=0):
    return pltpu.VMEM((count * HALO + extra, LANES), F32)


def first_halos(x, count, wind, cells):
    return pl.pallas_call(
        lambda *refs: first_body(count, *refs),
        out_shape=(message(count, 8), message(count), pltpu.VMEM((8, LANES), F32)),
        in_specs=[any_spec()] * 3,
        out_specs=(vmem_spec(),) * 3,
        scratch_shapes=[
            pltpu.VMEM((count, *x.shape[1:]), F32),
            pltpu.VMEM(wind.shape, F32),
            pltpu.VMEM(cells.shape, cells.dtype),
            pltpu.SemaphoreType.DMA((count // GROUP,)),
            pltpu.SemaphoreType.DMA((2,)),
        ],
        compiler_params=pltpu.CompilerParams(vmem_limit_bytes=FIRST_VMEM),
        cost_estimate=pl.CostEstimate(flops=0, bytes_accessed=2000000, transcendentals=0),
        name="first_halos",
    )(x, wind, cells)


def edge_ids():
    place = lane_ids() % SPAN
    edge = place
    for offset, first in zip(OFFSETS[1:], EDGES[1:]):
        edge = jnp.where(place >= offset, place - (offset - first), edge)
    return edge


def edge_slot(n, g, joined):
    return 2 * (GROUPS - 1) if joined else n * (GROUPS - 1) + g


def edge_shift(r, b):
    return (r * SPAN + OFFSETS[b] + 2 - EDGES[b]) % LANES


def edge_body(x, sea, after, q):
    lane = lane_ids()
    edge = edge_ids()

    def pack(g, count):
        for cell in range(CELLS):
            acc = jnp.zeros((8, LANES), F32)
            for r in range(count):
                for b, j0 in enumerate(BLOCKS):
                    rows = x[g * PACK + r, pl.ds(cell + 4 * j0, 8, stride=4), :]
                    rows = pltpu.roll(rows, edge_shift(r, b), 1)
                    acc = jnp.where(lane >= r * SPAN + OFFSETS[b], rows, acc)
            q[cell, g] = acc

    def body(g, _):
        pack(g, PACK)
        return 0

    lax.fori_loop(0, FREQS // PACK, body, 0)
    pack(GROUPS - 1, FREQS - (GROUPS - 1) * PACK)
    for cell in range(CELLS):
        mask = jnp.zeros((8, LANES), F32)
        for n, at in enumerate((LANES - 2, LANES - 1, 0, 1)):
            mask = jnp.where(edge == n, sea[pl.ds(cell, 1), pl.ds(at, 1)].astype(F32), mask)
        q[cell, GROUPS] = mask


def pack_edges(x, sea, after):
    return pl.pallas_call(
        edge_body,
        out_shape=pltpu.VMEM((CELLS, GROUPS + 1, 8, LANES), F32),
        in_specs=[vmem_spec()] * 3,
        out_specs=vmem_spec(),
        compiler_params=pltpu.CompilerParams(vmem_limit_bytes=VMEM),
        cost_estimate=pl.CostEstimate(flops=0, bytes_accessed=4000000, transcendentals=0),
        name="pack_edges",
    )(x, sea, after)


def second_body(start, count, x, south, north, one, two, merged):
    pick = edge_ids() < 2
    even = is_even()

    def group(g, joined):
        both = [jnp.where(pick, south[c, g], north[c, g]) for c in range(CELLS)]
        for c in range(CELLS):
            merged[c, g] = both[c]
        east, west = both[2:], both[:2]
        if joined:
            half = lane_ids() < LANES // 2
            east, west = ([jnp.where(half, a, pltpu.roll(b, LANES // 2, 1))] for a, b in (east, west))
        for n, (e, w) in enumerate(zip(east, west)):
            row = pl.ds(pl.multiple_of(count * HALO + edge_slot(n, g, joined) * 8, 8), 8)
            one[row, :] = jnp.where(even, e, w)
            two[row, :] = jnp.where(even, w, e)

    def body(g, _):
        group(g, False)
        return 0

    lax.fori_loop(0, GROUPS - 1, body, 0)
    group(GROUPS - 1, True)
    for c in range(CELLS):
        merged[c, GROUPS] = jnp.where(pick, south[c, GROUPS], north[c, GROUPS])
    halo_rows(x, start, one, two, 0, count)


def second_halos(x, start, count, south, north):
    return pl.pallas_call(
        lambda *refs: second_body(start, count, *refs),
        out_shape=(
            message(count, EDGE_ROWS),
            message(count, EDGE_ROWS),
            pltpu.VMEM((CELLS, GROUPS + 1, 8, LANES), F32),
        ),
        in_specs=[vmem_spec()] * 3,
        out_specs=(vmem_spec(),) * 3,
        compiler_params=pltpu.CompilerParams(vmem_limit_bytes=VMEM),
        cost_estimate=pl.CostEstimate(flops=0, bytes_accessed=2000000, transcendentals=0),
        name="second_halos",
    )(x, south, north)


def later_halos(x, start, count, *after):
    return pl.pallas_call(
        lambda x, *refs: halo_rows(x, start, *refs[-2:], 0, count),
        out_shape=(message(count), message(count)),
        in_specs=[vmem_spec()] * (1 + len(after)),
        out_specs=(vmem_spec(),) * 2,
        compiler_params=pltpu.CompilerParams(vmem_limit_bytes=VMEM),
        cost_estimate=pl.CostEstimate(flops=0, bytes_accessed=1000000, transcendentals=0),
        name="later_halos",
    )(x, *after)


def ghost_body(count, merged, one, two, weights, ghosts, token):
    even = is_even()
    token[...] = jnp.zeros_like(token)

    def spread(g, freqs, joined):
        rows = [
            pl.ds(pl.multiple_of(count * HALO + edge_slot(n, g, joined) * 8, 8), 8)
            for n in range(1 if joined else 2)
        ]
        west = [jnp.where(even, two[row, :], one[row, :]) for row in rows]
        east = [jnp.where(even, one[row, :], two[row, :]) for row in rows]
        if joined:
            west, east = ([a, pltpu.roll(a, LANES // 2, 1)] for (a,) in (west, east))
        ext = west + [merged[c, g] for c in range(CELLS)] + east
        for c in range(CELLS):
            total = weights[0, g] * ext[c]
            for d in range(1, 5):
                total = total + weights[d, g] * ext[c + d]
            total = total * merged[c, GROUPS]
            for r in range(freqs):
                for b in range(len(BLOCKS)):
                    ghosts[g * PACK + r, c, b] = pltpu.roll(total, (LANES - edge_shift(r, b)) % LANES, 1)

    def body(g, _):
        spread(g, PACK, False)
        return 0

    lax.fori_loop(0, FREQS // PACK, body, 0)
    spread(GROUPS - 1, FREQS - (GROUPS - 1) * PACK, True)


def move_ghosts(count, merged, one, two):
    return pl.pallas_call(
        lambda *refs: ghost_body(count, *refs),
        out_shape=(
            pltpu.VMEM((FREQS, CELLS, len(BLOCKS), 8, LANES), F32),
            pltpu.VMEM((8, LANES), F32),
        ),
        in_specs=[vmem_spec()] * 4,
        out_specs=(vmem_spec(),) * 2,
        compiler_params=pltpu.CompilerParams(vmem_limit_bytes=VMEM),
        cost_estimate=pl.CostEstimate(flops=0, bytes_accessed=2000000, transcendentals=0),
        name="move_ghosts",
    )(merged, one, two, PACKED)


def wind_body(cap, sources, after, hour, slots, weights, ang, sea, refr, *rest):
    pieces, (wind, sea8, turn, proj, table) = rest[:-5], rest[-5:]
    at = 0
    for piece in pieces:
        table[pl.ds(at, piece.shape[0]), :] = piece[...]
        at += piece.shape[0]
    late = hour[...]
    width = cap * sources
    me = lax.axis_index("lon")
    mine = cap * me
    high = mine + cap > LANES
    begin = jnp.where(high, mine - (width - LANES), mine)
    lane = lane_ids()
    rows = [jnp.zeros((8, LANES), F32)] * 2
    for s in range(sources):
        block = table[pl.ds(pl.multiple_of(8 * (s ^ me), 8), 8), :]
        for n, to in enumerate((cap * s, cap * s - (width - LANES))):
            if to < LANES and to + cap > 0:
                moved = pltpu.roll(block, (to + 2 * LANES - begin) % LANES, 1)
                rows[n] = jnp.where((lane >= to) & (lane < to + cap), moved, rows[n])

    def entries(n, c):
        now = [jnp.where(high, rows[n][r + 1 : r + 2], rows[n][r : r + 1]) for r in (2 * c, 2 * c + 4)]
        return jnp.broadcast_to((1.0 - late) * now[0] + late * now[1], (8, LANES))

    lists = [[entries(n, c) for n in range(2)] for c in range(2)]
    picked = [[None, None], [None, None]]
    for half in range(2):
        index = slots[pl.ds(8 * half, 8), :]
        low = index < LANES
        place = jnp.where(low, index, index - (width - LANES))
        for c in range(2):
            value = [jnp.take_along_axis(row, place, axis=1) for row in lists[c]]
            picked[half][c] = jnp.where(low, value[0], value[1])
    for c in range(2):
        total = weights[pl.ds(0, 8), :] * picked[0][c]
        total = total + weights[pl.ds(8, 8), :] * picked[1][c]
        wind[c] = total[:CELLS] + total[CELLS:]
    for cell in range(CELLS):
        row = pl.ds(cell, 1)
        sea8[cell] = jnp.broadcast_to(sea[row, :], (8, LANES)).astype(F32)
        for j0 in BLOCKS:
            j = pl.ds(j0, 8)
            turn[cell, j, :] = refr[0, row, :] * ang[4, j, :] - refr[1, row, :] * ang[5, j, :]
            proj[cell, j, :] = wind[0, row, :] * ang[2, j, :] + wind[1, row, :] * ang[3, j, :]


def surface(cap, sources, after, hour, pieces, slots, weights, sea, refr):
    return pl.pallas_call(
        lambda *refs: wind_body(cap, sources, *refs),
        out_shape=(
            pltpu.VMEM((2, CELLS, LANES), F32),
            pltpu.VMEM((CELLS, 8, LANES), F32),
            pltpu.VMEM((CELLS, DIRS, LANES), F32),
            pltpu.VMEM((CELLS, DIRS, LANES), F32),
        ),
        in_specs=[vmem_spec()] * (7 + len(pieces)),
        out_specs=(vmem_spec(),) * 4,
        scratch_shapes=[pltpu.VMEM((8 * sources, LANES), F32)],
        compiler_params=pltpu.CompilerParams(vmem_limit_bytes=VMEM),
        cost_estimate=pl.CostEstimate(flops=0, bytes_accessed=2000000, transcendentals=0),
        name="surface_wind",
    )(after, hour, slots, weights, ANGLES, sea, refr, *pieces)


def weight_body(scal, ang, after, table):
    def body(k, _):
        cour = scal[0, pl.ds(k, 1), :]
        for b, j0 in enumerate(BLOCKS):
            both = stencil(cour * ang[0, pl.ds(j0, 8), :]) + stencil(cour * ang[1, pl.ds(j0, 8), :])
            for n, weight in enumerate(both):
                table[k, b, n] = weight
        return 0

    lax.fori_loop(0, FREQS, body, 0)


def stencil_weights(after):
    return pl.pallas_call(
        weight_body,
        out_shape=pltpu.VMEM((FREQS, len(BLOCKS), 8, 8, LANES), F32),
        in_specs=[vmem_spec()] * 3,
        out_specs=vmem_spec(),
        compiler_params=pltpu.CompilerParams(vmem_limit_bytes=VMEM),
        cost_estimate=pl.CostEstimate(flops=0, bytes_accessed=2000000, transcendentals=0),
        name="stencil_weights",
    )(SCALARS, ANGLES, after)


def chunk_steps(
    first, scal, weights, x, one_ref, two_ref, ghosts, sea8, turn, proj, zs, gs, out, out_first
):
    lane = lane_ids()
    sub = lax.broadcasted_iota(jnp.int32, (8, LANES), 0)
    near_rows = (0, 8, 34, 42, 46)
    even = is_even()

    def from_west(rows):
        return jnp.where(even, two_ref[rows, :], one_ref[rows, :])

    def from_east(rows):
        return jnp.where(even, one_ref[rows, :], two_ref[rows, :])

    def advect(i, kk, sums):
        k = first + i * GROUP + kk
        sums = list(sums)
        for b, j0 in enumerate(BLOCKS):
            w0, w1, w2, w3, v0, v1, v2, v3 = (weights[k, b, n] for n in range(8))
            cells = [x[k, pl.ds(c + 4 * j0, 8, stride=4), :] for c in range(CELLS)]
            west = from_west(halo_at(i, kk, near_rows[b], 8))
            east = from_east(halo_at(i, kk, near_rows[b], 8))
            plus = [west, *cells, east]
            minus = plus[::-1]
            if b == 0:
                far, seq = from_west(halo_at(i, kk, 16, 8)), plus
            elif b == 2:
                far, seq = from_east(halo_at(i, kk, 23, 8)), minus
            elif b == 4:
                far, seq = from_west(halo_at(i, kk, 26, 8)), plus
            else:
                if b == 1:
                    pos = sub < 1
                    far_p, far_m = from_west(halo_at(i, kk, 24, 8)), from_east(halo_at(i, kk, 15, 8))
                else:
                    pos = sub >= 3
                    far_p, far_m = from_west(halo_at(i, kk, 22, 8)), from_east(halo_at(i, kk, 31, 8))
                far = jnp.where(pos, far_p, far_m)
                seq = [jnp.where(pos, p, m) for p, m in zip(plus, minus)]
            seq = [far, *seq]
            moved = [
                w0 * seq[c] + w1 * seq[c + 1] + w2 * seq[c + 2] + w3 * seq[c + 3] for c in range(CELLS)
            ]
            if b == 2:
                moved = moved[::-1]
            elif b in (1, 3):
                moved = [jnp.where(pos, p, m) for p, m in zip(moved, moved[::-1])]
            for c in range(CELLS):
                z = moved[c] * sea8[c]
                ghost = ghosts[k, c, b]
                s1 = pltpu.roll(jnp.where(lane == LANES - 1, ghost, z), 1, 1)
                n1 = pltpu.roll(jnp.where(lane == 0, ghost, z), LANES - 1, 1)
                if b <= 2:
                    s2 = pltpu.roll(jnp.where(lane >= LANES - 2, ghost, z), 2, 1)
                if b >= 2:
                    n2 = pltpu.roll(jnp.where(lane < 2, ghost, z), LANES - 2, 1)
                if b < 2:
                    up, down, far = s1, n1, s2
                elif b > 2:
                    up, down, far = n1, s1, n2
                else:
                    p = sub < 2
                    up, down = jnp.where(p, s1, n1), jnp.where(p, n1, s1)
                    far = jnp.where(p, s2, n2)
                z = v0 * far + v1 * up + v2 * z + v3 * down
                zs[kk, c, pl.ds(8 + j0, 8), :] = z
                sums[c] = sums[c] + (jnp.where(sub >= 4, z, 0.0) if b == 4 else z)
        return tuple(sums)

    def bend_grow(i, kk):
        k = first + i * GROUP + kk
        bend, gain, floor = (scal[n, pl.ds(k, 1), :] for n in range(1, 4))
        for c in range(CELLS):
            zs[kk, c, pl.ds(8 + DIRS, 1), :] = zs[kk, c, pl.ds(8, 1), :]
            for b, j0 in enumerate(BLOCKS):
                own = zs[kk, c, pl.ds(8 + j0, 8), :]
                nxt = zs[kk, c, pl.ds(9 + j0, 8), :]
                s = bend * turn[c, pl.ds(j0, 8), :]
                gs[kk, c, pl.ds(8 + j0, 8), :] = s * jnp.where(s > 0, own, nxt)
            gs[kk, c, pl.ds(7, 1), :] = gs[kk, c, pl.ds(7 + DIRS, 1), :]
            for b, j0 in enumerate(BLOCKS):
                own = zs[kk, c, pl.ds(8 + j0, 8), :]
                flux = gs[kk, c, pl.ds(8 + j0, 8), :]
                prev = gs[kk, c, pl.ds(7 + j0, 8), :]
                refracted = own - (flux - prev)
                growth = jnp.maximum(proj[c, pl.ds(j0, 8), :] * gain - floor, 0.0)
                out[out_first + i * GROUP + kk, pl.ds(c + 4 * j0, 8, stride=4), :] = refracted * jnp.exp2(growth)

    return advect, bend_grow


def no_sums():
    return (jnp.zeros((8, LANES), F32),) * CELLS


def main_body(
    first, count, scal, weights, x, west, east, ghosts, sea8, turn, proj, out, energy, zs, gs
):
    advect, bend_grow = chunk_steps(
        first, scal, weights, x, west, east, ghosts, sea8, turn, proj, zs, gs, out, 0
    )

    def body(i, sums):
        for kk in range(GROUP):
            sums = advect(i, kk, sums)
            bend_grow(i, kk)
        return sums

    for c, total in enumerate(lax.fori_loop(0, count // GROUP, body, no_sums())):
        energy[c] = total


def pass_scratch():
    return [pltpu.VMEM((GROUP, CELLS, 56, LANES), F32), pltpu.VMEM((GROUP, CELLS, 56, LANES), F32)]


def main_chunk(first, count, weights, x, west, east, ghosts, tables):
    return pl.pallas_call(
        lambda *refs: main_body(first, count, *refs),
        out_shape=(
            pltpu.VMEM((count, ROWS, LANES), F32),
            pltpu.VMEM((CELLS, 8, LANES), F32),
        ),
        in_specs=[vmem_spec()] * 9,
        out_specs=(vmem_spec(), vmem_spec()),
        scratch_shapes=pass_scratch(),
        compiler_params=pltpu.CompilerParams(vmem_limit_bytes=VMEM),
        cost_estimate=pl.CostEstimate(flops=0, bytes_accessed=1000000, transcendentals=0),
        name="chunk",
    )(SCALARS, weights, x, west, east, ghosts, *tables)


def tail_body(sizes, scal, weights, x, west, east, ghosts, wind, sea8, turn, proj, *rest):
    done = len(sizes) - 1
    parts, energies = rest[:done], rest[done : 2 * done]
    out_hbm, wind_hbm, obuf, zs, gs, out_sem, wind_sem = rest[2 * done :]
    stores, at = [pltpu.make_async_copy(wind, wind_hbm, wind_sem)], 0
    stores[0].start()
    count = sizes[-1]
    first = FREQS - count
    advect, bend_grow = chunk_steps(
        first, scal, weights, x, west, east, ghosts, sea8, turn, proj, zs, gs, obuf, first
    )
    assert count == GROUP
    sums = no_sums()
    for kk in range(GROUP):
        sums = advect(0, kk, sums)
    sub = lax.broadcasted_iota(jnp.int32, (8, LANES), 0)
    pattern = mask = jnp.zeros((8, LANES), F32)
    for c in range(CELLS):
        total = sums[c]
        for energy in energies:
            total = total + energy[c]
        mean = sea8[c] * (jnp.sum(total, axis=0, keepdims=True) * (1.0 / (FREQS * DIRS)))
        level = mean * (1.0 / energy_ref)
        pattern = jnp.where(sub % CELLS == c, level * level, pattern)
        mask = jnp.where(sub % CELLS == c, sea8[c], mask)
    for n, size in enumerate(sizes):
        if n == done:
            for kk in range(GROUP):
                bend_grow(0, kk)
        for low in range(0, size, PIECE):
            high = min(low + PIECE, size)

            def body(i, _, at=at, n=n):
                scale = jnp.exp2(-(scal[4, pl.ds(at + i, 1), :] * pattern)) * mask
                source, k = (parts[n], i) if n < done else (obuf, at + i)
                for r in range(0, ROWS, 8):
                    obuf[at + i, pl.ds(r, 8), :] = source[k, pl.ds(r, 8), :] * scale
                return 0

            lax.fori_loop(low, high, body, 0)
            span = pl.ds(at + low, high - low)
            stores.append(
                pltpu.make_async_copy(obuf.at[span], out_hbm.at[span], out_sem.at[len(stores) - 1])
            )
            stores[-1].start()
        at += size
    for store in stores:
        store.wait()


def tail_chunk(sizes, weights, x, west, east, ghosts, wind, tables, parts, energies):
    done = len(sizes) - 1
    return pl.pallas_call(
        lambda *refs: tail_body(sizes, *refs),
        out_shape=(
            jax.ShapeDtypeStruct((FREQS, ROWS, LANES), F32),
            jax.ShapeDtypeStruct((2, CELLS, LANES), F32),
        ),
        in_specs=[vmem_spec()] * (10 + 2 * done),
        out_specs=(any_spec(), any_spec()),
        scratch_shapes=[
            pltpu.VMEM((FREQS, ROWS, LANES), F32),
            *pass_scratch(),
            pltpu.SemaphoreType.DMA((FREQS // PIECE,)),
            pltpu.SemaphoreType.DMA,
        ],
        compiler_params=pltpu.CompilerParams(vmem_limit_bytes=VMEM),
        cost_estimate=pl.CostEstimate(flops=0, bytes_accessed=6000000, transcendentals=0),
        name="last_chunk",
    )(SCALARS, weights, x, west, east, ghosts, wind, *tables, *parts, *energies)


def line(axis):
    up = [(i, i + 1) for i in range(lax.axis_size(axis) - 1)]
    return up, [(j, i) for i, j in up]


def local(
    spectrum, sea_mask, refraction, atm_wind, hour_fraction, send_cells, recv_slots, recv_weights
):
    north_way, south_way = line("lat")
    x = spectrum.reshape(FREQS, ROWS, LANES)
    tiles = lax.axis_size("lon")
    swap_one = [(i, i ^ 1) for i in range(tiles)]
    swap_two = [(i, (i + 1 if i % 2 else i - 1) % tiles) for i in range(tiles)]
    cap = send_cells.shape[1] // tiles
    firsts = [sum(CHUNKS[:n]) for n in range(len(CHUNKS))]

    def exchange(one, two):
        return lax.ppermute(one, "lon", swap_one), lax.ppermute(two, "lon", swap_two)

    *sends, packed = first_halos(
        x, CHUNKS[0], atm_wind.reshape(4, LANES), send_cells
    )
    halos = [exchange(*sends)]
    q = pack_edges(x, sea_mask, packed)
    weights = stencil_weights(packed)
    south = lax.ppermute(q, "lat", north_way)
    north = lax.ppermute(q, "lat", south_way)
    *sends, merged = second_halos(x, firsts[1], CHUNKS[1], south, north)
    halos.append(exchange(*sends))
    halos.append(exchange(*later_halos(x, firsts[2], CHUNKS[2], *halos[0], weights)))

    lists = [jnp.concatenate([packed, halos[0][0][-8:]])]
    step = 2
    while step < tiles:
        held = lists[0] if len(lists) == 1 else jnp.concatenate(lists)
        lists.append(lax.ppermute(held, "lon", [(i, i ^ step) for i in range(tiles)]))
        step *= 2
    ghosts, token = move_ghosts(CHUNKS[1], merged, *halos[1])
    surface_wind, *tables = surface(
        cap,
        tiles,
        token,
        hour_fraction.reshape(1, 1),
        lists,
        recv_slots.reshape(4 * CELLS, LANES),
        recv_weights.reshape(4 * CELLS, LANES),
        sea_mask,
        refraction,
    )
    halos.append(exchange(*later_halos(x, firsts[3], CHUNKS[3], *halos[1], tables[0])))

    parts, energies = [], []
    for n, (first, count) in enumerate(zip(firsts, CHUNKS)):
        west, east = halos[n]
        if n < len(CHUNKS) - 1:
            part, energy = main_chunk(first, count, weights, x, west, east, ghosts, tables)
            parts.append(part)
            energies.append(energy)
        else:
            out, surface_wind = tail_chunk(
                CHUNKS, weights, x, west, east, ghosts, surface_wind, tables, parts, energies
            )
    return (out.reshape(spectrum.shape), surface_wind)


def solution(mesh):
    in_specs = (
        P(None, None, "lon", "lat"),
        P("lon", "lat"),
        P(None, "lon", "lat"),
        P(None, None, ("lon", "lat")),
        P(),
        P(("lon", "lat"), None),
        P(None, "lon", "lat"),
        P(None, "lon", "lat"),
    )
    out_specs = (P(None, None, "lon", "lat"), P(None, "lon", "lat"))
    return jax.shard_map(local, mesh=mesh, in_specs=in_specs, out_specs=out_specs, check_vma=False)
```
